32 devices in a mesh: dp: 8 (over z, y), fsdp: 4 (over x, core).
Axes of the slice: x: 2, y: 2, z: 4, core: 2. Of those that a mesh axis runs over, the one named last changes fastest.
Arguments:
- patches: bfloat16 [8, 832, 768], P('dp', 'fsdp'), may hold values from -6 to 6
- segment_ids: int32 [8, 832], P('dp', 'fsdp'), may hold values from 0 to 9, as said below
- live: int32 [8, 832], P('dp', 'fsdp'), may hold values from 0 to 1, as said below
- expert_ids: int32 [8, 832, 2], P('dp', 'fsdp'), may hold values from 0 to 7, as said below
- ranks: int32 [8, 832, 2], P('dp', 'fsdp'), may hold values from 0 to 55, as said below
- norm_gains: bfloat16 [4, 768], P(None, ('dp', 'fsdp')), may hold values from 0.099609375 to 1.8984375
- norm_biases: bfloat16 [4, 768], P(None, ('dp', 'fsdp')), may hold values from -1.75 to 1.75
- attn_qkv: bfloat16 [2, 768, 2304], P(None, ('dp', 'fsdp')), may hold values from -0.21875 to 0.21875
- attn_out: bfloat16 [2, 768, 768], P(None, ('dp', 'fsdp')), may hold values from -1.75 to 1.75
- mlp_in: bfloat16 [768, 3072], P(('dp', 'fsdp')), may hold values from -0.21875 to 0.21875
- mlp_out: bfloat16 [3072, 768], P(('dp', 'fsdp')), may hold values from -0.21875 to 0.21875
- router: bfloat16 [768, 8], P(('dp', 'fsdp')), may hold values from -0.109375 to 0.109375
- exp_in: bfloat16 [8, 768, 3072], P(None, ('dp', 'fsdp')), may hold values from -0.21875 to 0.21875
- exp_out: bfloat16 [8, 3072, 768], P(None, ('dp', 'fsdp')), may hold values from -0.4375 to 0.4375
- cotangent: bfloat16 [8, 832, 768], P('dp', 'fsdp'), may hold values from -6 to 6
Outputs:
- activations: bfloat16 [8, 832, 768], P('dp', 'fsdp')
- patch_grads: float32 [8, 832, 768], P('dp', 'fsdp')
- gain_grads: float32 [4, 768], P(None, ('dp', 'fsdp'))
- bias_grads: float32 [3, 768], P(None, ('dp', 'fsdp'))
- moe_bias_grad: float32 [768], P(('dp', 'fsdp'))
- qkv_grads: float32 [2, 768, 2304], P(None, ('dp', 'fsdp'))
- proj_grads: float32 [2, 768, 768], P(None, ('dp', 'fsdp'))
- mlp_in_grads: float32 [768, 3072], P(('dp', 'fsdp'))
- mlp_out_grads: float32 [3072, 768], P(('dp', 'fsdp'))
- router_grads: float32 [768, 8], P(('dp', 'fsdp'))
- exp_in_grads: float32 [8, 768, 3072], P(None, ('dp', 'fsdp'))
- exp_out_grads: float32 [8, 3072, 768], P(None, ('dp', 'fsdp'))
The draws below stay inside these ranges and needn't reach their ends.
Inputs may be any that keep to these rules, and one draw needn't show every extreme that they name: `segment_ids`: within a row segment numbers never fall and each image is contiguous, numbered from 0; every row ends with padding, at least its last patch, and every padded patch carries segment number 9, which no live patch shares. In each group of 1 row of one dp index one row, drawn from the seed, begins with an image from patch 0 past patch 3 * 208. `live`: padding only at the end of a row. `expert_ids`: A patch's two experts differ; every expert is named. For the patches of one device and each expert, the live choices naming that expert, all first choices before all second ones and earlier patches first, hold ranks 0, 1, 2, ... in order; 55 marks a choice dropped by capacity and every choice of a padded patch.
All inputs are finite; a program needn't handle non-finite values.
Results may differ from the reference program's by a relative error of at most 0.028.
Values may be sent and summed in bfloat16 or wider, within the bound.
No kernel may reach another device: no remote copies, remote signals or barrier semaphores. Data moves between devices by JAX's collectives and lax.ppermute only.
A program may use at most 512 MiB of HBM per device.

```python
import jax
import jax.numpy as jnp
from jax import lax

D = 768
HEADS = 12
HD = 64
FF = 3072
E = 8
LEN = 832
SEQ_DP = 1
PATCH_DEV = 208
TOK_DEV = 208
ROWS = 8
CAP = 55
N_DP = 8
N_FSDP = 4


def layout(key):
    key = jax.random.fold_in(key, 11)
    key_len, key_row, key_big = jax.random.split(key, 3)
    pieces = 10
    lengths = jax.random.randint(key_len, (ROWS, pieces), LEN // 8, LEN // 2 + 1)
    chosen = jax.random.randint(key_row, (ROWS // SEQ_DP,), 0, SEQ_DP)
    is_big = jnp.arange(ROWS) % SEQ_DP == jnp.repeat(chosen, SEQ_DP)
    big_length = jax.random.randint(key_big, (ROWS,), 3 * LEN // 4 + 1, 7 * LEN // 8 + 1)
    first_len = jnp.where(is_big, big_length, lengths[:, 0])
    lengths = jnp.concatenate([first_len[:, None], lengths[:, 1:]], axis=1)
    bounds = jnp.cumsum(lengths, axis=1)
    finish = jnp.max(jnp.where(bounds <= LEN - 1, bounds, 0), axis=1)
    position = jnp.arange(LEN)
    segment = jnp.sum((bounds[:, None, :] <= position[None, :, None]).astype(jnp.int32), axis=2)
    alive = (position[None, :] < finish[:, None]).astype(jnp.int32)
    segment = jnp.where(alive > 0, segment, pieces - 1)
    return (segment.astype(jnp.int32), alive)


def block_view(array):
    rest = array.shape[2:]
    array = array.reshape((ROWS // SEQ_DP, SEQ_DP, LEN // PATCH_DEV, PATCH_DEV) + rest)
    array = jnp.swapaxes(array, 1, 2)
    return array.reshape((ROWS // SEQ_DP * (LEN // PATCH_DEV), TOK_DEV) + rest)


def row_view(array):
    rest = array.shape[2:]
    array = array.reshape((ROWS // SEQ_DP, LEN // PATCH_DEV, SEQ_DP, PATCH_DEV) + rest)
    array = jnp.swapaxes(array, 1, 2)
    return array.reshape((ROWS, LEN) + rest)


def routing(key):
    segment, alive = layout(key)
    key = jax.random.fold_in(key, 23)
    key_one, key_two, key_perm, key_off = jax.random.split(key, 4)
    low_pick = jnp.minimum(jax.random.randint(key_one, (ROWS, LEN), 0, E), jax.random.randint(key_two, (ROWS, LEN), 0, E))
    labels = jax.random.permutation(key_perm, E)
    first_pick = labels[low_pick]
    offset = jax.random.randint(key_off, (ROWS, LEN), 1, E)
    second_pick = (first_pick + offset) % E
    picks = jnp.stack([first_pick, second_pick], axis=-1).astype(jnp.int32)
    block_picks = block_view(picks)
    block_alive = block_view(alive)
    blocks = block_picks.shape[0]
    order = jnp.swapaxes(block_picks, 1, 2).reshape(blocks, 2 * TOK_DEV)
    order_alive = jnp.concatenate([block_alive, block_alive], axis=1)
    onehot = (order[:, :, None] == jnp.arange(E)[None, None, :]).astype(jnp.int32) * order_alive[:, :, None]
    before = jnp.cumsum(onehot, axis=1) - onehot
    slot_rank = jnp.sum(before * onehot, axis=2)
    slot_rank = jnp.where(order_alive > 0, jnp.minimum(slot_rank, CAP), CAP)
    slot_rank = jnp.swapaxes(slot_rank.reshape(blocks, 2, TOK_DEV), 1, 2)
    return (picks, row_view(slot_rank).astype(jnp.int32))


def draw_segment_ids(key, part):
    segment, alive = layout(key)
    return segment


def draw_live(key, part):
    segment, alive = layout(key)
    return alive


def draw_expert_ids(key, part):
    picks, slot_rank = routing(key)
    return picks


def draw_ranks(key, part):
    picks, slot_rank = routing(key)
    return slot_rank


def shard_levels(rng, dims, cuts, low, top_value):
    level, own = 1.0, jax.random.fold_in(rng, 6)
    for dim, parts in cuts:
        steps = jnp.exp(jax.random.uniform(jax.random.fold_in(own, dim), (parts,), jnp.float32, low / len(cuts), top_value / len(cuts)))
        level = level * jnp.repeat(steps, dims[dim] // parts).reshape([-1 if axis == dim else 1 for axis in range(len(dims))])
    return level


def normal_values(rng, dims, width, bound, cuts=(), kind=jnp.bfloat16):
    entries = jax.random.normal(rng, dims, jnp.float32) * width
    if len(cuts) > 0:
        entries = shard_levels(rng, dims, cuts, -0.22, 0.18) * entries
    return jnp.clip(entries, min=-bound, max=bound).astype(kind)


def setup_inputs(seed: int = 0) -> dict:
    arg_keys = jax.random.split(jax.random.key(seed), 16)
    patches = normal_values(arg_keys[0], (ROWS, LEN, D), 1.0, 6.0, ((0, 8), (1, 4)))
    segment_ids = draw_segment_ids(jax.random.fold_in(arg_keys[15], 71), 0)
    live = draw_live(jax.random.fold_in(arg_keys[15], 71), 0)
    expert_ids = draw_expert_ids(jax.random.fold_in(arg_keys[15], 71), 0)
    ranks = draw_ranks(jax.random.fold_in(arg_keys[15], 71), 0)
    norm_gains = jnp.clip(1.0 + 0.18 * jax.random.normal(arg_keys[5], (4, D), jnp.float32), 0.099609375, 1.8984375).astype(jnp.bfloat16)
    norm_biases = normal_values(arg_keys[6], (4, D), 0.3, 1.75, ((1, 32),))
    attn_qkv = normal_values(arg_keys[7], (2, D, 3 * D), D ** -0.5, 0.21875, ((1, 32),))
    attn_out = normal_values(arg_keys[8], (2, D, D), (D // 64) ** -0.5, 1.75, ((1, 32),))
    mlp_in = normal_values(arg_keys[9], (D, FF), D ** -0.5, 0.21875, ((0, 32),))
    mlp_out = normal_values(arg_keys[10], (FF, D), (FF // 4) ** -0.5, 0.21875, ((0, 32),))
    router = normal_values(arg_keys[11], (D, E), (4 * D) ** -0.5, 0.109375, ((0, 32),))
    exp_in = normal_values(arg_keys[12], (E, D, FF), D ** -0.5, 0.21875, ((1, 32),))
    exp_out = normal_values(arg_keys[13], (E, FF, D), (FF // 16) ** -0.5, 0.4375, ((1, 32),))
    cotangent = normal_values(arg_keys[14], (ROWS, LEN, D), 1.0, 6.0, ((0, 8), (1, 4)))
    return dict(patches=patches, segment_ids=segment_ids, live=live, expert_ids=expert_ids, ranks=ranks, norm_gains=norm_gains, norm_biases=norm_biases, attn_qkv=attn_qkv, attn_out=attn_out, mlp_in=mlp_in, mlp_out=mlp_out, router=router, exp_in=exp_in, exp_out=exp_out, cotangent=cotangent)


PRECISE = lax.Precision.HIGHEST
EPSILON = 1e-06

@jax.custom_vjp
def low(v):
    return lax.optimization_barrier(v.astype(jnp.bfloat16)).astype(jnp.float32)

@jax.custom_vjp
def low_back(v):
    return v

def low_keep(v):
    return (low(v), None)

def low_pass(kept, grad):
    return (grad,)

def back_keep(v):
    return (v, None)

def back_low(kept, grad):
    return (low(grad),)
low.defvjp(low_keep, low_pass)
low_back.defvjp(back_keep, back_low)

def normalize(state, norm_gain, norm_bias):
    centre = lax.optimization_barrier(jnp.mean(state, axis=-1, keepdims=True))
    centred = state - centre
    spread = lax.optimization_barrier(jnp.mean(centred * centred, axis=-1, keepdims=True))
    return centred * lax.rsqrt(spread + EPSILON) * norm_gain + norm_bias

def attend_row(block_items):
    queries, keys_row, values, seg_row, live_row = block_items
    scores = jnp.einsum('qhd,khd->hqk', queries, keys_row, precision=PRECISE) * HD ** (-0.5)
    scores = low_back(scores)
    allowed = seg_row[:, None] == seg_row[None, :]
    scores = jnp.where(allowed[None], scores, -1e+30)
    weights = jax.nn.softmax(scores, axis=-1)
    mixed = jnp.einsum('hqk,khd->qhd', low(weights), values, precision=PRECISE)
    return mixed * live_row[:, None, None]

def attention(state, segment_ids, live_rows, norm_gain, norm_bias, w_qkv, w_out):
    row_count = state.shape[0]
    normed = low(normalize(state, norm_gain, norm_bias))
    mixed_all = jnp.einsum('rld,de->rle', normed, w_qkv, precision=PRECISE)
    mixed_all = low_back(low(mixed_all))
    queries = mixed_all[..., :D].reshape(row_count, LEN, HEADS, HD)
    keys_all = mixed_all[..., D:2 * D].reshape(row_count, LEN, HEADS, HD)
    values = mixed_all[..., 2 * D:].reshape(row_count, LEN, HEADS, HD)
    heads_out = lax.map(jax.checkpoint(attend_row), (queries, keys_all, values, segment_ids, live_rows))
    heads_out = low_back(low(heads_out.reshape(row_count, LEN, D)))
    branch = low_back(jnp.einsum('rld,de->rle', heads_out, w_out, precision=PRECISE))
    return state + branch

def dense_ffn(state, norm_gain, norm_bias, w_in, w_back):
    normed = low(normalize(state, norm_gain, norm_bias))
    inner_pre = low_back(jnp.einsum('rld,df->rlf', normed, w_in, precision=PRECISE))
    hidden = low(jax.nn.gelu(inner_pre, approximate=False))
    branch = low_back(jnp.einsum('rlf,fd->rld', hidden, w_back, precision=PRECISE))
    return state + branch

def to_blocks(array):
    rest = array.shape[2:]
    array = array.reshape((N_DP, SEQ_DP, N_FSDP, PATCH_DEV) + rest)
    array = jnp.swapaxes(array, 1, 2)
    return array.reshape((N_DP * N_FSDP, TOK_DEV) + rest)

def from_blocks(array):
    rest = array.shape[2:]
    array = array.reshape((N_DP, N_FSDP, SEQ_DP, PATCH_DEV) + rest)
    array = jnp.swapaxes(array, 1, 2)
    return array.reshape((ROWS, LEN) + rest)

def experts_block(block_items, w_router, w_in, w_back):
    normed, choice_ids, rank_ids = block_items
    logits = low_back(jnp.dot(normed, w_router, precision=PRECISE))
    softmax_rows = jax.nn.softmax(logits, axis=-1)
    choose = (choice_ids[:, :, None] == jnp.arange(E)[None, None, :]).astype(jnp.float32)
    slot_hot = (rank_ids[:, :, None] == jnp.arange(CAP)[None, None, :]).astype(jnp.float32)
    kept_mask = (rank_ids < CAP).astype(jnp.float32)
    gate_low = low(lax.optimization_barrier(jnp.sum(softmax_rows[:, None, :] * choose, axis=-1)) * kept_mask)
    dispatch = jnp.einsum('tke,tkc->tec', choose, slot_hot, precision=PRECISE)
    combine = jnp.einsum('tk,tke,tkc->tec', gate_low, choose, slot_hot, precision=PRECISE)
    slot_rows = low_back(jnp.einsum('tec,td->ecd', dispatch, normed, precision=PRECISE))
    inner_pre = low_back(jnp.einsum('ecd,edf->ecf', slot_rows, w_in, precision=PRECISE))
    hidden = low(jax.nn.gelu(inner_pre, approximate=False))
    result = low_back(low(jnp.einsum('ecf,efd->ecd', hidden, w_back, precision=PRECISE)))
    return jnp.einsum('tec,ecd->td', combine, result, precision=PRECISE)

def reference(patches, segment_ids, live, expert_ids, ranks, norm_gains, norm_biases, attn_qkv, attn_out, mlp_in, mlp_out, router, exp_in, exp_out, cotangent):
    live_rows = live.astype(jnp.float32)

    def forward(start, gains, biases, w_qkv, w_out, w_in, w_back, w_router, expert_in, expert_back):
        state = attention(start, segment_ids, live_rows, gains[0], biases[0], w_qkv[0], w_out[0])
        state = dense_ffn(state, gains[1], biases[1], w_in, w_back)
        state = attention(state, segment_ids, live_rows, gains[2], biases[2], w_qkv[1], w_out[1])
        normed = low(normalize(state, gains[3], biases[3]))

        def expert_step(block_items):
            return experts_block(block_items, w_router, expert_in, expert_back)
        mixed_blocks = lax.map(jax.checkpoint(expert_step), (to_blocks(normed), to_blocks(expert_ids), to_blocks(ranks)))
        return state + low_back(from_blocks(mixed_blocks))
    inputs = tuple((argument.astype(jnp.float32) for argument in (patches, norm_gains, norm_biases, attn_qkv, attn_out, mlp_in, mlp_out, router, exp_in, exp_out)))
    result, pullback = jax.vjp(forward, *inputs)
    grads = pullback(cotangent.astype(jnp.float32))
    return (result.astype(jnp.bfloat16), grads[0], grads[1], grads[2][:3], grads[2][3], grads[3], grads[4], grads[5], grads[6], grads[7], grads[8], grads[9])
```

```python
import jax
import jax.numpy as jnp
from jax import lax
from jax.sharding import PartitionSpec as P

HEADS = 12
HD = 64
EPSILON = 1e-06
NF = 4
ALL = ("dp", "fsdp")
BF = jnp.bfloat16
F32 = jnp.float32


def mm(left, right):
    return jnp.dot(left, right, preferred_element_type=F32)


def mm_tn(left, right):
    return lax.dot_general(left, right, (((0,), (0,)), ((), ())), preferred_element_type=F32)


def mm_nt(left, right):
    return lax.dot_general(left, right, (((1,), (1,)), ((), ())), preferred_element_type=F32)


def gelu(values):
    return 0.5 * values * (1.0 + lax.erf(values * (0.5**0.5)))


def gelu_slope(values):
    cdf = 0.5 * (1.0 + lax.erf(values * (0.5**0.5)))
    return cdf + values * jnp.exp(-0.5 * values * values) * 0.3989422804014327


def scale_rows(rows):
    centre = jnp.mean(rows, axis=-1, keepdims=True)
    centred = rows - centre
    inv_scale = lax.rsqrt(jnp.mean(centred * centred, axis=-1, keepdims=True) + EPSILON)
    return centred * inv_scale, inv_scale


def norm_back(out_grad, scaled, inv_scale, gain):
    weighted = out_grad * gain
    return inv_scale * (
        weighted
        - jnp.mean(weighted, axis=-1, keepdims=True)
        - scaled * jnp.mean(weighted * scaled, axis=-1, keepdims=True)
    )


def swap(value, bits):
    return lax.ppermute(value, "fsdp", [(i, i ^ bits) for i in range(NF)])


def gather_row(block):
    across = swap(block, 2)
    beside = swap(block, 1)
    corner = swap(across, 1)
    return jnp.concatenate([block, beside, across, corner], axis=0)


def scatter_row(partial):
    blocks = partial.reshape((NF, -1) + partial.shape[1:])
    send = jnp.stack([blocks[1], blocks[3]]).astype(BF)
    got = swap(send, 1).astype(F32)
    far = swap((blocks[2] + got[1]).astype(BF), 2).astype(F32)
    return blocks[0] + got[0] + far


def exchange(value, axes, groups=None):
    return lax.all_to_all(value, axes, 0, 0, axis_index_groups=groups, tiled=True)


def attend(qkv, code_row, live_all):
    tokens = qkv.shape[0]
    heads = HEADS // NF
    parts = qkv.reshape(tokens, 3, heads, HD)
    allowed = (code_row[:, None] == code_row[None, :])[None]
    scores = jnp.einsum("qhd,khd->hqk", parts[:, 0], parts[:, 1], preferred_element_type=F32)
    scores = jnp.where(allowed, scores * HD**-0.5, -1e30)
    top = jnp.max(scores, axis=-1, keepdims=True)
    shifted = jnp.exp(scores - top)
    total = jnp.sum(shifted, axis=-1, keepdims=True)
    low = (shifted / total).astype(BF)
    out = jnp.einsum("hqk,khd->qhd", low, parts[:, 2], preferred_element_type=F32)
    out = (out.reshape(tokens, heads * HD) * live_all[:, None]).astype(BF)
    return out, top + jnp.log(total)


def attend_back(qkv, out_grad, lse, code_row):
    tokens = qkv.shape[0]
    heads = HEADS // NF
    parts = qkv.reshape(tokens, 3, heads, HD)
    out_grad = out_grad.reshape(tokens, heads, HD)
    allowed = (code_row[:, None] == code_row[None, :])[None]
    scores = jnp.einsum("qhd,khd->hqk", parts[:, 0], parts[:, 1], preferred_element_type=F32)
    soft = jnp.exp(jnp.where(allowed, scores * HD**-0.5, -1e30) - lse)
    values_grad = jnp.einsum("hqk,qhd->khd", soft.astype(BF), out_grad, preferred_element_type=F32)
    soft_grad = jnp.einsum("qhd,khd->hqk", out_grad, parts[:, 2], preferred_element_type=F32)
    row_dot = jnp.sum(soft * soft_grad, axis=-1, keepdims=True)
    score_grad = (soft * (soft_grad - row_dot)).astype(BF)
    query_grad = jnp.einsum("hqk,khd->qhd", score_grad, parts[:, 1], preferred_element_type=F32)
    keys_grad = jnp.einsum("hqk,qhd->khd", score_grad, parts[:, 0], preferred_element_type=F32)
    scale = HD**-0.5
    grads = jnp.stack([query_grad * scale, keys_grad * scale, values_grad], axis=1)
    return grads.astype(BF).reshape(tokens, 3 * heads * HD)


def make_shards(n_dp):
    n_all = n_dp * NF

    def shards(
        patches, segment_ids, live, expert_ids, ranks, norm_gains, norm_biases, attn_qkv, attn_out,
        mlp_in, mlp_out, router, exp_in, exp_out, cotangent,
    ):
        width = patches.shape[-1]
        tokens = patches.shape[0] * patches.shape[1]
        experts = exp_in.shape[0]
        clones = n_dp // experts
        part = width // NF
        rows = attn_qkv.shape[1]
        hid = mlp_out.shape[0]
        own_f = lax.axis_index("fsdp")
        own_dp = lax.axis_index("dp")
        groups = ring = None
        if clones > 1:
            groups = [[g * experts + e for e in range(experts)] for g in range(clones)]
            ring = [[g * experts + e for g in range(clones)] for e in range(experts)]
        capacity = (210 * tokens + 100 * experts - 1) // (100 * experts)
        slots = (capacity + 7) // 8 * 8

        code = (segment_ids * 2 + live).reshape(tokens)
        code_all = gather_row(code)
        live_all = (code_all % 2).astype(F32)
        rows_all = gather_row(patches.reshape(tokens, width))

        def qkv_block(layer):
            weight = attn_qkv[layer].reshape(rows, 3, NF, part)
            return jnp.transpose(weight, (2, 0, 1, 3)).reshape(NF, rows, 3 * part)

        def to_everyone(blocks):
            full = jnp.broadcast_to(blocks[None], (n_dp,) + blocks.shape)
            full = full.reshape((n_all,) + blocks.shape[1:])
            return exchange(full, ALL).reshape((n_all * blocks.shape[1],) + blocks.shape[2:])

        small = jnp.concatenate(
            [norm_gains.T, norm_biases.T, router, jnp.zeros((rows, 128 - 8 - experts), BF)], axis=1
        )
        first = to_everyone(
            jnp.concatenate([jnp.broadcast_to(small[None], (NF, rows, 128)), qkv_block(0)], axis=2)
        )
        small_all, w_qkv0 = first[:, :128], first[:, 128:]
        norms = small_all[:, :8].T.astype(F32)
        gains, biases = norms[:4], norms[4:]
        w_router = small_all[:, 8 : 8 + experts]
        w_out0 = lax.all_gather(attn_out[0], ALL, axis=0, tiled=True)
        w_out1 = lax.all_gather(attn_out[1], ALL, axis=0, tiled=True)

        mlp_block = jnp.transpose(mlp_in.reshape(rows, n_dp, NF, hid), (2, 0, 1, 3))
        w_mlp_in = to_everyone(mlp_block.reshape(NF, rows, n_dp * hid))
        w_mlp_out = lax.all_gather(mlp_out, "dp", axis=0, tiled=True)
        w_qkv1 = to_everyone(qkv_block(1))

        in_block = jnp.transpose(exp_in.reshape(experts, rows, n_dp, NF, hid), (0, 3, 1, 2, 4))
        in_block = in_block.reshape(experts * NF, rows, n_dp * hid)
        if clones == 1:
            w_exp_in = exchange(in_block, ALL).reshape(width, n_dp * hid)
        else:
            held = in_block.reshape(experts, NF, rows, n_dp * hid)
            held = exchange(jnp.swapaxes(held, 0, 1), "fsdp")
            held = exchange(jnp.swapaxes(held, 0, 1), "dp", groups)
            w_exp_in = lax.all_gather(held, "dp", axis_index_groups=ring).reshape(width, n_dp * hid)
        w_exp_out = exchange(exp_out, "dp", groups)
        if clones > 1:
            w_exp_out = lax.all_gather(w_exp_out, "dp", axis_index_groups=ring)
        w_exp_out = w_exp_out.reshape(n_dp * hid, width)

        choice = expert_ids.reshape(tokens, 2)
        rank = ranks.reshape(tokens, 2)
        place = jnp.where(rank < capacity, choice * slots + rank, -1)
        slot_index = jnp.arange(experts * slots, dtype=jnp.int32)[:, None]
        pick = (place[:, 0][None] == slot_index) | (place[:, 1][None] == slot_index)
        pick = pick.astype(BF)

        def to_experts(block):
            held = mm(pick, block).astype(BF).reshape(experts, slots, width)
            return gather_row(exchange(held, "dp", groups).reshape(experts * slots, width))

        def from_experts(partial):
            held = scatter_row(partial).astype(BF).reshape(experts, slots, width)
            held = exchange(held, "dp", groups).reshape(experts * slots, width)
            return mm_tn(pick, held)

        top_grad = cotangent.reshape(tokens, width)
        dz = to_experts(top_grad)

        def out_project(out, weight):
            blocks = out.reshape(NF, tokens, part)
            total = None
            for k in range(NF):
                got = blocks[0] if k == 0 else swap(blocks[k], k)
                piece = lax.dynamic_slice_in_dim(weight, (own_f ^ k) * part, part, 0)
                term = mm(got, piece)
                total = term if total is None else total + term
            return total

        h0 = patches.reshape(tokens, width).astype(F32)
        xhat0_all, _ = scale_rows(rows_all.astype(F32))
        a0 = (xhat0_all * gains[0] + biases[0]).astype(BF)
        qkv0 = mm(a0, w_qkv0).astype(BF)
        o0, lse0 = attend(qkv0, code_all, live_all)
        h1 = h0 + out_project(o0, w_out0)

        xhat1, inv1 = scale_rows(h1)
        c0 = gather_row((xhat1 * gains[1] + biases[1]).astype(BF))
        u0 = mm(c0, w_mlp_in)
        g0 = gelu(u0).astype(BF)
        h2 = h1 + scatter_row(mm(g0, w_mlp_out))

        xhat2, inv2 = scale_rows(h2)
        a1 = gather_row((xhat2 * gains[2] + biases[2]).astype(BF))
        qkv1 = mm(a1, w_qkv1).astype(BF)
        o1, lse1 = attend(qkv1, code_all, live_all)
        h3 = h2 + out_project(o1, w_out1)

        xhat3, inv3 = scale_rows(h3)
        x = to_experts((xhat3 * gains[3] + biases[3]).astype(BF))
        probs = jax.nn.softmax(mm(x, w_router), axis=-1)
        mine = (jnp.arange(experts) == own_dp % experts).astype(F32)[None]
        prob = jnp.sum(probs * mine, axis=-1, keepdims=True)
        gate = prob.astype(BF).astype(F32)
        ue = mm(x, w_exp_in)
        ge = gelu(ue).astype(BF)
        y = mm(ge, w_exp_out)
        dyx = (gate * dz.astype(F32)).astype(BF)
        due = (mm_nt(dyx, w_exp_out) * gelu_slope(ue)).astype(BF)
        dgate = jnp.sum(dz.astype(F32) * y, axis=-1, keepdims=True)
        dlogits = (dgate * prob * (mine - probs)).astype(BF)
        dx = mm_nt(due, w_exp_in) + mm_nt(dlogits, w_router)
        router_part = mm_tn(x, dlogits)
        exp_in_part = mm_tn(x, due).astype(BF)
        exp_out_part = mm_tn(ge, dyx).astype(BF)

        dc1 = from_experts(dx)
        h4 = h3 + from_experts(gate * y)
        activations = h4.astype(BF)

        if clones == 1:
            got = exchange(exp_in_part.reshape(n_all, rows, n_dp * hid), ALL)
            got = got.reshape(experts, NF, rows, n_dp, hid)
            exp_in_grads = jnp.transpose(got, (0, 2, 3, 1, 4)).reshape(experts, rows, n_dp * NF * hid)
            got = exchange(exp_out_part.reshape(experts, hid, width), "dp")
            exp_out_grads = got.astype(F32)
        else:
            held = lax.psum_scatter(
                exp_in_part.reshape(clones, experts, NF, rows, n_dp * hid), "dp", axis_index_groups=ring
            )
            held = exchange(held, "dp", groups)
            held = exchange(jnp.swapaxes(held, 0, 1), "fsdp")
            got = held.reshape(NF, experts, rows, n_dp, hid)
            exp_in_grads = jnp.transpose(got, (1, 2, 3, 0, 4)).reshape(experts, rows, n_dp * NF * hid)
            held = lax.psum_scatter(
                exp_out_part.reshape(clones, experts, hid, width), "dp", axis_index_groups=ring
            )
            exp_out_grads = exchange(held, "dp", groups).astype(F32)
        exp_in_grads = exp_in_grads.astype(F32)

        def rows_to_owners(grad):
            cols = grad.shape[1]
            got = exchange(grad.astype(BF).reshape(n_all, rows, cols), ALL)
            return got.reshape(n_dp, NF, rows, cols).astype(F32)

        def qkv_layout(total):
            parts = total.reshape(NF, rows, 3, part)
            return jnp.transpose(parts, (1, 2, 0, 3)).reshape(rows, 3 * width)

        def out_to_owners(grad):
            got = exchange(grad.astype(BF).reshape(n_dp, rows, width), "dp")
            total = jnp.sum(got.astype(F32), axis=0)
            route = []
            for d in range(n_dp):
                for f in range(NF):
                    route.append((d * NF + f, f * n_dp + d))
            return lax.ppermute(total, ALL, route)

        def attention_back(grad, qkv, out, lse, a_all, w_qkv, w_out):
            dy = gather_row(grad.astype(BF))
            w_mine = lax.dynamic_slice_in_dim(w_out, own_f * part, part, 0)
            do = (mm_nt(dy, w_mine) * live_all[:, None]).astype(BF)
            out_part = mm_tn(out, dy)
            dqkv = attend_back(qkv, do, lse, code_all)
            return mm_nt(dqkv, w_qkv), mm_tn(a_all, dqkv), out_part

        def sums(out_grad, xhat):
            return jnp.sum(out_grad * xhat, axis=0), jnp.sum(out_grad, axis=0)

        gain3, bias3 = sums(dc1, xhat3)
        grad = top_grad.astype(F32) + norm_back(dc1, xhat3, inv3, gains[3])

        da1, qkv_part1, out_part1 = attention_back(grad, qkv1, o1, lse1, a1, w_qkv1, w_out1)
        proj1 = out_to_owners(out_part1)
        qkv_grad1 = qkv_layout(jnp.sum(rows_to_owners(qkv_part1), axis=0))
        da1 = scatter_row(da1)
        gain2, bias2 = sums(da1, xhat2)
        grad = grad + norm_back(da1, xhat2, inv2, gains[2])

        dm = gather_row(grad.astype(BF))
        du0 = (mm_nt(dm, w_mlp_out) * gelu_slope(u0)).astype(BF)
        mlp_out_part = mm_tn(g0, dm).astype(BF).reshape(n_dp, hid, width)
        mlp_out_grads = jnp.sum(exchange(mlp_out_part, "dp").astype(F32), axis=0)
        mlp_in_part = jnp.sum(rows_to_owners(mm_tn(c0, du0)), axis=0)
        mlp_in_part = mlp_in_part.reshape(NF, rows, n_dp, hid)
        mlp_in_grads = jnp.transpose(mlp_in_part, (1, 2, 0, 3)).reshape(rows, n_dp * NF * hid)
        dc0 = scatter_row(mm_nt(du0, w_mlp_in))
        gain1, bias1 = sums(dc0, xhat1)
        grad = grad + norm_back(dc0, xhat1, inv1, gains[1])

        da0, qkv_part0, out_part0 = attention_back(grad, qkv0, o0, lse0, a0, w_qkv0, w_out0)
        proj0 = out_to_owners(out_part0)
        gain0, bias0 = sums(da0, xhat0_all)
        columns = jnp.stack([gain0, gain1, gain2, gain3, bias0, bias1, bias2, bias3], axis=1)
        columns = jnp.concatenate(
            [columns, router_part, jnp.zeros((width, 128 - 8 - experts), F32), qkv_part0], axis=1
        )
        got = rows_to_owners(columns)
        total = jnp.sum(got, axis=0)
        small_grads = jnp.sum(total[:, :, :128], axis=0)
        qkv_grad0 = qkv_layout(total[:, :, 128:])
        da0 = scatter_row(da0)
        xhat0, inv0 = scale_rows(h0)
        grad = grad + norm_back(da0, xhat0, inv0, gains[0])

        norm_grads = small_grads[:, :8].T
        return (
            activations.reshape(patches.shape),
            grad.reshape(patches.shape),
            norm_grads[:4],
            norm_grads[4:7],
            norm_grads[7],
            jnp.stack([qkv_grad0, qkv_grad1]),
            jnp.stack([proj0, proj1]),
            mlp_in_grads,
            mlp_out_grads,
            small_grads[:, 8 : 8 + experts],
            exp_in_grads,
            exp_out_grads,
        )

    return shards


def solution(mesh):
    by_row = P("dp", "fsdp", None)
    second = P(None, ("dp", "fsdp"), None)
    first = P(("dp", "fsdp"), None)
    pair = P("dp", "fsdp")
    norm = P(None, ("dp", "fsdp"))
    return jax.shard_map(
        make_shards(mesh.shape["dp"]),
        mesh=mesh,
        in_specs=(
            by_row, pair, pair, by_row, by_row, norm, norm, second, second, first, first, first,
            second, second, by_row,
        ),
        out_specs=(
            by_row, by_row, norm, norm, P(("dp", "fsdp")), second, second, first, first, first,
            second, second,
        ),
        check_vma=False,
    )
```

```python
import functools

import jax
import jax.numpy as jnp
from jax import lax
from jax.experimental import pallas as pl
from jax.experimental.pallas import tpu as pltpu
from jax.sharding import PartitionSpec as P

HEADS = 12
HD = 64
EPSILON = 1e-06
NF = 4
ALL = ("dp", "fsdp")
BF = jnp.bfloat16
F32 = jnp.float32


def mm(left, right):
    return jnp.dot(left, right, preferred_element_type=F32)


def mm_tn(left, right):
    return lax.dot_general(left, right, (((0,), (0,)), ((), ())), preferred_element_type=F32)


def mm_nt(left, right):
    return lax.dot_general(left, right, (((1,), (1,)), ((), ())), preferred_element_type=F32)


def gelu(values):
    return 0.5 * values * (1.0 + lax.erf(values * (0.5**0.5)))


def gelu_slope(values):
    cdf = 0.5 * (1.0 + lax.erf(values * (0.5**0.5)))
    return cdf + values * jnp.exp(-0.5 * values * values) * 0.3989422804014327


def scale_rows(rows):
    centre = jnp.mean(rows, axis=-1, keepdims=True)
    centred = rows - centre
    inv_scale = lax.rsqrt(jnp.mean(centred * centred, axis=-1, keepdims=True) + EPSILON)
    return centred * inv_scale, inv_scale


def norm_back(out_grad, scaled, inv_scale, gain):
    weighted = out_grad * gain
    return inv_scale * (
        weighted
        - jnp.mean(weighted, axis=-1, keepdims=True)
        - scaled * jnp.mean(weighted * scaled, axis=-1, keepdims=True)
    )


def swap(value, bits):
    return lax.ppermute(value, "fsdp", [(i, i ^ bits) for i in range(NF)])


def gather_blocks(block):
    across = swap(block, 2)
    beside = swap(block, 1)
    corner = swap(across, 1)
    return [block, beside, across, corner]


def gather_row(block):
    return jnp.concatenate(gather_blocks(block), axis=0)


def scatter_blocks(send, keep):
    got = swap(send, 1).astype(F32)
    far = swap((keep[1] + got[1]).astype(BF), 2).astype(F32)
    return keep[0] + got[0] + far


def scatter_row(partial):
    blocks = partial.reshape((NF, -1) + partial.shape[1:])
    return scatter_blocks(jnp.stack([blocks[1], blocks[3]]).astype(BF), (blocks[0], blocks[2]))


def after(value, *others):
    return lax.optimization_barrier((value,) + others)[0]


def deal(blocks):
    own = lax.axis_index("fsdp")
    got = []
    for k in range(NF):
        block = lax.dynamic_index_in_dim(blocks, own ^ k, 0, keepdims=False)
        got.append(block if k == 0 else swap(block, k))
    odd, far = own % 2 == 1, own >= 2
    got = [jnp.where(odd, got[k ^ 1], got[k]) for k in range(NF)]
    return jnp.stack([jnp.where(far, got[k ^ 2], got[k]) for k in range(NF)])


def exchange(value, axes, groups=None):
    return lax.all_to_all(value, axes, 0, 0, axis_index_groups=groups, tiled=True)


def dot(left, right, left_dim, right_dim):
    dims = (((left_dim,), (right_dim,)), ((), ()))
    return lax.dot_general(left, right, dims, preferred_element_type=F32)


def attend_kernel(qkv_ref, col_ref, row_ref, out_ref, lse_ref, *, heads):
    part = heads * HD
    live = (col_ref[...] % 2).astype(F32)
    for h in range(heads):
        q = qkv_ref[:, h * HD : (h + 1) * HD] * BF(HD**-0.5)
        k = qkv_ref[:, part + h * HD : part + (h + 1) * HD]
        v = qkv_ref[:, 2 * part + h * HD : 2 * part + (h + 1) * HD]
        scores = jnp.where(col_ref[...] == row_ref[...], dot(k, q, 1, 1), -1e30)
        top = jnp.max(scores, axis=0, keepdims=True)
        shifted = jnp.exp(scores - top)
        total = jnp.sum(shifted, axis=0, keepdims=True)
        soft = (shifted * (1.0 / total)).astype(BF)
        out_ref[:, h * HD : (h + 1) * HD] = (dot(soft, v, 0, 0) * live).astype(BF)
        lse_ref[h : h + 1] = top + jnp.log(total)


def attend_back_kernel(qkv_ref, do_ref, lse_ref, col_ref, row_ref, out_ref, *, heads):
    part = heads * HD
    for h in range(heads):
        q = qkv_ref[:, h * HD : (h + 1) * HD] * BF(HD**-0.5)
        k = qkv_ref[:, part + h * HD : part + (h + 1) * HD]
        v = qkv_ref[:, 2 * part + h * HD : 2 * part + (h + 1) * HD]
        do = do_ref[:, h * HD : (h + 1) * HD]
        soft = jnp.exp(dot(k, q, 1, 1) - lse_ref[h : h + 1])
        soft = jnp.where(col_ref[...] == row_ref[...], soft, 0.0)
        soft_grad = dot(v, do, 1, 1)
        row_dot = jnp.sum(soft * soft_grad, axis=0, keepdims=True)
        score_grad = (soft * (soft_grad - row_dot)).astype(BF)
        dq = dot(score_grad, k, 0, 0) * HD**-0.5
        out_ref[:, h * HD : (h + 1) * HD] = dq.astype(BF)
        dk = dot(score_grad, q, 1, 0)
        out_ref[:, part + h * HD : part + (h + 1) * HD] = dk.astype(BF)
        dv = dot(soft.astype(BF), do, 1, 0)
        out_ref[:, 2 * part + h * HD : 2 * part + (h + 1) * HD] = dv.astype(BF)


def whole(kernel, outs, args, flops):
    space = pl.BlockSpec(memory_space=pltpu.VMEM)
    return pl.pallas_call(
        kernel,
        out_shape=outs,
        in_specs=[space] * len(args),
        out_specs=jax.tree.map(lambda _: space, outs),
        compiler_params=pltpu.CompilerParams(vmem_limit_bytes=40 * 2**20),
        cost_estimate=pl.CostEstimate(flops=flops, bytes_accessed=2**21, transcendentals=0),
    )(*args)


def attend(qkv, code_row):
    tokens = qkv.shape[0]
    heads = HEADS // NF
    outs = (
        jax.ShapeDtypeStruct((tokens, heads * HD), BF),
        jax.ShapeDtypeStruct((heads, tokens), F32),
    )
    args = (qkv, code_row[:, None], code_row[None])
    return whole(functools.partial(attend_kernel, heads=heads), outs, args, 5 * 10**9)


def attend_back(qkv, out_grad, lse, code_row):
    heads = HEADS // NF
    outs = jax.ShapeDtypeStruct(qkv.shape, BF)
    args = (qkv, out_grad, lse, code_row[:, None], code_row[None])
    return whole(functools.partial(attend_back_kernel, heads=heads), outs, args, 7 * 10**9)


def expert_kernel(*refs, blocks):
    own_ref, x_refs, dz_refs = refs[0], refs[1 : 1 + blocks], refs[1 + blocks : 1 + 2 * blocks]
    in_ref, out_ref, router_ref = refs[1 + 2 * blocks : 4 + 2 * blocks]
    dx_send, dx_keep, y_send, y_keep, din_ref, dout_ref, drouter_ref = refs[4 + 2 * blocks :][:7]
    din, dout = refs[-2:]
    w_in, w_out, router = in_ref[...], out_ref[...], router_ref[...]
    drouter = None
    for i in range(blocks):
        x, dz = x_refs[i][...], dz_refs[i][...]
        ue = mm(x, w_in)
        cdf = 0.5 * (1.0 + lax.erf(ue * (0.5**0.5)))
        slope = cdf + ue * jnp.exp(-0.5 * ue * ue) * 0.3989422804014327
        ge = (ue * cdf).astype(BF)
        y = mm(ge, w_out)
        logits = mm(x, router)
        lane = lax.broadcasted_iota(jnp.int32, logits.shape, 1)
        shifted = jnp.exp(logits - jnp.max(logits, axis=1, keepdims=True))
        probs = shifted / jnp.sum(shifted, axis=1, keepdims=True)
        mine = (lane == own_ref[0]).astype(F32)
        prob = jnp.sum(probs * mine, axis=1, keepdims=True)
        gate = prob.astype(BF).astype(F32)
        dz_wide = dz.astype(F32)
        dyx = (gate * dz_wide).astype(BF)
        due = (dot(dyx, w_out, 1, 1) * slope).astype(BF)
        dgate = jnp.sum(dz_wide * y, axis=1, keepdims=True)
        dlogits = (dgate * prob * (mine - probs)).astype(BF)
        dx = dot(due, w_in, 1, 1) + dot(dlogits, router, 1, 1)
        y = gate * y
        if i % 2 == 0:
            dx_keep[i // 2], y_keep[i // 2] = dx, y
        else:
            dx_send[i // 2], y_send[i // 2] = dx.astype(BF), y.astype(BF)
        if i == 0:
            din[...], dout[...], drouter = dot(x, due, 0, 0), dot(ge, dyx, 0, 0), dot(x, dlogits, 0, 0)
        else:
            din[...] += dot(x, due, 0, 0)
            dout[...] += dot(ge, dyx, 0, 0)
            drouter += dot(x, dlogits, 0, 0)
    din_ref[...], dout_ref[...], drouter_ref[...] = din[...].astype(BF), dout[...].astype(BF), drouter


def expert_compute(own, x_blocks, dz_blocks, w_in, w_out, router):
    tall, width = x_blocks[0].shape
    hidden = w_in.shape[1]
    count = len(x_blocks)
    send = jax.ShapeDtypeStruct((count // 2, tall, width), BF)
    keep = jax.ShapeDtypeStruct((count // 2, tall, width), F32)
    outs = (
        send, keep, send, keep, jax.ShapeDtypeStruct(w_in.shape, BF), jax.ShapeDtypeStruct(w_out.shape, BF),
        jax.ShapeDtypeStruct(router.shape, F32),
    )
    space = pl.BlockSpec(memory_space=pltpu.VMEM)
    return pl.pallas_call(
        functools.partial(expert_kernel, blocks=count),
        out_shape=outs,
        in_specs=[pl.BlockSpec(memory_space=pltpu.SMEM)] + [space] * (2 * count + 3),
        out_specs=(space,) * len(outs),
        scratch_shapes=[pltpu.VMEM(w_in.shape, F32), pltpu.VMEM(w_out.shape, F32)],
        compiler_params=pltpu.CompilerParams(vmem_limit_bytes=56 * 2**20),
        cost_estimate=pl.CostEstimate(
            flops=16 * count * tall * width * hidden, bytes_accessed=2**24, transcendentals=0
        ),
    )(own.astype(jnp.int32)[None], *x_blocks, *dz_blocks, w_in, w_out, router)


def make_shards(n_dp):
    n_all = n_dp * NF

    def shards(
        patches, segment_ids, live, expert_ids, ranks, norm_gains, norm_biases, attn_qkv, attn_out,
        mlp_in, mlp_out, router, exp_in, exp_out, cotangent,
    ):
        width = patches.shape[-1]
        tokens = patches.shape[0] * patches.shape[1]
        experts = exp_in.shape[0]
        clones = n_dp // experts
        part = width // NF
        rows = attn_qkv.shape[1]
        hid = mlp_out.shape[0]
        own_f = lax.axis_index("fsdp")
        own_dp = lax.axis_index("dp")
        groups = ring = None
        if clones > 1:
            groups = [[g * experts + e for e in range(experts)] for g in range(clones)]
            ring = [[g * experts + e for g in range(clones)] for e in range(experts)]
        capacity = (210 * tokens + 100 * experts - 1) // (100 * experts)
        slots = (capacity + 7) // 8 * 8

        code = (segment_ids * 2 + live).reshape(tokens)
        code_all = gather_row(code)
        live_all = (code_all % 2).astype(F32)
        rows_all = gather_row(patches.reshape(tokens, width))

        def qkv_block(layer):
            weight = attn_qkv[layer].reshape(rows, 3, NF, part)
            return jnp.transpose(weight, (2, 0, 1, 3)).reshape(NF, rows, 3 * part)

        small = jnp.concatenate(
            [norm_gains.T, norm_biases.T, router, jnp.zeros((rows, 128 - 8 - experts), BF)], axis=1
        )
        small = jnp.broadcast_to(small[None], (NF, rows, 128))
        def to_everyone(blocks):
            full = jnp.broadcast_to(blocks[None], (n_dp,) + blocks.shape)
            return exchange(full.reshape((n_all, rows, -1)), ALL).reshape(width, -1)

        first = to_everyone(jnp.concatenate([small, qkv_block(0)], axis=2))
        small_all, w_qkv0 = first[:, :128], first[:, 128:]
        norms = small_all[:, :8].T.astype(F32)
        gains, biases = norms[:4], norms[4:]
        w_router = small_all[:, 8 : 8 + experts]

        mlp_block = jnp.transpose(mlp_in.reshape(rows, n_dp, NF, hid), (2, 0, 1, 3))
        mlp_block = deal(mlp_block.reshape(NF, rows, n_dp * hid)).reshape(NF * rows, width)
        mlp_all = lax.all_gather(jnp.concatenate([mlp_block, mlp_out], axis=0), "dp")
        w_mlp_in = mlp_all[:, : NF * rows].reshape(width, n_dp * hid)
        w_mlp_out = mlp_all[:, NF * rows :].reshape(n_dp * hid, width)

        to_heads = [(j, j % n_dp * NF + j // n_dp) for j in range(n_all)]
        to_owner = [(b, a) for a, b in to_heads]
        held = lax.ppermute(jnp.concatenate([attn_out[0], attn_out[1]], axis=0), ALL, to_heads)
        held = exchange(jnp.broadcast_to(after(held, first)[None], (n_dp,) + held.shape), "dp")
        w_out0, w_out1 = held[:, :rows].reshape(part, width), held[:, rows:].reshape(part, width)

        in_block = jnp.transpose(exp_in.reshape(experts, rows, n_dp, NF, hid), (0, 3, 1, 2, 4))
        in_block = in_block.reshape(experts * NF, rows, n_dp * hid)
        if clones == 1:
            held = jnp.broadcast_to(qkv_block(1)[None], (n_dp, NF, rows, 3 * part)).reshape(n_all, rows, -1)
            held = exchange(after(jnp.concatenate([in_block, held], axis=2), w_out0), ALL).reshape(width, -1)
            w_exp_in, w_qkv1 = held[:, : n_dp * hid], held[:, n_dp * hid :]
        else:
            held = in_block.reshape(experts, NF, rows, n_dp * hid)
            held = exchange(jnp.swapaxes(held, 0, 1), "fsdp")
            held = exchange(jnp.swapaxes(held, 0, 1), "dp", groups)
            w_exp_in = lax.all_gather(held, "dp", axis_index_groups=ring).reshape(width, n_dp * hid)
            w_qkv1 = to_everyone(qkv_block(1))
        choice = expert_ids.reshape(tokens, 2)
        rank = ranks.reshape(tokens, 2)
        place = jnp.where(rank < capacity, choice * slots + rank, -1)
        slot_index = jnp.arange(experts * slots, dtype=jnp.int32)[:, None]
        pick = (place[:, 0][None] == slot_index) | (place[:, 1][None] == slot_index)
        pick = pick.astype(BF)

        def to_experts(block):
            held = mm(pick, block).astype(BF).reshape(experts, slots, width)
            return exchange(held, "dp", groups).reshape(experts * slots, width)

        top_grad = cotangent.reshape(tokens, width)
        dz = to_experts(after(top_grad, w_exp_in))

        h0 = patches.reshape(tokens, width).astype(F32)
        xhat0_all, _ = scale_rows(rows_all.astype(F32))
        a0 = (xhat0_all * gains[0] + biases[0]).astype(BF)
        qkv0 = mm(a0, w_qkv0).astype(BF)
        o0, lse0 = attend(qkv0, code_all)
        h1 = h0 + scatter_row(mm(o0, w_out0))

        xhat1, inv1 = scale_rows(h1)
        c0 = gather_row((xhat1 * gains[1] + biases[1]).astype(BF))
        u0 = mm(c0, w_mlp_in)
        g0 = after(gelu(u0).astype(BF), w_qkv1)
        h2 = h1 + scatter_row(mm(g0, w_mlp_out))

        xhat2, inv2 = scale_rows(h2)
        a1 = after(gather_row((xhat2 * gains[2] + biases[2]).astype(BF)), w_exp_in)
        qkv1 = mm(a1, w_qkv1).astype(BF)
        o1, lse1 = attend(qkv1, code_all)
        h3 = h2 + scatter_row(mm(o1, w_out1))

        xhat3, inv3 = scale_rows(h3)
        c1 = after((xhat3 * gains[3] + biases[3]).astype(BF), dz)
        dz = gather_blocks(after(dz, c1))
        x = to_experts(c1)
        w_exp_out = exchange(after(exp_out, x, dz[2]), "dp", groups)
        if clones > 1:
            w_exp_out = lax.all_gather(w_exp_out, "dp", axis_index_groups=ring)
        w_exp_out = w_exp_out.reshape(n_dp * hid, width)
        x = gather_blocks(x)
        dx_send, dx_keep, y_send, y_keep, exp_in_part, exp_out_part, router_part = expert_compute(
            own_dp % experts, x, dz, w_exp_in, w_exp_out, w_router
        )
        dx = scatter_blocks(dx_send, dx_keep).astype(BF)
        y = scatter_blocks(after(y_send, dx), y_keep).astype(BF)
        dx = exchange(dx.reshape(experts, slots, width), "dp", groups)

        if clones == 1:
            back = exp_out_part.reshape(experts, hid, width)
            in_got = exchange(after(exp_in_part.reshape(n_all, rows, n_dp * hid), dx), ALL)
            got = exchange(after(back, in_got), "dp")
            exp_out_grads = got.astype(F32)
            in_got = in_got.reshape(experts, NF, rows, n_dp, hid)
            exp_in_grads = jnp.transpose(in_got, (0, 2, 3, 1, 4))
        else:
            back = lax.psum_scatter(
                exp_out_part.reshape(clones, experts, hid, width), "dp", axis_index_groups=ring
            )
            exp_out_grads = exchange(back, "dp", groups).astype(F32)
            got = exp_out_grads
            held = lax.psum_scatter(
                exp_in_part.reshape(clones, experts, NF, rows, n_dp * hid), "dp", axis_index_groups=ring
            )
            held = exchange(held, "dp", groups)
            held = exchange(jnp.swapaxes(held, 0, 1), "fsdp")
            in_got = held.reshape(NF, experts, rows, n_dp, hid)
            exp_in_grads = jnp.transpose(in_got, (1, 2, 3, 0, 4))
        exp_in_grads = exp_in_grads.reshape(experts, rows, n_dp * NF * hid).astype(F32)
        dc1 = mm_tn(pick, after(dx, exp_in_part).reshape(experts * slots, width))

        def rows_to_owners(grad):
            cols = grad.shape[1]
            got = exchange(grad.astype(BF).reshape(n_all, rows, cols), ALL)
            return got.reshape(n_dp, NF, rows, cols).astype(F32)

        def qkv_layout(total):
            parts = total.reshape(NF, rows, 3, part)
            return jnp.transpose(parts, (1, 2, 0, 3)).reshape(rows, 3 * width)

        def sums(out_grad, xhat):
            return jnp.sum(out_grad * xhat, axis=0), jnp.sum(out_grad, axis=0)

        gain3, bias3 = sums(dc1, xhat3)
        grad = top_grad.astype(F32) + norm_back(dc1, xhat3, inv3, gains[3])

        dy1 = gather_row(grad.astype(BF))
        do1 = (mm_nt(dy1, w_out1) * live_all[:, None]).astype(BF)
        dqkv1 = attend_back(qkv1, do1, lse1, code_all)
        da1 = scatter_row(mm_nt(after(dqkv1, in_got), w_qkv1))
        out_part1 = mm_tn(o1, dy1).astype(BF)
        qkv_part1 = mm_tn(a1, dqkv1).astype(BF)
        gain2, bias2 = sums(da1, xhat2)
        grad = grad + norm_back(da1, xhat2, inv2, gains[2])

        dm = gather_row(grad.astype(BF))
        du0 = (mm_nt(after(dm, qkv_part1, got), w_mlp_out) * gelu_slope(u0)).astype(BF)
        dc0 = scatter_row(mm_nt(du0, w_mlp_in))
        mlp_in_part = mm_tn(c0, du0).astype(BF)
        dense_part = jnp.concatenate(
            [
                mlp_in_part.reshape(n_dp, NF * rows, width),
                mm_tn(g0, dm).astype(BF).reshape(n_dp, NF * rows, width),
                qkv_part1.reshape(n_dp, NF * rows, 3 * part),
                out_part1.reshape(n_dp, NF * rows, part),
            ],
            axis=2,
        )
        dense_sum = lax.psum_scatter(dense_part, "dp")
        gain1, bias1 = sums(dc0, xhat1)
        grad = grad + norm_back(dc0, xhat1, inv1, gains[1])

        dy0 = gather_row(grad.astype(BF))
        do0 = (mm_nt(after(dy0, dense_part), w_out0) * live_all[:, None]).astype(BF)
        out_part0 = mm_tn(o0, dy0).astype(BF).reshape(n_dp, rows, width)
        y = y.reshape(experts, slots, width)
        if clones == 1:
            held = exchange(after(jnp.concatenate([y, out_part0], axis=1), got), "dp")
            y, out_got0 = held[:, :slots], held[:, slots:]
        else:
            y, out_got0 = exchange(y, "dp", groups), exchange(out_part0, "dp")
        h4 = h3 + mm_tn(pick, y.reshape(experts * slots, width))
        activations = h4.astype(BF)
        dqkv0 = attend_back(qkv0, do0, lse0, code_all)
        da0 = mm_nt(dqkv0, w_qkv0)
        qkv_part0 = mm_tn(a0, dqkv0)
        gain0, bias0 = sums(da0, xhat0_all)
        columns = jnp.stack([gain0, gain1, gain2, gain3, bias0, bias1, bias2, bias3], axis=1)
        columns = jnp.concatenate(
            [columns, router_part, jnp.zeros((width, 128 - 8 - experts), F32), qkv_part0], axis=1
        )
        tail = rows_to_owners(after(columns, y))
        total = jnp.sum(tail, axis=0)
        small_grads = jnp.sum(total[:, :, :128], axis=0)
        qkv_grad0 = qkv_layout(total[:, :, 128:])
        held = jnp.concatenate([dense_sum[:, :width], dense_sum[:, 2 * width : 2 * width + 3 * part]], axis=1)
        held = exchange(held.reshape(NF, rows, -1), "fsdp").astype(F32)
        mlp_in_grads = held[..., :width].reshape(NF, rows, n_dp, hid)
        mlp_in_grads = jnp.transpose(mlp_in_grads, (1, 2, 0, 3)).reshape(rows, n_dp * NF * hid)
        qkv_grad1 = qkv_layout(held[..., width:])
        mlp_out_grads = dense_sum[:, width : 2 * width].astype(F32)
        out_sum1 = dense_sum[:, 2 * width + 3 * part :].reshape(rows, width).astype(F32)
        out_sums = jnp.stack([jnp.sum(out_got0.astype(F32), axis=0), out_sum1])
        proj_grads = lax.ppermute(out_sums, ALL, to_owner)
        da0 = scatter_row(da0)
        xhat0, inv0 = scale_rows(h0)
        grad = grad + norm_back(da0, xhat0, inv0, gains[0])

        norm_grads = small_grads[:, :8].T
        return (
            activations.reshape(patches.shape),
            grad.reshape(patches.shape),
            norm_grads[:4],
            norm_grads[4:7],
            norm_grads[7],
            jnp.stack([qkv_grad0, qkv_grad1]),
            proj_grads,
            mlp_in_grads,
            mlp_out_grads,
            small_grads[:, 8 : 8 + experts],
            exp_in_grads,
            exp_out_grads,
        )

    return shards


def solution(mesh):
    by_row = P("dp", "fsdp", None)
    second = P(None, ("dp", "fsdp"), None)
    first = P(("dp", "fsdp"), None)
    pair = P("dp", "fsdp")
    norm = P(None, ("dp", "fsdp"))
    return jax.shard_map(
        make_shards(mesh.shape["dp"]),
        mesh=mesh,
        in_specs=(
            by_row, pair, pair, by_row, by_row, norm, norm, second, second, first, first, first,
            second, second, by_row,
        ),
        out_specs=(
            by_row, by_row, norm, norm, P(("dp", "fsdp")), second, second, first, first, first,
            second, second,
        ),
        check_vma=False,
    )
```

```python
import functools

import jax
import jax.numpy as jnp
from jax import lax
from jax.experimental import pallas as pl
from jax.experimental.pallas import tpu as pltpu
from jax.sharding import PartitionSpec as P

HEADS = 12
HD = 64
EPSILON = 1e-06
NF = 4
ALL = ("dp", "fsdp")
BF = jnp.bfloat16
F32 = jnp.float32


def mm(left, right):
    return jnp.dot(left, right, preferred_element_type=F32)


def mm_tn(left, right):
    return lax.dot_general(left, right, (((0,), (0,)), ((), ())), preferred_element_type=F32)


def mm_nt(left, right):
    return lax.dot_general(left, right, (((1,), (1,)), ((), ())), preferred_element_type=F32)


def gelu(values):
    return 0.5 * values * (1.0 + lax.erf(values * (0.5**0.5)))


def gelu_slope(values):
    cdf = 0.5 * (1.0 + lax.erf(values * (0.5**0.5)))
    return cdf + values * jnp.exp(-0.5 * values * values) * 0.3989422804014327


def scale_rows(rows):
    centre = jnp.mean(rows, axis=-1, keepdims=True)
    centred = rows - centre
    inv_scale = lax.rsqrt(jnp.mean(centred * centred, axis=-1, keepdims=True) + EPSILON)
    return centred * inv_scale, inv_scale


def norm_back(out_grad, scaled, inv_scale, gain):
    weighted = out_grad * gain
    return inv_scale * (
        weighted
        - jnp.mean(weighted, axis=-1, keepdims=True)
        - scaled * jnp.mean(weighted * scaled, axis=-1, keepdims=True)
    )


def swap(value, bits):
    return lax.ppermute(value, "fsdp", [(i, i ^ bits) for i in range(NF)])


def gather_blocks(block):
    across = swap(block, 2)
    beside = swap(block, 1)
    corner = swap(across, 1)
    return [block, beside, across, corner]


def gather_row(block):
    return jnp.concatenate(gather_blocks(block), axis=0)


def scatter_blocks(send, keep):
    got = swap(send, 1).astype(F32)
    far = swap((keep[1] + got[1]).astype(BF), 2).astype(F32)
    return keep[0] + got[0] + far


def scatter_row(partial):
    blocks = partial.reshape((NF, -1) + partial.shape[1:])
    return scatter_blocks(jnp.stack([blocks[1], blocks[3]]).astype(BF), (blocks[0], blocks[2]))


def after(value, *others):
    return lax.optimization_barrier((value,) + others)[0]


def deal(blocks):
    own = lax.axis_index("fsdp")
    got = []
    for k in range(NF):
        block = lax.dynamic_index_in_dim(blocks, own ^ k, 0, keepdims=False)
        got.append(block if k == 0 else swap(block, k))
    odd, far = own % 2 == 1, own >= 2
    got = [jnp.where(odd, got[k ^ 1], got[k]) for k in range(NF)]
    return jnp.stack([jnp.where(far, got[k ^ 2], got[k]) for k in range(NF)])


def exchange(value, axes, groups=None):
    return lax.all_to_all(value, axes, 0, 0, axis_index_groups=groups, tiled=True)


def dot(left, right, left_dim, right_dim):
    dims = (((left_dim,), (right_dim,)), ((), ()))
    return lax.dot_general(left, right, dims, preferred_element_type=F32)


def put_partial(partial, send_ref, keep_ref):
    tall = partial.shape[0] // NF
    for k in range(NF):
        block = partial[k * tall : (k + 1) * tall]
        if k % 2 == 0:
            keep_ref[k // 2] = block
        else:
            send_ref[k // 2] = block.astype(BF)


def partial_shapes(tokens, width):
    tall = tokens // NF
    return (
        jax.ShapeDtypeStruct((NF // 2, tall, width), BF),
        jax.ShapeDtypeStruct((NF // 2, tall, width), F32),
    )


def attend_kernel(*refs, count, heads):
    a_refs, (w_ref, wo_ref, col_ref, row_ref) = refs[:count], refs[count : count + 4]
    qkv_ref, out_ref, lse_ref, send_ref, keep_ref = refs[count + 4 :]
    tall = a_refs[0].shape[0]
    for k in range(count):
        qkv_ref[k * tall : (k + 1) * tall] = mm(a_refs[k][...], w_ref[...]).astype(BF)
    part = heads * HD
    live = (col_ref[...] % 2).astype(F32)
    for h in range(heads):
        q = qkv_ref[:, h * HD : (h + 1) * HD] * BF(HD**-0.5)
        k = qkv_ref[:, part + h * HD : part + (h + 1) * HD]
        v = qkv_ref[:, 2 * part + h * HD : 2 * part + (h + 1) * HD]
        scores = jnp.where(col_ref[...] == row_ref[...], dot(k, q, 1, 1), -1e30)
        top = jnp.max(scores, axis=0, keepdims=True)
        shifted = jnp.exp(scores - top)
        total = jnp.sum(shifted, axis=0, keepdims=True)
        soft = (shifted * (1.0 / total)).astype(BF)
        out_ref[:, h * HD : (h + 1) * HD] = (dot(soft, v, 0, 0) * live).astype(BF)
        lse_ref[h : h + 1] = top + jnp.log(total)
    put_partial(mm(out_ref[...], wo_ref[...]), send_ref, keep_ref)


def attend_back_kernel(*refs, count, heads):
    dy_refs, (w_ref, wo_ref, qkv_ref, lse_ref, col_ref, row_ref) = refs[:count], refs[count : count + 6]
    dqkv_ref, send_ref, keep_ref, do_ref = refs[count + 6 :]
    tall = dy_refs[0].shape[0]
    part = heads * HD
    for k in range(count):
        live = (col_ref[k * tall : (k + 1) * tall] % 2).astype(F32)
        do_ref[k * tall : (k + 1) * tall] = (dot(dy_refs[k][...], wo_ref[...], 1, 1) * live).astype(BF)
    for h in range(heads):
        q = qkv_ref[:, h * HD : (h + 1) * HD] * BF(HD**-0.5)
        k = qkv_ref[:, part + h * HD : part + (h + 1) * HD]
        v = qkv_ref[:, 2 * part + h * HD : 2 * part + (h + 1) * HD]
        do = do_ref[:, h * HD : (h + 1) * HD]
        soft = jnp.exp(dot(k, q, 1, 1) - lse_ref[h : h + 1])
        soft = jnp.where(col_ref[...] == row_ref[...], soft, 0.0)
        soft_grad = dot(v, do, 1, 1)
        row_dot = jnp.sum(soft * soft_grad, axis=0, keepdims=True)
        score_grad = (soft * (soft_grad - row_dot)).astype(BF)
        dq = dot(score_grad, k, 0, 0) * HD**-0.5
        dqkv_ref[:, h * HD : (h + 1) * HD] = dq.astype(BF)
        dk = dot(score_grad, q, 1, 0)
        dqkv_ref[:, part + h * HD : part + (h + 1) * HD] = dk.astype(BF)
        dv = dot(soft.astype(BF), do, 1, 0)
        dqkv_ref[:, 2 * part + h * HD : 2 * part + (h + 1) * HD] = dv.astype(BF)
    put_partial(dot(dqkv_ref[...], w_ref[...], 1, 1), send_ref, keep_ref)


def mlp_kernel(*refs):
    c_refs, (in_ref, out_ref, u_ref, g_ref, send_ref, keep_ref) = refs[:NF], refs[NF:]
    for k in range(NF):
        u = mm(c_refs[k][...], in_ref[...])
        u_ref[k] = u
        g = gelu(u).astype(BF)
        g_ref[k] = g
        partial = mm(g, out_ref[...])
        if k % 2 == 0:
            keep_ref[k // 2] = partial
        else:
            send_ref[k // 2] = partial.astype(BF)


def mlp_back_kernel(*refs):
    dm_refs, (u_ref, in_ref, out_ref, du_ref, send_ref, keep_ref) = refs[:NF], refs[NF:]
    for k in range(NF):
        du = (dot(dm_refs[k][...], out_ref[...], 1, 1) * gelu_slope(u_ref[k])).astype(BF)
        du_ref[k] = du
        partial = dot(du, in_ref[...], 1, 1)
        if k % 2 == 0:
            keep_ref[k // 2] = partial
        else:
            send_ref[k // 2] = partial.astype(BF)


def mlp_weights_kernel(*refs):
    c_refs, dm_refs = refs[:NF], refs[NF : 2 * NF]
    du_ref, g_ref, rest_ref, out_ref, sum_ref = refs[2 * NF :]
    groups, rows, width = rest_ref.shape
    for step in range(2):
        for k in range(NF):
            if step == 0:
                term = dot(c_refs[k][...], du_ref[k], 0, 0)
            else:
                term = dot(g_ref[k], dm_refs[k][...], 0, 0)
            if k == 0:
                sum_ref[...] = term
            else:
                sum_ref[...] += term
        for d in range(groups):
            out_ref[d, :, step * width : (step + 1) * width] = sum_ref[d * rows : (d + 1) * rows].astype(BF)
    for d in range(groups):
        out_ref[d, :, 2 * width :] = rest_ref[d]


def whole(kernel, outs, args, flops, scratch=()):
    space = pl.BlockSpec(memory_space=pltpu.VMEM)
    return pl.pallas_call(
        kernel,
        out_shape=outs,
        in_specs=[space] * len(args),
        out_specs=jax.tree.map(lambda _: space, outs),
        scratch_shapes=scratch,
        compiler_params=pltpu.CompilerParams(vmem_limit_bytes=48 * 2**20),
        cost_estimate=pl.CostEstimate(flops=flops, bytes_accessed=2**21, transcendentals=0),
    )(*args)


def attend(a_blocks, w_qkv, w_out, code_row):
    tokens, width = code_row.shape[0], w_qkv.shape[0]
    heads = HEADS // NF
    part = heads * HD
    outs = (
        jax.ShapeDtypeStruct((tokens, 3 * part), BF),
        jax.ShapeDtypeStruct((tokens, part), BF),
        jax.ShapeDtypeStruct((heads, tokens), F32),
    ) + partial_shapes(tokens, width)
    kernel = functools.partial(attend_kernel, count=len(a_blocks), heads=heads)
    args = (*a_blocks, w_qkv, w_out, code_row[:, None], code_row[None])
    return whole(kernel, outs, args, 8 * 10**9)


def attend_back(dy_blocks, w_qkv, w_out, qkv, lse, code_row):
    tokens, width = code_row.shape[0], w_qkv.shape[0]
    heads = HEADS // NF
    outs = (jax.ShapeDtypeStruct(qkv.shape, BF),) + partial_shapes(tokens, width)
    kernel = functools.partial(attend_back_kernel, count=len(dy_blocks), heads=heads)
    args = (*dy_blocks, w_qkv, w_out, qkv, lse, code_row[:, None], code_row[None])
    return whole(kernel, outs, args, 11 * 10**9, (pltpu.VMEM((tokens, heads * HD), BF),))


def mlp(c_blocks, w_in, w_out):
    tall, width = c_blocks[0].shape
    outs = (
        jax.ShapeDtypeStruct((NF, tall, w_in.shape[1]), F32),
        jax.ShapeDtypeStruct((NF, tall, w_in.shape[1]), BF),
    ) + partial_shapes(NF * tall, width)
    return whole(mlp_kernel, outs, (*c_blocks, w_in, w_out), 5 * 10**9)


def mlp_back(dm_blocks, u, w_in, w_out):
    tall, width = dm_blocks[0].shape
    outs = (jax.ShapeDtypeStruct(u.shape, BF),) + partial_shapes(NF * tall, width)
    return whole(mlp_back_kernel, outs, (*dm_blocks, u, w_in, w_out), 6 * 10**9)


def mlp_weights(c_blocks, dm_blocks, du, g, rest):
    groups, rows, width = rest.shape
    if rows % 16 == 0:
        outs = jax.ShapeDtypeStruct((groups, rows, 3 * width), BF)
        args = (*c_blocks, *dm_blocks, du, g, rest)
        return whole(mlp_weights_kernel, outs, args, 5 * 10**9, (pltpu.VMEM((width, width), F32),))
    parts = [mm_tn(jnp.concatenate(c_blocks, axis=0), du.reshape(-1, width))]
    parts.append(mm_tn(g.reshape(-1, width), jnp.concatenate(dm_blocks, axis=0)))
    parts = [value.astype(BF).reshape(groups, rows, width) for value in parts]
    return jnp.concatenate(parts + [rest], axis=2)


def expert_kernel(*refs, blocks):
    own_ref, x_refs, dz_refs = refs[0], refs[1 : 1 + blocks], refs[1 + blocks : 1 + 2 * blocks]
    in_ref, out_ref, router_ref = refs[1 + 2 * blocks : 4 + 2 * blocks]
    dx_send, dx_keep, y_send, y_keep, din_ref, dout_ref, drouter_ref = refs[4 + 2 * blocks :][:7]
    din, dout = refs[-2:]
    w_in, w_out, router = in_ref[...], out_ref[...], router_ref[...]
    drouter = None
    for i in range(blocks):
        x, dz = x_refs[i][...], dz_refs[i][...]
        ue = mm(x, w_in)
        cdf = 0.5 * (1.0 + lax.erf(ue * (0.5**0.5)))
        slope = cdf + ue * jnp.exp(-0.5 * ue * ue) * 0.3989422804014327
        ge = (ue * cdf).astype(BF)
        y = mm(ge, w_out)
        logits = mm(x, router)
        lane = lax.broadcasted_iota(jnp.int32, logits.shape, 1)
        shifted = jnp.exp(logits - jnp.max(logits, axis=1, keepdims=True))
        probs = shifted / jnp.sum(shifted, axis=1, keepdims=True)
        mine = (lane == own_ref[0]).astype(F32)
        prob = jnp.sum(probs * mine, axis=1, keepdims=True)
        gate = prob.astype(BF).astype(F32)
        dz_wide = dz.astype(F32)
        dyx = (gate * dz_wide).astype(BF)
        due = (dot(dyx, w_out, 1, 1) * slope).astype(BF)
        dgate = jnp.sum(dz_wide * y, axis=1, keepdims=True)
        dlogits = (dgate * prob * (mine - probs)).astype(BF)
        dx = dot(due, w_in, 1, 1) + dot(dlogits, router, 1, 1)
        y = gate * y
        if i % 2 == 0:
            dx_keep[i // 2], y_keep[i // 2] = dx, y
        else:
            dx_send[i // 2], y_send[i // 2] = dx.astype(BF), y.astype(BF)
        if i == 0:
            din[...], dout[...], drouter = dot(x, due, 0, 0), dot(ge, dyx, 0, 0), dot(x, dlogits, 0, 0)
        else:
            din[...] += dot(x, due, 0, 0)
            dout[...] += dot(ge, dyx, 0, 0)
            drouter += dot(x, dlogits, 0, 0)
    din_ref[...], dout_ref[...], drouter_ref[...] = din[...].astype(BF), dout[...].astype(BF), drouter


def expert_compute(own, x_blocks, dz_blocks, w_in, w_out, router):
    tall, width = x_blocks[0].shape
    hidden = w_in.shape[1]
    count = len(x_blocks)
    send = jax.ShapeDtypeStruct((count // 2, tall, width), BF)
    keep = jax.ShapeDtypeStruct((count // 2, tall, width), F32)
    outs = (
        send, keep, send, keep, jax.ShapeDtypeStruct(w_in.shape, BF), jax.ShapeDtypeStruct(w_out.shape, BF),
        jax.ShapeDtypeStruct(router.shape, F32),
    )
    space = pl.BlockSpec(memory_space=pltpu.VMEM)
    return pl.pallas_call(
        functools.partial(expert_kernel, blocks=count),
        out_shape=outs,
        in_specs=[pl.BlockSpec(memory_space=pltpu.SMEM)] + [space] * (2 * count + 3),
        out_specs=(space,) * len(outs),
        scratch_shapes=[pltpu.VMEM(w_in.shape, F32), pltpu.VMEM(w_out.shape, F32)],
        compiler_params=pltpu.CompilerParams(vmem_limit_bytes=56 * 2**20),
        cost_estimate=pl.CostEstimate(
            flops=16 * count * tall * width * hidden, bytes_accessed=2**24, transcendentals=0
        ),
    )(own.astype(jnp.int32)[None], *x_blocks, *dz_blocks, w_in, w_out, router)


def make_shards(n_dp):
    n_all = n_dp * NF

    def shards(
        patches, segment_ids, live, expert_ids, ranks, norm_gains, norm_biases, attn_qkv, attn_out,
        mlp_in, mlp_out, router, exp_in, exp_out, cotangent,
    ):
        width = patches.shape[-1]
        tokens = patches.shape[0] * patches.shape[1]
        experts = exp_in.shape[0]
        clones = n_dp // experts
        part = width // NF
        rows = attn_qkv.shape[1]
        hid = mlp_out.shape[0]
        own_f = lax.axis_index("fsdp")
        own_dp = lax.axis_index("dp")
        groups = ring = None
        if clones > 1:
            groups = [[g * experts + e for e in range(experts)] for g in range(clones)]
            ring = [[g * experts + e for g in range(clones)] for e in range(experts)]
        capacity = (210 * tokens + 100 * experts - 1) // (100 * experts)
        slots = (capacity + 7) // 8 * 8

        code = (segment_ids * 2 + live).reshape(tokens)
        code_all = gather_row(code)
        live_all = (code_all % 2).astype(F32)
        rows_all = gather_row(patches.reshape(tokens, width))

        def qkv_block(layer):
            weight = attn_qkv[layer].reshape(rows, 3, NF, part)
            return jnp.transpose(weight, (2, 0, 1, 3)).reshape(NF, rows, 3 * part)

        small = jnp.concatenate(
            [norm_gains.T, norm_biases.T, router, jnp.zeros((rows, 128 - 8 - experts), BF)], axis=1
        )
        small = jnp.broadcast_to(small[None], (NF, rows, 128))
        def to_everyone(blocks):
            full = jnp.broadcast_to(blocks[None], (n_dp,) + blocks.shape)
            return exchange(full.reshape((n_all, rows, -1)), ALL).reshape(width, -1)

        first = to_everyone(jnp.concatenate([small, qkv_block(0)], axis=2))
        small_all, w_qkv0 = first[:, :128], first[:, 128:]
        norms = small_all[:, :8].T.astype(F32)
        gains, biases = norms[:4], norms[4:]
        w_router = small_all[:, 8 : 8 + experts]

        mlp_block = jnp.transpose(mlp_in.reshape(rows, n_dp, NF, hid), (2, 0, 1, 3))
        mlp_block = deal(mlp_block.reshape(NF, rows, n_dp * hid)).reshape(NF * rows, width)
        mlp_all = lax.all_gather(jnp.concatenate([mlp_block, mlp_out], axis=0), "dp")
        w_mlp_in = mlp_all[:, : NF * rows].reshape(width, n_dp * hid)
        w_mlp_out = mlp_all[:, NF * rows :].reshape(n_dp * hid, width)

        to_heads = [(j, j % n_dp * NF + j // n_dp) for j in range(n_all)]
        to_owner = [(b, a) for a, b in to_heads]
        held = lax.ppermute(jnp.concatenate([attn_out[0], attn_out[1]], axis=0), ALL, to_heads)
        held = exchange(jnp.broadcast_to(after(held, first)[None], (n_dp,) + held.shape), "dp")
        w_out0, w_out1 = held[:, :rows].reshape(part, width), held[:, rows:].reshape(part, width)

        in_block = jnp.transpose(exp_in.reshape(experts, rows, n_dp, NF, hid), (0, 3, 1, 2, 4))
        in_block = in_block.reshape(experts * NF, rows, n_dp * hid)
        if clones == 1:
            held = jnp.broadcast_to(qkv_block(1)[None], (n_dp, NF, rows, 3 * part)).reshape(n_all, rows, -1)
            in_block = jnp.concatenate([in_block, held], axis=2)
            w_qkv0 = after(w_qkv0, in_block)
            held = exchange(after(in_block, w_out0), ALL).reshape(width, -1)
            w_exp_in, w_qkv1 = held[:, : n_dp * hid], held[:, n_dp * hid :]
        else:
            held = in_block.reshape(experts, NF, rows, n_dp * hid)
            held = exchange(jnp.swapaxes(held, 0, 1), "fsdp")
            held = exchange(jnp.swapaxes(held, 0, 1), "dp", groups)
            w_exp_in = lax.all_gather(held, "dp", axis_index_groups=ring).reshape(width, n_dp * hid)
            w_qkv1 = to_everyone(qkv_block(1))
        choice = expert_ids.reshape(tokens, 2)
        rank = ranks.reshape(tokens, 2)
        place = jnp.where(rank < capacity, choice * slots + rank, -1)
        slot_index = jnp.arange(experts * slots, dtype=jnp.int32)[:, None]
        pick = (place[:, 0][None] == slot_index) | (place[:, 1][None] == slot_index)
        pick = pick.astype(BF)

        def to_experts(block):
            held = mm(pick, block).astype(BF).reshape(experts, slots, width)
            return exchange(held, "dp", groups).reshape(experts * slots, width)

        top_grad = cotangent.reshape(tokens, width)
        if clones == 1:
            dz = mm(pick, top_grad).astype(BF).reshape(experts, slots, width)
            held = exchange(after(jnp.concatenate([dz, exp_out], axis=1), w_exp_in), "dp")
            dz, w_exp_out = held[:, :slots].reshape(experts * slots, width), held[:, slots:]
        else:
            dz = to_experts(top_grad)
            w_exp_out = exchange(exp_out, "dp", groups)
            w_exp_out = lax.all_gather(w_exp_out, "dp", axis_index_groups=ring)
        w_exp_out = w_exp_out.reshape(n_dp * hid, width)

        h0 = patches.reshape(tokens, width).astype(F32)
        xhat0_all, _ = scale_rows(rows_all.astype(F32))
        a0 = (xhat0_all * gains[0] + biases[0]).astype(BF)
        qkv0, o0, lse0, send, keep = attend([a0], w_qkv0, w_out0, code_all)
        h1 = h0 + scatter_blocks(send, keep)

        xhat1, inv1 = scale_rows(h1)
        c0 = gather_blocks((xhat1 * gains[1] + biases[1]).astype(BF))
        u0, g0, send, keep = mlp(c0, w_mlp_in, w_mlp_out)
        h2 = h1 + scatter_blocks(send, keep)

        xhat2, inv2 = scale_rows(h2)
        a1 = gather_blocks(after((xhat2 * gains[2] + biases[2]).astype(BF), w_exp_in))
        qkv1, o1, lse1, send, keep = attend(a1, w_qkv1, w_out1, code_all)
        h3 = h2 + scatter_blocks(send, keep)

        xhat3, inv3 = scale_rows(h3)
        c1 = after((xhat3 * gains[3] + biases[3]).astype(BF), dz, w_exp_out)
        dz = gather_blocks(after(dz, c1))
        x = to_experts(c1)
        x = gather_blocks(x)
        dx_send, dx_keep, y_send, y_keep, exp_in_part, exp_out_part, router_part = expert_compute(
            own_dp % experts, x, dz, w_exp_in, w_exp_out, w_router
        )
        dx = scatter_blocks(dx_send, dx_keep).astype(BF)
        y = scatter_blocks(after(y_send, dx), y_keep).astype(BF)
        y_summed = y
        dx = exchange(dx.reshape(experts, slots, width), "dp", groups)

        if clones == 1:
            back = exp_out_part.reshape(experts, hid, width)
            back = jnp.concatenate([y.reshape(experts, slots, width), back], axis=1)
            in_got = exchange(after(exp_in_part.reshape(n_all, rows, n_dp * hid), dx), ALL)
            got = exchange(after(back, in_got), "dp")
            y, exp_out_grads = got[:, :slots], got[:, slots:].astype(F32)
            in_got = in_got.reshape(experts, NF, rows, n_dp, hid)
            exp_in_grads = jnp.transpose(in_got, (0, 2, 3, 1, 4))
        else:
            back = lax.psum_scatter(
                exp_out_part.reshape(clones, experts, hid, width), "dp", axis_index_groups=ring
            )
            exp_out_grads = exchange(back, "dp", groups).astype(F32)
            got = exp_out_grads
            y = exchange(y.reshape(experts, slots, width), "dp", groups)
            held = lax.psum_scatter(
                exp_in_part.reshape(clones, experts, NF, rows, n_dp * hid), "dp", axis_index_groups=ring
            )
            held = exchange(held, "dp", groups)
            held = exchange(jnp.swapaxes(held, 0, 1), "fsdp")
            in_got = held.reshape(NF, experts, rows, n_dp, hid)
            exp_in_grads = jnp.transpose(in_got, (1, 2, 3, 0, 4))
        exp_in_grads = exp_in_grads.reshape(experts, rows, n_dp * NF * hid).astype(F32)
        dc1 = mm_tn(pick, after(dx, exp_in_part, y_summed).reshape(experts * slots, width))

        def rows_to_owners(grad):
            cols = grad.shape[1]
            got = exchange(grad.astype(BF).reshape(n_all, rows, cols), ALL)
            return got.reshape(n_dp, NF, rows, cols).astype(F32)

        def qkv_layout(total):
            parts = total.reshape(NF, rows, 3, part)
            return jnp.transpose(parts, (1, 2, 0, 3)).reshape(rows, 3 * width)

        def sums(out_grad, xhat):
            return jnp.sum(out_grad * xhat, axis=0), jnp.sum(out_grad, axis=0)

        gain3, bias3 = sums(dc1, xhat3)
        grad = top_grad.astype(F32) + norm_back(dc1, xhat3, inv3, gains[3])

        dy1 = gather_blocks(grad.astype(BF))
        dqkv1, send, keep = attend_back(dy1, w_qkv1, w_out1, qkv1, lse1, code_all)
        da1 = scatter_blocks(after(send, in_got), keep)
        attn_part = [
            mm_tn(jnp.concatenate(a1, axis=0), dqkv1).astype(BF).reshape(n_dp, NF * rows, 3 * part),
            mm_tn(o1, jnp.concatenate(dy1, axis=0)).astype(BF).reshape(n_dp, NF * rows, part),
        ]
        attn_part = jnp.concatenate(attn_part, axis=2)
        gain2, bias2 = sums(da1, xhat2)
        grad = grad + norm_back(da1, xhat2, inv2, gains[2])

        dm = gather_blocks(grad.astype(BF))
        du0, send, keep = mlp_back(dm, after(u0, attn_part), w_mlp_in, w_mlp_out)
        dc0 = scatter_blocks(send, keep)
        dense_part = mlp_weights(c0, dm, du0, after(g0, got), attn_part)
        dense_sum = lax.psum_scatter(dense_part, "dp")
        gain1, bias1 = sums(dc0, xhat1)
        grad = grad + norm_back(dc0, xhat1, inv1, gains[1])

        dy0 = gather_blocks(grad.astype(BF))
        dqkv0, send, keep = attend_back([after(dy0[0], dense_part), *dy0[1:]], w_qkv0, w_out0, qkv0, lse0, code_all)
        out_part0 = mm_tn(o0, jnp.concatenate(dy0, axis=0)).astype(BF).reshape(n_dp, rows, width)
        out_got0 = exchange(after(out_part0, got), "dp")
        qkv_part0 = mm_tn(a0, dqkv0)
        h4 = h3 + mm_tn(pick, y.reshape(experts * slots, width))
        activations = h4.astype(BF)
        da0 = scatter_blocks(send, keep)
        xhat0_blocks = xhat0_all.reshape(NF, tokens, width)
        gain0 = bias0 = 0.0
        for k in range(NF):
            block = keep[k // 2] if k % 2 == 0 else send[k // 2].astype(F32)
            block_gain, block_bias = sums(block, xhat0_blocks[k])
            gain0, bias0 = gain0 + block_gain, bias0 + block_bias
        columns = jnp.stack([gain0, gain1, gain2, gain3, bias0, bias1, bias2, bias3], axis=1)
        columns = jnp.concatenate(
            [columns, router_part, jnp.zeros((width, 128 - 8 - experts), F32), qkv_part0], axis=1
        )
        tail = rows_to_owners(after(columns, out_got0))
        total = jnp.sum(tail, axis=0)
        small_grads = jnp.sum(total[:, :, :128], axis=0)
        qkv_grad0 = qkv_layout(total[:, :, 128:])
        dense_sum = after(dense_sum, tail)
        held = jnp.concatenate([dense_sum[:, :width], dense_sum[:, 2 * width : 2 * width + 3 * part]], axis=1)
        held = exchange(held.reshape(NF, rows, -1), "fsdp").astype(F32)
        mlp_in_grads = held[..., :width].reshape(NF, rows, n_dp, hid)
        mlp_in_grads = jnp.transpose(mlp_in_grads, (1, 2, 0, 3)).reshape(rows, n_dp * NF * hid)
        qkv_grad1 = qkv_layout(held[..., width:])
        mlp_out_grads = dense_sum[:, width : 2 * width].astype(F32)
        out_sum1 = dense_sum[:, 2 * width + 3 * part :].reshape(rows, width).astype(F32)
        out_sums = jnp.stack([jnp.sum(out_got0.astype(F32), axis=0), out_sum1])
        proj_grads = lax.ppermute(out_sums, ALL, to_owner)
        xhat0, inv0 = scale_rows(h0)
        grad = grad + norm_back(da0, xhat0, inv0, gains[0])

        norm_grads = small_grads[:, :8].T
        return (
            activations.reshape(patches.shape),
            grad.reshape(patches.shape),
            norm_grads[:4],
            norm_grads[4:7],
            norm_grads[7],
            jnp.stack([qkv_grad0, qkv_grad1]),
            proj_grads,
            mlp_in_grads,
            mlp_out_grads,
            small_grads[:, 8 : 8 + experts],
            exp_in_grads,
            exp_out_grads,
        )

    return shards


def solution(mesh):
    by_row = P("dp", "fsdp", None)
    second = P(None, ("dp", "fsdp"), None)
    first = P(("dp", "fsdp"), None)
    pair = P("dp", "fsdp")
    norm = P(None, ("dp", "fsdp"))
    return jax.shard_map(
        make_shards(mesh.shape["dp"]),
        mesh=mesh,
        in_specs=(
            by_row, pair, pair, by_row, by_row, norm, norm, second, second, first, first, first,
            second, second, by_row,
        ),
        out_specs=(
            by_row, by_row, norm, norm, P(("dp", "fsdp")), second, second, first, first, first,
            second, second,
        ),
        check_vma=False,
    )
```

```python
import functools

import jax
import jax.numpy as jnp
from jax import lax
from jax.experimental import pallas as pl
from jax.experimental.pallas import tpu as pltpu
from jax.sharding import PartitionSpec as P

HEADS = 12
HD = 64
EPSILON = 1e-06
NF = 4
ALL = ("dp", "fsdp")
BF = jnp.bfloat16
F32 = jnp.float32


def mm(left, right):
    return jnp.dot(left, right, preferred_element_type=F32)


def mm_tn(left, right):
    return lax.dot_general(left, right, (((0,), (0,)), ((), ())), preferred_element_type=F32)


def mm_nt(left, right):
    return lax.dot_general(left, right, (((1,), (1,)), ((), ())), preferred_element_type=F32)


def gelu(values):
    return 0.5 * values * (1.0 + lax.erf(values * (0.5**0.5)))


def gelu_slope(values):
    cdf = 0.5 * (1.0 + lax.erf(values * (0.5**0.5)))
    return cdf + values * jnp.exp(-0.5 * values * values) * 0.3989422804014327


def scale_rows(rows):
    centre = jnp.mean(rows, axis=-1, keepdims=True)
    centred = rows - centre
    inv_scale = lax.rsqrt(jnp.mean(centred * centred, axis=-1, keepdims=True) + EPSILON)
    return centred * inv_scale, inv_scale


def norm_back(out_grad, scaled, inv_scale, gain):
    weighted = out_grad * gain
    return inv_scale * (
        weighted
        - jnp.mean(weighted, axis=-1, keepdims=True)
        - scaled * jnp.mean(weighted * scaled, axis=-1, keepdims=True)
    )


def swap(value, bits):
    return lax.ppermute(value, "fsdp", [(i, i ^ bits) for i in range(NF)])


def gather_blocks(block):
    across = swap(block, 2)
    beside = swap(block, 1)
    corner = swap(across, 1)
    return [block, beside, across, corner]


def gather_row(block):
    return jnp.concatenate(gather_blocks(block), axis=0)


def scatter_blocks(send, keep, *others):
    got = swap(send, 1).astype(F32)
    far = (keep[1] + got[1]).astype(BF)
    far = swap(after(far, *others) if others else far, 2).astype(F32)
    return keep[0] + got[0] + far


def scatter_row(partial):
    blocks = partial.reshape((NF, -1) + partial.shape[1:])
    return scatter_blocks(jnp.stack([blocks[1], blocks[3]]).astype(BF), (blocks[0], blocks[2]))


def after(value, *others):
    return lax.optimization_barrier((value,) + others)[0]


def deal(blocks):
    own = lax.axis_index("fsdp")
    got = []
    for k in range(NF):
        block = lax.dynamic_index_in_dim(blocks, own ^ k, 0, keepdims=False)
        got.append(block if k == 0 else swap(block, k))
    odd, far = own % 2 == 1, own >= 2
    got = [jnp.where(odd, got[k ^ 1], got[k]) for k in range(NF)]
    return jnp.stack([jnp.where(far, got[k ^ 2], got[k]) for k in range(NF)])


def exchange(value, axes, groups=None):
    return lax.all_to_all(value, axes, 0, 0, axis_index_groups=groups, tiled=True)


def dot(left, right, left_dim, right_dim):
    dims = (((left_dim,), (right_dim,)), ((), ()))
    return lax.dot_general(left, right, dims, preferred_element_type=F32)


def put_partial(partial, send_ref, keep_ref):
    tall = partial.shape[0] // NF
    for k in range(NF):
        block = partial[k * tall : (k + 1) * tall]
        if k % 2 == 0:
            keep_ref[k // 2] = block
        else:
            send_ref[k // 2] = block.astype(BF)


def partial_shapes(tokens, width):
    tall = tokens // NF
    return (
        jax.ShapeDtypeStruct((NF // 2, tall, width), BF),
        jax.ShapeDtypeStruct((NF // 2, tall, width), F32),
    )


def project_kernel(out_ref, wo_ref, send_ref, keep_ref):
    put_partial(mm(out_ref[...], wo_ref[...]), send_ref, keep_ref)


def attend_kernel(*refs, count, heads, lanes):
    a_refs, (w_ref, col_ref, row_ref) = refs[:count], refs[count : count + 3]
    qkv_ref, out_ref, lse_ref = refs[count + 3 :]
    tall = a_refs[0].shape[0]
    for k in range(count):
        qkv_ref[k * tall : (k + 1) * tall] = mm(a_refs[k][...], w_ref[:, lanes]).astype(BF)
    part = heads * HD
    live = (col_ref[...] % 2).astype(F32)
    for h in range(heads):
        q = qkv_ref[:, h * HD : (h + 1) * HD] * BF(HD**-0.5)
        k = qkv_ref[:, part + h * HD : part + (h + 1) * HD]
        v = qkv_ref[:, 2 * part + h * HD : 2 * part + (h + 1) * HD]
        scores = jnp.where(col_ref[...] == row_ref[...], dot(k, q, 1, 1), -1e30)
        top = jnp.max(scores, axis=0, keepdims=True)
        shifted = jnp.exp(scores - top)
        total = jnp.sum(shifted, axis=0, keepdims=True)
        soft = (shifted * (1.0 / total)).astype(BF)
        out_ref[:, h * HD : (h + 1) * HD] = (dot(soft, v, 0, 0) * live).astype(BF)
        lse_ref[h : h + 1] = top + jnp.log(total)


def attend_back_kernel(*refs, count, heads, lanes):
    dy_refs, (w_ref, wo_ref, qkv_ref, lse_ref, col_ref, row_ref) = refs[:count], refs[count : count + 6]
    dqkv_ref, send_ref, keep_ref, do_ref = refs[count + 6 :]
    tall = dy_refs[0].shape[0]
    part = heads * HD
    for k in range(count):
        live = (col_ref[k * tall : (k + 1) * tall] % 2).astype(F32)
        do_ref[k * tall : (k + 1) * tall] = (dot(dy_refs[k][...], wo_ref[...], 1, 1) * live).astype(BF)
    for h in range(heads):
        q = qkv_ref[:, h * HD : (h + 1) * HD] * BF(HD**-0.5)
        k = qkv_ref[:, part + h * HD : part + (h + 1) * HD]
        v = qkv_ref[:, 2 * part + h * HD : 2 * part + (h + 1) * HD]
        do = do_ref[:, h * HD : (h + 1) * HD]
        soft = jnp.exp(dot(k, q, 1, 1) - lse_ref[h : h + 1])
        soft = jnp.where(col_ref[...] == row_ref[...], soft, 0.0)
        soft_grad = dot(v, do, 1, 1)
        row_dot = jnp.sum(soft * soft_grad, axis=0, keepdims=True)
        score_grad = (soft * (soft_grad - row_dot)).astype(BF)
        dq = dot(score_grad, k, 0, 0) * HD**-0.5
        dqkv_ref[:, h * HD : (h + 1) * HD] = dq.astype(BF)
        dk = dot(score_grad, q, 1, 0)
        dqkv_ref[:, part + h * HD : part + (h + 1) * HD] = dk.astype(BF)
        dv = dot(soft.astype(BF), do, 1, 0)
        dqkv_ref[:, 2 * part + h * HD : 2 * part + (h + 1) * HD] = dv.astype(BF)
    put_partial(dot(dqkv_ref[...], w_ref[:, lanes], 1, 1), send_ref, keep_ref)


def mlp_parts(w_ref):
    groups, rows, width = w_ref.shape
    half = rows // 2
    return w_ref[:, :half].reshape(groups * half, width), w_ref[:, half:].reshape(groups * half, width)


def mlp_kernel(*refs):
    c_refs, (w_ref, u_ref, g_ref, send_ref, keep_ref) = refs[:NF], refs[NF:]
    w_in, w_out = mlp_parts(w_ref)
    for k in range(NF):
        u = mm(c_refs[k][...], w_in)
        u_ref[k] = u
        g = gelu(u).astype(BF)
        g_ref[k] = g
        partial = mm(g, w_out)
        if k % 2 == 0:
            keep_ref[k // 2] = partial
        else:
            send_ref[k // 2] = partial.astype(BF)


def mlp_back_kernel(*refs):
    dm_refs, (u_ref, w_ref, du_ref, send_ref, keep_ref) = refs[:NF], refs[NF:]
    w_in, w_out = mlp_parts(w_ref)
    for k in range(NF):
        du = (dot(dm_refs[k][...], w_out, 1, 1) * gelu_slope(u_ref[k])).astype(BF)
        du_ref[k] = du
        partial = dot(du, w_in, 1, 1)
        if k % 2 == 0:
            keep_ref[k // 2] = partial
        else:
            send_ref[k // 2] = partial.astype(BF)


def mlp_weights_kernel(*refs):
    c_refs, dm_refs = refs[:NF], refs[NF : 2 * NF]
    du_ref, g_ref, rest_ref, out_ref, sum_ref = refs[2 * NF :]
    groups, rows, width = rest_ref.shape
    for step in range(2):
        for k in range(NF):
            if step == 0:
                term = dot(c_refs[k][...], du_ref[k], 0, 0)
            else:
                term = dot(g_ref[k], dm_refs[k][...], 0, 0)
            if k == 0:
                sum_ref[...] = term
            else:
                sum_ref[...] += term
        for d in range(groups):
            out_ref[d, :, step * width : (step + 1) * width] = sum_ref[d * rows : (d + 1) * rows].astype(BF)
    for d in range(groups):
        out_ref[d, :, 2 * width :] = rest_ref[d]


def whole(kernel, outs, args, flops, scratch=()):
    space = pl.BlockSpec(memory_space=pltpu.VMEM)
    return pl.pallas_call(
        kernel,
        out_shape=outs,
        in_specs=[space] * len(args),
        out_specs=jax.tree.map(lambda _: space, outs),
        scratch_shapes=scratch,
        compiler_params=pltpu.CompilerParams(vmem_limit_bytes=48 * 2**20),
        cost_estimate=pl.CostEstimate(flops=flops, bytes_accessed=2**16, transcendentals=0),
    )(*args)


def attend(a_blocks, w_qkv, w_out, code_row):
    w_qkv, lanes = w_qkv
    tokens, width = code_row.shape[0], w_qkv.shape[0]
    heads = HEADS // NF
    part = heads * HD
    outs = (
        jax.ShapeDtypeStruct((tokens, 3 * part), BF),
        jax.ShapeDtypeStruct((tokens, part), BF),
        jax.ShapeDtypeStruct((heads, tokens), F32),
    )
    kernel = functools.partial(attend_kernel, count=len(a_blocks), heads=heads, lanes=lanes)
    args = (*a_blocks, w_qkv, code_row[:, None], code_row[None])
    qkv, out, lse = whole(kernel, outs, args, 4 * 10**8)
    send, keep = whole(project_kernel, partial_shapes(tokens, width), (out, w_out), 10**8)
    return qkv, out, lse, send, keep


def attend_back(dy_blocks, w_qkv, w_out, qkv, lse, code_row):
    w_qkv, lanes = w_qkv
    tokens, width = code_row.shape[0], w_qkv.shape[0]
    heads = HEADS // NF
    outs = (jax.ShapeDtypeStruct(qkv.shape, BF),) + partial_shapes(tokens, width)
    kernel = functools.partial(attend_back_kernel, count=len(dy_blocks), heads=heads, lanes=lanes)
    args = (*dy_blocks, w_qkv, w_out, qkv, lse, code_row[:, None], code_row[None])
    return whole(kernel, outs, args, 11 * 10**9, (pltpu.VMEM((tokens, heads * HD), BF),))


def mlp(c_blocks, weights):
    tall, width = c_blocks[0].shape
    hidden = weights.shape[0] * weights.shape[1] // 2
    outs = (
        jax.ShapeDtypeStruct((NF, tall, hidden), F32),
        jax.ShapeDtypeStruct((NF, tall, hidden), BF),
    ) + partial_shapes(NF * tall, width)
    return whole(mlp_kernel, outs, (*c_blocks, weights), 3 * 10**8)


def mlp_back(dm_blocks, u, weights):
    tall, width = dm_blocks[0].shape
    outs = (jax.ShapeDtypeStruct(u.shape, BF),) + partial_shapes(NF * tall, width)
    return whole(mlp_back_kernel, outs, (*dm_blocks, u, weights), 6 * 10**9)


def mlp_weights(c_blocks, dm_blocks, du, g, rest):
    groups, rows, width = rest.shape
    if rows % 16 == 0:
        outs = jax.ShapeDtypeStruct((groups, rows, 3 * width), BF)
        args = (*c_blocks, *dm_blocks, du, g, rest)
        return whole(mlp_weights_kernel, outs, args, 5 * 10**9, (pltpu.VMEM((width, width), F32),))
    parts = [mm_tn(jnp.concatenate(c_blocks, axis=0), du.reshape(-1, width))]
    parts.append(mm_tn(g.reshape(-1, width), jnp.concatenate(dm_blocks, axis=0)))
    parts = [value.astype(BF).reshape(groups, rows, width) for value in parts]
    return jnp.concatenate(parts + [rest], axis=2)


def expert_kernel(*refs):
    own_ref, x_refs, dz_refs, in_refs, out_refs = refs[0], refs[1:3], refs[3:5], refs[5:7], refs[7:9]
    router_ref, dx_send, dx_keep, y_send, y_keep = refs[9:14]
    din_own, din_far, dout_own, dout_far, drouter_ref, din_sum, dout_sum = refs[14:]
    router = router_ref[...]
    for i in range(2):
        x, dz = x_refs[i][...], dz_refs[i][...]
        logits = mm(x, router)
        lane = lax.broadcasted_iota(jnp.int32, logits.shape, 1)
        shifted = jnp.exp(logits - jnp.max(logits, axis=1, keepdims=True))
        probs = shifted / jnp.sum(shifted, axis=1, keepdims=True)
        mine = (lane == own_ref[0]).astype(F32)
        prob = jnp.sum(probs * mine, axis=1, keepdims=True)
        gate = prob.astype(BF).astype(F32)
        dz_wide = dz.astype(F32)
        dyx = (gate * dz_wide).astype(BF)
        y = dx = None
        for j in range(2):
            w_in, w_out = in_refs[j][...], out_refs[j][...]
            ue = mm(x, w_in)
            cdf = 0.5 * (1.0 + lax.erf(ue * (0.5**0.5)))
            slope = cdf + ue * jnp.exp(-0.5 * ue * ue) * 0.3989422804014327
            ge = (ue * cdf).astype(BF)
            due = (dot(dyx, w_out, 1, 1) * slope).astype(BF)
            term = mm(ge, w_out)
            y = term if j == 0 else y + term
            term = dot(due, w_in, 1, 1)
            dx = term if j == 0 else dx + term
            din, dout = dot(x, due, 0, 0), dot(ge, dyx, 0, 0)
            din_ref, dout_ref = (din_own, dout_own) if j == 0 else (din_sum, dout_sum)
            if i == 0:
                din_ref[...], dout_ref[...] = din, dout
            else:
                din_ref[...] += din
                dout_ref[...] += dout
        dgate = jnp.sum(dz_wide * y, axis=1, keepdims=True)
        dlogits = (dgate * prob * (mine - probs)).astype(BF)
        dx = dx + dot(dlogits, router, 1, 1)
        y = gate * y
        if i == 0:
            dx_keep[...], y_keep[...], drouter_ref[...] = dx, y, dot(x, dlogits, 0, 0)
        else:
            dx_send[...], y_send[...] = dx.astype(BF), y.astype(BF)
            drouter_ref[...] += dot(x, dlogits, 0, 0)
    din_far[...], dout_far[...] = din_sum[...].astype(BF), dout_sum[...].astype(BF)


def expert_compute(own, x_blocks, dz_blocks, w_in, w_out, router):
    tall, width = x_blocks[0].shape
    square = w_in[0].shape
    send, keep = jax.ShapeDtypeStruct((tall, width), BF), jax.ShapeDtypeStruct((tall, width), F32)
    near, far = jax.ShapeDtypeStruct(square, F32), jax.ShapeDtypeStruct(square, BF)
    outs = (send, keep, send, keep, near, far, near, far, jax.ShapeDtypeStruct(router.shape, F32))
    space = pl.BlockSpec(memory_space=pltpu.VMEM)
    return pl.pallas_call(
        expert_kernel,
        out_shape=outs,
        in_specs=[pl.BlockSpec(memory_space=pltpu.SMEM)] + [space] * 9,
        out_specs=(space,) * len(outs),
        scratch_shapes=[pltpu.VMEM(square, F32), pltpu.VMEM(square, F32)],
        compiler_params=pltpu.CompilerParams(vmem_limit_bytes=56 * 2**20),
        cost_estimate=pl.CostEstimate(
            flops=64 * tall * width * square[1], bytes_accessed=2**24, transcendentals=0
        ),
    )(own.astype(jnp.int32)[None], *x_blocks, *dz_blocks, *w_in, *w_out, router)


def make_shards(n_dp):
    n_all = n_dp * NF

    def shards(
        patches, segment_ids, live, expert_ids, ranks, norm_gains, norm_biases, attn_qkv, attn_out,
        mlp_in, mlp_out, router, exp_in, exp_out, cotangent,
    ):
        width = patches.shape[-1]
        tokens = patches.shape[0] * patches.shape[1]
        experts = exp_in.shape[0]
        clones = n_dp // experts
        part = width // NF
        rows = attn_qkv.shape[1]
        hid = mlp_out.shape[0]
        own_f = lax.axis_index("fsdp")
        own_dp = lax.axis_index("dp")
        groups = ring = None
        if clones > 1:
            groups = [[g * experts + e for e in range(experts)] for g in range(clones)]
            ring = [[g * experts + e for g in range(clones)] for e in range(experts)]
        capacity = (210 * tokens + 100 * experts - 1) // (100 * experts)
        slots = (capacity + 7) // 8 * 8

        code = (segment_ids * 2 + live).reshape(tokens)
        code_all = gather_row(code)
        live_all = (code_all % 2).astype(F32)
        rows_all = gather_row(patches.reshape(tokens, width))

        def qkv_block(layer):
            weight = attn_qkv[layer].reshape(rows, 3, NF, part)
            return jnp.transpose(weight, (2, 0, 1, 3)).reshape(NF, rows, 3 * part)

        small = jnp.concatenate(
            [norm_gains.T, norm_biases.T, router, jnp.zeros((rows, 128 - 8 - experts), BF)], axis=1
        )
        small = jnp.broadcast_to(small[None], (NF, rows, 128))
        def to_everyone(blocks):
            full = jnp.broadcast_to(blocks[None], (n_dp,) + blocks.shape)
            return exchange(full.reshape((n_all, rows, -1)), ALL).reshape(width, -1)

        first = to_everyone(jnp.concatenate([small, qkv_block(0)], axis=2))
        small_all, w_qkv0 = first[:, :128], (first, slice(128, 128 + 3 * part))
        norms = small_all[:, :8].T.astype(F32)
        gains, biases = norms[:4], norms[4:]
        w_router = small_all[:, 8 : 8 + experts]

        mlp_block = jnp.transpose(mlp_in.reshape(rows, n_dp, NF, hid), (2, 0, 1, 3))
        mlp_block = deal(mlp_block.reshape(NF, rows, n_dp * hid)).reshape(NF * rows, width)
        mlp_all = lax.all_gather(jnp.concatenate([mlp_block, mlp_out], axis=0), "dp")

        to_heads = [(j, j % n_dp * NF + j // n_dp) for j in range(n_all)]
        to_owner = [(b, a) for a, b in to_heads]
        held_out = lax.ppermute(attn_out, ALL, to_heads)
        held = after(held_out[0], first)
        w_out0 = exchange(jnp.broadcast_to(held[None], (n_dp, rows, width)), "dp").reshape(part, width)

        choice = expert_ids.reshape(tokens, 2)
        rank = ranks.reshape(tokens, 2)
        place = jnp.where(rank < capacity, choice * slots + rank, -1)
        slot_index = jnp.arange(experts * slots, dtype=jnp.int32)[:, None]
        pick = (place[:, 0][None] == slot_index) | (place[:, 1][None] == slot_index)
        pick = pick.astype(BF)

        def to_experts(block):
            held = mm(pick, block).astype(BF).reshape(experts, slots, width)
            return exchange(held, "dp", groups).reshape(experts * slots, width)

        top_grad = cotangent.reshape(tokens, width)
        in_block = jnp.transpose(exp_in.reshape(experts, rows, n_dp, NF, hid), (3, 0, 1, 2, 4))
        in_block = in_block.reshape(NF, experts, rows, n_dp * hid)
        if clones == 1:
            in_block = jnp.swapaxes(deal(in_block), 0, 1).reshape(experts, NF * rows, n_dp * hid)
            held = deal(qkv_block(1)).reshape(NF * rows, 3 * part)
            held = jnp.concatenate([held, held_out[1].reshape(NF * rows, part)], axis=1)
            held = jnp.broadcast_to(held[None], (n_dp,) + held.shape)
            in_block = jnp.concatenate([in_block, held], axis=2)

        h0 = patches.reshape(tokens, width).astype(F32)
        xhat0_all, _ = scale_rows(rows_all.astype(F32))
        a0 = (xhat0_all * gains[0] + biases[0]).astype(BF)
        qkv0, o0, lse0, send, keep = attend([a0], w_qkv0, w_out0, code_all)
        h1 = h0 + scatter_blocks(after(send, in_block) if clones == 1 else send, keep)

        if clones == 1:
            held = exchange(after(in_block, w_out0), "dp").reshape(width, -1)
            cut = n_dp * hid
            w_exp_in, w_qkv1 = held[:, :cut], (held, slice(cut, cut + 3 * part))
            w_out1 = held[:, cut + 3 * part :].reshape(part, width)
        else:
            held = exchange(in_block, "fsdp")
            held = exchange(jnp.swapaxes(held, 0, 1), "dp", groups)
            w_exp_in = lax.all_gather(held, "dp", axis_index_groups=ring).reshape(width, n_dp * hid)
            w_qkv1 = (to_everyone(qkv_block(1)), slice(0, 3 * part))
            w_out1 = lax.all_gather(held_out[1], "dp").reshape(part, width)
        if clones == 1:
            dz = mm(pick, top_grad).astype(BF).reshape(experts, slots, width)
            held = exchange(after(jnp.concatenate([dz, exp_out], axis=1), w_exp_in), "dp")
            dz, w_exp_out = held[:, :slots].reshape(experts * slots, width), held[:, slots:]
        else:
            dz = to_experts(top_grad)
            w_exp_out = exchange(exp_out, "dp", groups)
            w_exp_out = lax.all_gather(w_exp_out, "dp", axis_index_groups=ring)
        w_exp_out = w_exp_out.reshape(n_dp * hid, width)

        xhat1, inv1 = scale_rows(h1)
        c0 = gather_blocks((xhat1 * gains[1] + biases[1]).astype(BF))
        u0, g0, send, keep = mlp(c0, mlp_all)
        h2 = h1 + scatter_blocks(send, keep)

        w_in_far = swap(w_exp_in, 2)
        xhat2, inv2 = scale_rows(h2)
        a1 = gather_blocks(after((xhat2 * gains[2] + biases[2]).astype(BF), w_exp_in))
        qkv1, o1, lse1, send, keep = attend(a1, w_qkv1, w_out1, code_all)
        h3 = h2 + scatter_blocks(send, keep, w_in_far)

        xhat3, inv3 = scale_rows(h3)
        c1 = after((xhat3 * gains[3] + biases[3]).astype(BF), dz, w_exp_out)
        w_out_far = swap(w_exp_out, 2)
        dz = (dz, swap(dz, 1))
        x = after(to_experts(c1), w_out_far)
        x = (x, swap(x, 1))
        dx_send, dx_keep, y_send, y_keep, din_own, din_far, dout_own, dout_far, router_part = expert_compute(
            own_dp % experts, x, dz, (w_exp_in, w_in_far), (w_exp_out, w_out_far), w_router
        )
        dx = (dx_keep + swap(dx_send, 1).astype(F32)).astype(BF)
        y = (y_keep + swap(after(y_send, dx), 1).astype(F32)).astype(BF)
        exp_in_part = (din_own + swap(after(din_far, dx), 2).astype(F32)).astype(BF)
        exp_out_part = (dout_own + swap(after(dout_far, exp_in_part), 2).astype(F32)).astype(BF)
        dx = exchange(dx.reshape(experts, slots, width), "dp", groups)

        if clones == 1:
            back = exp_out_part.reshape(experts, hid, width)
            back = jnp.concatenate([y.reshape(experts, slots, width), back], axis=1)
            in_got = exchange(after(exp_in_part.reshape(n_dp, NF * rows, n_dp * hid), dx), "dp")
            got = exchange(after(back, in_got), "dp")
            y, exp_out_grads = got[:, :slots], got[:, slots:].astype(F32)
        else:
            back = lax.psum_scatter(
                exp_out_part.reshape(clones, experts, hid, width), "dp", axis_index_groups=ring
            )
            exp_out_grads = exchange(back, "dp", groups).astype(F32)
            got = exp_out_grads
            y = exchange(y.reshape(experts, slots, width), "dp", groups)
            held = lax.psum_scatter(
                exp_in_part.reshape(clones, experts, NF, rows, n_dp * hid), "dp", axis_index_groups=ring
            )
            in_got = exchange(held, "dp", groups)
        dc1 = mm_tn(pick, after(dx, exp_in_part).reshape(experts * slots, width))

        def rows_to_owners(grad):
            cols = grad.shape[1]
            got = exchange(grad.astype(BF).reshape(n_all, rows, cols), ALL)
            return got.reshape(n_dp, NF, rows, cols).astype(F32)

        def qkv_layout(total):
            parts = total.reshape(NF, rows, 3, part)
            return jnp.transpose(parts, (1, 2, 0, 3)).reshape(rows, 3 * width)

        def sums(out_grad, xhat):
            return jnp.sum(out_grad * xhat, axis=0), jnp.sum(out_grad, axis=0)

        gain3, bias3 = sums(dc1, xhat3)
        grad = top_grad.astype(F32) + norm_back(dc1, xhat3, inv3, gains[3])

        dy1 = gather_blocks(grad.astype(BF))
        dqkv1, send, keep = attend_back(dy1, w_qkv1, w_out1, qkv1, lse1, code_all)
        da1 = scatter_blocks(after(send, in_got), keep)
        attn_part = [
            mm_tn(jnp.concatenate(a1, axis=0), dqkv1).astype(BF).reshape(n_dp, NF * rows, 3 * part),
            mm_tn(o1, jnp.concatenate(dy1, axis=0)).astype(BF).reshape(n_dp, NF * rows, part),
        ]
        attn_part = jnp.concatenate(attn_part, axis=2)
        gain2, bias2 = sums(da1, xhat2)
        grad = grad + norm_back(da1, xhat2, inv2, gains[2])

        dm = gather_blocks(grad.astype(BF))
        du0, send, keep = mlp_back(dm, after(u0, attn_part), mlp_all)
        dc0 = scatter_blocks(send, keep)
        dense_part = mlp_weights(c0, dm, du0, after(g0, got), attn_part)
        dense_sum = lax.psum_scatter(dense_part, "dp")
        gain1, bias1 = sums(dc0, xhat1)
        grad = grad + norm_back(dc0, xhat1, inv1, gains[1])

        dy0 = gather_blocks(grad.astype(BF))
        dqkv0, send, keep = attend_back([after(dy0[0], dense_part), *dy0[1:]], w_qkv0, w_out0, qkv0, lse0, code_all)
        out_part0 = mm_tn(o0, jnp.concatenate(dy0, axis=0)).astype(BF).reshape(n_dp, rows, width)
        out_got0 = exchange(after(out_part0, got), "dp")
        qkv_part0 = mm_tn(a0, dqkv0)
        h4 = h3 + mm_tn(pick, y.reshape(experts * slots, width))
        activations = h4.astype(BF)
        da0 = scatter_blocks(send, keep)
        xhat0_blocks = xhat0_all.reshape(NF, tokens, width)
        gain0 = bias0 = 0.0
        for k in range(NF):
            block = keep[k // 2] if k % 2 == 0 else send[k // 2].astype(F32)
            block_gain, block_bias = sums(block, xhat0_blocks[k])
            gain0, bias0 = gain0 + block_gain, bias0 + block_bias
        columns = jnp.stack([gain0, gain1, gain2, gain3, bias0, bias1, bias2, bias3], axis=1)
        columns = jnp.concatenate(
            [columns, router_part, jnp.zeros((width, 128 - 8 - experts), F32), qkv_part0], axis=1
        )
        tail = rows_to_owners(after(columns, out_got0))
        total = jnp.sum(tail, axis=0)
        small_grads = jnp.sum(total[:, :, :128], axis=0)
        qkv_grad0 = qkv_layout(total[:, :, 128:])
        dense_sum = after(dense_sum, tail)
        in_got = jnp.swapaxes(after(in_got, dqkv0).reshape(experts, NF, rows, n_dp * hid), 0, 1)
        in_got = deal(in_got).reshape(NF, experts, rows, n_dp, hid)
        exp_in_grads = jnp.transpose(in_got, (1, 2, 3, 0, 4))
        exp_in_grads = exp_in_grads.reshape(experts, rows, n_dp * NF * hid).astype(F32)
        held = jnp.concatenate([dense_sum[:, :width], dense_sum[:, 2 * width : 2 * width + 3 * part]], axis=1)
        held = exchange(held.reshape(NF, rows, -1), "fsdp").astype(F32)
        mlp_in_grads = held[..., :width].reshape(NF, rows, n_dp, hid)
        mlp_in_grads = jnp.transpose(mlp_in_grads, (1, 2, 0, 3)).reshape(rows, n_dp * NF * hid)
        qkv_grad1 = qkv_layout(held[..., width:])
        mlp_out_grads = dense_sum[:, width : 2 * width].astype(F32)
        out_sum1 = dense_sum[:, 2 * width + 3 * part :].reshape(rows, width).astype(F32)
        out_sums = jnp.stack([jnp.sum(out_got0.astype(F32), axis=0), out_sum1])
        proj_grads = lax.ppermute(out_sums, ALL, to_owner)
        xhat0, inv0 = scale_rows(h0)
        grad = grad + norm_back(da0, xhat0, inv0, gains[0])

        norm_grads = small_grads[:, :8].T
        return (
            activations.reshape(patches.shape),
            grad.reshape(patches.shape),
            norm_grads[:4],
            norm_grads[4:7],
            norm_grads[7],
            jnp.stack([qkv_grad0, qkv_grad1]),
            proj_grads,
            mlp_in_grads,
            mlp_out_grads,
            small_grads[:, 8 : 8 + experts],
            exp_in_grads,
            exp_out_grads,
        )

    return shards


def solution(mesh):
    by_row = P("dp", "fsdp", None)
    second = P(None, ("dp", "fsdp"), None)
    first = P(("dp", "fsdp"), None)
    pair = P("dp", "fsdp")
    norm = P(None, ("dp", "fsdp"))
    return jax.shard_map(
        make_shards(mesh.shape["dp"]),
        mesh=mesh,
        in_specs=(
            by_row, pair, pair, by_row, by_row, norm, norm, second, second, first, first, first,
            second, second, by_row,
        ),
        out_specs=(
            by_row, by_row, norm, norm, P(("dp", "fsdp")), second, second, first, first, first,
            second, second,
        ),
        check_vma=False,
    )
```

```python
import functools

import jax
import jax.numpy as jnp
from jax import lax
from jax.experimental import pallas as pl
from jax.experimental.pallas import tpu as pltpu
from jax.sharding import PartitionSpec as P

HEADS = 12
HD = 64
EPSILON = 1e-06
NF = 4
ALL = ("dp", "fsdp")
BF = jnp.bfloat16
F32 = jnp.float32


def mm(left, right):
    return jnp.dot(left, right, preferred_element_type=F32)


def mm_tn(left, right):
    return lax.dot_general(left, right, (((0,), (0,)), ((), ())), preferred_element_type=F32)


def mm_nt(left, right):
    return lax.dot_general(left, right, (((1,), (1,)), ((), ())), preferred_element_type=F32)


def gelu(values):
    return 0.5 * values * (1.0 + lax.erf(values * (0.5**0.5)))


def gelu_slope(values):
    cdf = 0.5 * (1.0 + lax.erf(values * (0.5**0.5)))
    return cdf + values * jnp.exp(-0.5 * values * values) * 0.3989422804014327


def scale_rows(rows):
    centre = jnp.mean(rows, axis=-1, keepdims=True)
    centred = rows - centre
    inv_scale = lax.rsqrt(jnp.mean(centred * centred, axis=-1, keepdims=True) + EPSILON)
    return centred * inv_scale, inv_scale


def norm_back(out_grad, scaled, inv_scale, gain):
    weighted = out_grad * gain
    return inv_scale * (
        weighted
        - jnp.mean(weighted, axis=-1, keepdims=True)
        - scaled * jnp.mean(weighted * scaled, axis=-1, keepdims=True)
    )


def swap(value, bits):
    return lax.ppermute(value, "fsdp", [(i, i ^ bits) for i in range(NF)])


def gather_blocks(block):
    across = swap(block, 2)
    beside = swap(block, 1)
    corner = swap(across, 1)
    return [block, beside, across, corner]


def gather_row(block):
    return jnp.concatenate(gather_blocks(block), axis=0)


def scatter_blocks(send, keep, *others):
    got = swap(send, 1).astype(F32)
    far = (keep[1] + got[1]).astype(BF)
    far = swap(after(far, *others) if others else far, 2).astype(F32)
    return keep[0] + got[0] + far


def scatter_row(partial):
    blocks = partial.reshape((NF, -1) + partial.shape[1:])
    return scatter_blocks(jnp.stack([blocks[1], blocks[3]]).astype(BF), (blocks[0], blocks[2]))


def after(value, *others):
    return lax.optimization_barrier((value,) + others)[0]


def deal(blocks):
    own = lax.axis_index("fsdp")
    got = []
    for k in range(NF):
        block = lax.dynamic_index_in_dim(blocks, own ^ k, 0, keepdims=False)
        got.append(block if k == 0 else swap(block, k))
    odd, far = own % 2 == 1, own >= 2
    got = [jnp.where(odd, got[k ^ 1], got[k]) for k in range(NF)]
    return jnp.stack([jnp.where(far, got[k ^ 2], got[k]) for k in range(NF)])


def exchange(value, axes, groups=None):
    return lax.all_to_all(value, axes, 0, 0, axis_index_groups=groups, tiled=True)


def dot(left, right, left_dim, right_dim):
    dims = (((left_dim,), (right_dim,)), ((), ()))
    return lax.dot_general(left, right, dims, preferred_element_type=F32)


def put_partial(partial, send_ref, keep_ref):
    tall = partial.shape[0] // NF
    for k in range(NF):
        block = partial[k * tall : (k + 1) * tall]
        if k % 2 == 0:
            keep_ref[k // 2] = block
        else:
            send_ref[k // 2] = block.astype(BF)


def partial_shapes(tokens, width):
    tall = tokens // NF
    return (
        jax.ShapeDtypeStruct((NF // 2, tall, width), BF),
        jax.ShapeDtypeStruct((NF // 2, tall, width), F32),
    )


def project_kernel(out_ref, wo_ref, send_ref, keep_ref):
    put_partial(mm(out_ref[...], wo_ref[...]), send_ref, keep_ref)


def attend_kernel(*refs, count, heads, lanes):
    a_refs, (w_ref, col_ref, row_ref) = refs[:count], refs[count : count + 3]
    qkv_ref, out_ref, lse_ref = refs[count + 3 :]
    tall = a_refs[0].shape[0]
    for k in range(count):
        qkv_ref[k * tall : (k + 1) * tall] = mm(a_refs[k][...], w_ref[:, lanes]).astype(BF)
    part = heads * HD
    live = (col_ref[...] % 2).astype(F32)
    for h in range(heads):
        q = qkv_ref[:, h * HD : (h + 1) * HD] * BF(HD**-0.5)
        k = qkv_ref[:, part + h * HD : part + (h + 1) * HD]
        v = qkv_ref[:, 2 * part + h * HD : 2 * part + (h + 1) * HD]
        scores = jnp.where(col_ref[...] == row_ref[...], dot(k, q, 1, 1), -1e30)
        top = jnp.max(scores, axis=0, keepdims=True)
        shifted = jnp.exp(scores - top)
        total = jnp.sum(shifted, axis=0, keepdims=True)
        soft = (shifted * (1.0 / total)).astype(BF)
        out_ref[:, h * HD : (h + 1) * HD] = (dot(soft, v, 0, 0) * live).astype(BF)
        lse_ref[h : h + 1] = top + jnp.log(total)


def attend_back_kernel(*refs, count, heads, lanes):
    dy_refs, (w_ref, wo_ref, qkv_ref, lse_ref, col_ref, row_ref) = refs[:count], refs[count : count + 6]
    dqkv_ref, send_ref, keep_ref, do_ref = refs[count + 6 :]
    tall = dy_refs[0].shape[0]
    part = heads * HD
    for k in range(count):
        live = (col_ref[k * tall : (k + 1) * tall] % 2).astype(F32)
        do_ref[k * tall : (k + 1) * tall] = (dot(dy_refs[k][...], wo_ref[...], 1, 1) * live).astype(BF)
    for h in range(heads):
        q = qkv_ref[:, h * HD : (h + 1) * HD] * BF(HD**-0.5)
        k = qkv_ref[:, part + h * HD : part + (h + 1) * HD]
        v = qkv_ref[:, 2 * part + h * HD : 2 * part + (h + 1) * HD]
        do = do_ref[:, h * HD : (h + 1) * HD]
        soft = jnp.exp(dot(k, q, 1, 1) - lse_ref[h : h + 1])
        soft = jnp.where(col_ref[...] == row_ref[...], soft, 0.0)
        soft_grad = dot(v, do, 1, 1)
        row_dot = jnp.sum(soft * soft_grad, axis=0, keepdims=True)
        score_grad = (soft * (soft_grad - row_dot)).astype(BF)
        dq = dot(score_grad, k, 0, 0) * HD**-0.5
        dqkv_ref[:, h * HD : (h + 1) * HD] = dq.astype(BF)
        dk = dot(score_grad, q, 1, 0)
        dqkv_ref[:, part + h * HD : part + (h + 1) * HD] = dk.astype(BF)
        dv = dot(soft.astype(BF), do, 1, 0)
        dqkv_ref[:, 2 * part + h * HD : 2 * part + (h + 1) * HD] = dv.astype(BF)
    put_partial(dot(dqkv_ref[...], w_ref[:, lanes], 1, 1), send_ref, keep_ref)


def mlp_parts(w_ref):
    groups, rows, width = w_ref.shape
    half = rows // 2
    return w_ref[:, :half].reshape(groups * half, width), w_ref[:, half:].reshape(groups * half, width)


def mlp_kernel(*refs):
    c_refs, (w_ref, u_ref, g_ref, send_ref, keep_ref) = refs[:NF], refs[NF:]
    w_in, w_out = mlp_parts(w_ref)
    for k in range(NF):
        u = mm(c_refs[k][...], w_in)
        u_ref[k] = u
        g = gelu(u).astype(BF)
        g_ref[k] = g
        partial = mm(g, w_out)
        if k % 2 == 0:
            keep_ref[k // 2] = partial
        else:
            send_ref[k // 2] = partial.astype(BF)


def mlp_back_kernel(*refs):
    dm_refs, (u_ref, w_ref, du_ref, send_ref, keep_ref) = refs[:NF], refs[NF:]
    w_in, w_out = mlp_parts(w_ref)
    for k in range(NF):
        du = (dot(dm_refs[k][...], w_out, 1, 1) * gelu_slope(u_ref[k])).astype(BF)
        du_ref[k] = du
        partial = dot(du, w_in, 1, 1)
        if k % 2 == 0:
            keep_ref[k // 2] = partial
        else:
            send_ref[k // 2] = partial.astype(BF)


def mlp_weights_kernel(*refs):
    c_refs, dm_refs = refs[:NF], refs[NF : 2 * NF]
    du_ref, g_ref, rest_ref, out_ref, sum_ref = refs[2 * NF :]
    groups, rows, width = rest_ref.shape
    for step in range(2):
        for k in range(NF):
            if step == 0:
                term = dot(c_refs[k][...], du_ref[k], 0, 0)
            else:
                term = dot(g_ref[k], dm_refs[k][...], 0, 0)
            if k == 0:
                sum_ref[...] = term
            else:
                sum_ref[...] += term
        for d in range(groups):
            out_ref[d, :, step * width : (step + 1) * width] = sum_ref[d * rows : (d + 1) * rows].astype(BF)
    for d in range(groups):
        out_ref[d, :, 2 * width :] = rest_ref[d]


def whole(kernel, outs, args, flops, scratch=()):
    space = pl.BlockSpec(memory_space=pltpu.VMEM)
    return pl.pallas_call(
        kernel,
        out_shape=outs,
        in_specs=[space] * len(args),
        out_specs=jax.tree.map(lambda _: space, outs),
        scratch_shapes=scratch,
        compiler_params=pltpu.CompilerParams(vmem_limit_bytes=48 * 2**20),
        cost_estimate=pl.CostEstimate(flops=flops, bytes_accessed=2**16, transcendentals=0),
    )(*args)


def attend(a_blocks, w_qkv, w_out, code_row):
    w_qkv, lanes = w_qkv
    tokens, width = code_row.shape[0], w_qkv.shape[0]
    heads = HEADS // NF
    part = heads * HD
    outs = (
        jax.ShapeDtypeStruct((tokens, 3 * part), BF),
        jax.ShapeDtypeStruct((tokens, part), BF),
        jax.ShapeDtypeStruct((heads, tokens), F32),
    )
    kernel = functools.partial(attend_kernel, count=len(a_blocks), heads=heads, lanes=lanes)
    args = (*a_blocks, w_qkv, code_row[:, None], code_row[None])
    qkv, out, lse = whole(kernel, outs, args, 4 * 10**8)
    send, keep = whole(project_kernel, partial_shapes(tokens, width), (out, w_out), 10**8)
    return qkv, out, lse, send, keep


def attend_back(dy_blocks, w_qkv, w_out, qkv, lse, code_row):
    w_qkv, lanes = w_qkv
    tokens, width = code_row.shape[0], w_qkv.shape[0]
    heads = HEADS // NF
    outs = (jax.ShapeDtypeStruct(qkv.shape, BF),) + partial_shapes(tokens, width)
    kernel = functools.partial(attend_back_kernel, count=len(dy_blocks), heads=heads, lanes=lanes)
    args = (*dy_blocks, w_qkv, w_out, qkv, lse, code_row[:, None], code_row[None])
    return whole(kernel, outs, args, 11 * 10**9, (pltpu.VMEM((tokens, heads * HD), BF),))


def mlp(c_blocks, weights):
    tall, width = c_blocks[0].shape
    hidden = weights.shape[0] * weights.shape[1] // 2
    outs = (
        jax.ShapeDtypeStruct((NF, tall, hidden), F32),
        jax.ShapeDtypeStruct((NF, tall, hidden), BF),
    ) + partial_shapes(NF * tall, width)
    return whole(mlp_kernel, outs, (*c_blocks, weights), 3 * 10**8)


def mlp_back(dm_blocks, u, weights):
    tall, width = dm_blocks[0].shape
    outs = (jax.ShapeDtypeStruct(u.shape, BF),) + partial_shapes(NF * tall, width)
    return whole(mlp_back_kernel, outs, (*dm_blocks, u, weights), 10**8)


def mlp_weights(c_blocks, dm_blocks, du, g, rest):
    groups, rows, width = rest.shape
    if rows % 16 == 0:
        outs = jax.ShapeDtypeStruct((groups, rows, 3 * width), BF)
        args = (*c_blocks, *dm_blocks, du, g, rest)
        return whole(mlp_weights_kernel, outs, args, 10**8, (pltpu.VMEM((width, width), F32),))
    parts = [mm_tn(jnp.concatenate(c_blocks, axis=0), du.reshape(-1, width))]
    parts.append(mm_tn(g.reshape(-1, width), jnp.concatenate(dm_blocks, axis=0)))
    parts = [value.astype(BF).reshape(groups, rows, width) for value in parts]
    return jnp.concatenate(parts + [rest], axis=2)


def expert_kernel(*refs):
    own_ref, x_refs, dz_refs, in_refs, out_refs = refs[0], refs[1:3], refs[3:5], refs[5:7], refs[7:9]
    router_ref, dx_send, dx_keep, y_send, y_keep = refs[9:14]
    din_own, din_far, dout_own, dout_far, drouter_ref, din_sum, dout_sum = refs[14:]
    router = router_ref[...]
    for i in range(2):
        x, dz = x_refs[i][...], dz_refs[i][...]
        logits = mm(x, router)
        lane = lax.broadcasted_iota(jnp.int32, logits.shape, 1)
        shifted = jnp.exp(logits - jnp.max(logits, axis=1, keepdims=True))
        probs = shifted / jnp.sum(shifted, axis=1, keepdims=True)
        mine = (lane == own_ref[0]).astype(F32)
        prob = jnp.sum(probs * mine, axis=1, keepdims=True)
        gate = prob.astype(BF).astype(F32)
        dz_wide = dz.astype(F32)
        dyx = (gate * dz_wide).astype(BF)
        y = dx = None
        for j in range(2):
            w_in, w_out = in_refs[j][...], out_refs[j][...]
            ue = mm(x, w_in)
            cdf = 0.5 * (1.0 + lax.erf(ue * (0.5**0.5)))
            slope = cdf + ue * jnp.exp(-0.5 * ue * ue) * 0.3989422804014327
            ge = (ue * cdf).astype(BF)
            due = (dot(dyx, w_out, 1, 1) * slope).astype(BF)
            term = mm(ge, w_out)
            y = term if j == 0 else y + term
            term = dot(due, w_in, 1, 1)
            dx = term if j == 0 else dx + term
            din, dout = dot(x, due, 0, 0), dot(ge, dyx, 0, 0)
            din_ref, dout_ref = (din_own, dout_own) if j == 0 else (din_sum, dout_sum)
            if i == 0:
                din_ref[...], dout_ref[...] = din, dout
            else:
                din_ref[...] += din
                dout_ref[...] += dout
        dgate = jnp.sum(dz_wide * y, axis=1, keepdims=True)
        dlogits = (dgate * prob * (mine - probs)).astype(BF)
        dx = dx + dot(dlogits, router, 1, 1)
        y = gate * y
        if i == 0:
            dx_keep[...], y_keep[...], drouter_ref[...] = dx, y, dot(x, dlogits, 0, 0)
        else:
            dx_send[...], y_send[...] = dx.astype(BF), y.astype(BF)
            drouter_ref[...] += dot(x, dlogits, 0, 0)
    din_far[...], dout_far[...] = din_sum[...].astype(BF), dout_sum[...].astype(BF)


def expert_compute(own, x_blocks, dz_blocks, w_in, w_out, router):
    tall, width = x_blocks[0].shape
    square = w_in[0].shape
    send, keep = jax.ShapeDtypeStruct((tall, width), BF), jax.ShapeDtypeStruct((tall, width), F32)
    near, far = jax.ShapeDtypeStruct(square, F32), jax.ShapeDtypeStruct(square, BF)
    outs = (send, keep, send, keep, near, far, near, far, jax.ShapeDtypeStruct(router.shape, F32))
    space = pl.BlockSpec(memory_space=pltpu.VMEM)
    return pl.pallas_call(
        expert_kernel,
        out_shape=outs,
        in_specs=[pl.BlockSpec(memory_space=pltpu.SMEM)] + [space] * 9,
        out_specs=(space,) * len(outs),
        scratch_shapes=[pltpu.VMEM(square, F32), pltpu.VMEM(square, F32)],
        compiler_params=pltpu.CompilerParams(vmem_limit_bytes=56 * 2**20),
        cost_estimate=pl.CostEstimate(
            flops=64 * tall * width * square[1], bytes_accessed=2**24, transcendentals=0
        ),
    )(own.astype(jnp.int32)[None], *x_blocks, *dz_blocks, *w_in, *w_out, router)


def make_shards(n_dp):
    n_all = n_dp * NF

    def shards(
        patches, segment_ids, live, expert_ids, ranks, norm_gains, norm_biases, attn_qkv, attn_out,
        mlp_in, mlp_out, router, exp_in, exp_out, cotangent,
    ):
        width = patches.shape[-1]
        tokens = patches.shape[0] * patches.shape[1]
        experts = exp_in.shape[0]
        clones = n_dp // experts
        part = width // NF
        rows = attn_qkv.shape[1]
        hid = mlp_out.shape[0]
        own_f = lax.axis_index("fsdp")
        own_dp = lax.axis_index("dp")
        groups = ring = None
        if clones > 1:
            groups = [[g * experts + e for e in range(experts)] for g in range(clones)]
            ring = [[g * experts + e for g in range(clones)] for e in range(experts)]
        capacity = (210 * tokens + 100 * experts - 1) // (100 * experts)
        slots = (capacity + 7) // 8 * 8

        code = (segment_ids * 2 + live).reshape(tokens)
        code_all = gather_row(code)
        live_all = (code_all % 2).astype(F32)
        rows_all = gather_row(patches.reshape(tokens, width))

        def qkv_block(layer):
            weight = attn_qkv[layer].reshape(rows, 3, NF, part)
            return jnp.transpose(weight, (2, 0, 1, 3)).reshape(NF, rows, 3 * part)

        small = jnp.concatenate(
            [norm_gains.T, norm_biases.T, router, jnp.zeros((rows, 128 - 8 - experts), BF)], axis=1
        )
        small = jnp.broadcast_to(small[None], (NF, rows, 128))
        def to_everyone(blocks):
            full = jnp.broadcast_to(blocks[None], (n_dp,) + blocks.shape)
            return exchange(full.reshape((n_all, rows, -1)), ALL).reshape(width, -1)

        first = to_everyone(jnp.concatenate([small, qkv_block(0)], axis=2))
        small_all, w_qkv0 = first[:, :128], (first, slice(128, 128 + 3 * part))
        norms = small_all[:, :8].T.astype(F32)
        gains, biases = norms[:4], norms[4:]
        w_router = small_all[:, 8 : 8 + experts]

        mlp_block = jnp.transpose(mlp_in.reshape(rows, n_dp, NF, hid), (2, 0, 1, 3))
        mlp_block = deal(mlp_block.reshape(NF, rows, n_dp * hid)).reshape(NF * rows, width)
        mlp_all = lax.all_gather(jnp.concatenate([mlp_block, mlp_out], axis=0), "dp")

        to_heads = [(j, j % n_dp * NF + j // n_dp) for j in range(n_all)]
        to_owner = [(b, a) for a, b in to_heads]
        held_out = lax.ppermute(attn_out, ALL, to_heads)
        held = after(held_out[0], first)
        w_out0 = exchange(jnp.broadcast_to(held[None], (n_dp, rows, width)), "dp").reshape(part, width)

        choice = expert_ids.reshape(tokens, 2)
        rank = ranks.reshape(tokens, 2)
        place = jnp.where(rank < capacity, choice * slots + rank, -1)
        slot_index = jnp.arange(experts * slots, dtype=jnp.int32)[:, None]
        pick = (place[:, 0][None] == slot_index) | (place[:, 1][None] == slot_index)
        pick = pick.astype(BF)

        def to_experts(block):
            held = mm(pick, block).astype(BF).reshape(experts, slots, width)
            return exchange(held, "dp", groups).reshape(experts * slots, width)

        top_grad = cotangent.reshape(tokens, width)
        in_block = jnp.transpose(exp_in.reshape(experts, rows, n_dp, NF, hid), (3, 0, 1, 2, 4))
        in_block = in_block.reshape(NF, experts, rows, n_dp * hid)
        if clones == 1:
            in_block = jnp.swapaxes(deal(in_block), 0, 1).reshape(experts, NF * rows, n_dp * hid)
            held = deal(qkv_block(1)).reshape(NF * rows, 3 * part)
            held = jnp.concatenate([held, held_out[1].reshape(NF * rows, part)], axis=1)
            held = jnp.broadcast_to(held[None], (n_dp,) + held.shape)
            in_block = jnp.concatenate([in_block, held], axis=2)

        h0 = patches.reshape(tokens, width).astype(F32)
        xhat0_all, _ = scale_rows(rows_all.astype(F32))
        a0 = (xhat0_all * gains[0] + biases[0]).astype(BF)
        qkv0, o0, lse0, send, keep = attend([a0], w_qkv0, w_out0, code_all)
        h1 = h0 + scatter_blocks(after(send, in_block) if clones == 1 else send, keep)

        if clones == 1:
            held = exchange(after(in_block, w_out0), "dp").reshape(width, -1)
            cut = n_dp * hid
            w_exp_in, w_qkv1 = held[:, :cut], (held, slice(cut, cut + 3 * part))
            w_out1 = held[:, cut + 3 * part :].reshape(part, width)
        else:
            held = exchange(in_block, "fsdp")
            held = exchange(jnp.swapaxes(held, 0, 1), "dp", groups)
            w_exp_in = lax.all_gather(held, "dp", axis_index_groups=ring).reshape(width, n_dp * hid)
            w_qkv1 = (to_everyone(qkv_block(1)), slice(0, 3 * part))
            w_out1 = lax.all_gather(held_out[1], "dp").reshape(part, width)
        if clones == 1:
            dz = mm(pick, top_grad).astype(BF).reshape(experts, slots, width)
            held = exchange(after(jnp.concatenate([dz, exp_out], axis=1), w_exp_in), "dp")
            dz, w_exp_out = held[:, :slots].reshape(experts * slots, width), held[:, slots:]
        else:
            dz = to_experts(top_grad)
            w_exp_out = exchange(exp_out, "dp", groups)
            w_exp_out = lax.all_gather(w_exp_out, "dp", axis_index_groups=ring)
        w_exp_out = w_exp_out.reshape(n_dp * hid, width)

        xhat1, inv1 = scale_rows(h1)
        c0 = gather_blocks((xhat1 * gains[1] + biases[1]).astype(BF))
        u0, g0, send, keep = mlp(c0, mlp_all)
        h2 = h1 + scatter_blocks(send, keep)

        w_in_far = swap(w_exp_in, 2)
        xhat2, inv2 = scale_rows(h2)
        a1 = gather_blocks(after((xhat2 * gains[2] + biases[2]).astype(BF), w_exp_in))
        qkv1, o1, lse1, send, keep = attend(a1, w_qkv1, w_out1, code_all)
        h3 = h2 + scatter_blocks(send, keep, w_in_far)

        xhat3, inv3 = scale_rows(h3)
        c1 = after((xhat3 * gains[3] + biases[3]).astype(BF), dz, w_exp_out)
        w_out_far = swap(w_exp_out, 2)
        dz = (dz, swap(dz, 1))
        x = after(to_experts(c1), w_out_far)
        x = (x, swap(x, 1))
        dx_send, dx_keep, y_send, y_keep, din_own, din_far, dout_own, dout_far, router_part = expert_compute(
            own_dp % experts, x, dz, (w_exp_in, w_in_far), (w_exp_out, w_out_far), w_router
        )
        dx = (dx_keep + swap(dx_send, 1).astype(F32)).astype(BF)
        y = (y_keep + swap(after(y_send, dx), 1).astype(F32)).astype(BF)
        exp_in_part = (din_own + swap(after(din_far, dx), 2).astype(F32)).astype(BF)
        exp_out_part = (dout_own + swap(after(dout_far, exp_in_part), 2).astype(F32)).astype(BF)
        dx = exchange(dx.reshape(experts, slots, width), "dp", groups)

        if clones == 1:
            back = exp_out_part.reshape(experts, hid, width)
            back = jnp.concatenate([y.reshape(experts, slots, width), back], axis=1)
            in_got = exchange(after(exp_in_part.reshape(n_dp, NF * rows, n_dp * hid), dx), "dp")
            got = exchange(after(back, in_got), "dp")
            y, exp_out_grads = got[:, :slots], got[:, slots:].astype(F32)
        else:
            back = lax.psum_scatter(
                exp_out_part.reshape(clones, experts, hid, width), "dp", axis_index_groups=ring
            )
            exp_out_grads = exchange(back, "dp", groups).astype(F32)
            got = exp_out_grads
            y = exchange(y.reshape(experts, slots, width), "dp", groups)
            held = lax.psum_scatter(
                exp_in_part.reshape(clones, experts, NF, rows, n_dp * hid), "dp", axis_index_groups=ring
            )
            in_got = exchange(held, "dp", groups)
        dc1 = mm_tn(pick, after(dx, exp_in_part).reshape(experts * slots, width))

        def rows_to_owners(grad):
            cols = grad.shape[1]
            got = exchange(grad.astype(BF).reshape(n_all, rows, cols), ALL)
            return got.reshape(n_dp, NF, rows, cols).astype(F32)

        def qkv_layout(total):
            parts = total.reshape(NF, rows, 3, part)
            return jnp.transpose(parts, (1, 2, 0, 3)).reshape(rows, 3 * width)

        def sums(out_grad, xhat):
            return jnp.sum(out_grad * xhat, axis=0), jnp.sum(out_grad, axis=0)

        gain3, bias3 = sums(dc1, xhat3)
        grad = top_grad.astype(F32) + norm_back(dc1, xhat3, inv3, gains[3])

        dy1 = gather_blocks(grad.astype(BF))
        dqkv1, send, keep = attend_back(dy1, w_qkv1, w_out1, qkv1, lse1, code_all)
        da1 = scatter_blocks(after(send, in_got), keep)
        attn_part = [
            mm_tn(jnp.concatenate(a1, axis=0), dqkv1).astype(BF).reshape(n_dp, NF * rows, 3 * part),
            mm_tn(o1, jnp.concatenate(dy1, axis=0)).astype(BF).reshape(n_dp, NF * rows, part),
        ]
        attn_part = jnp.concatenate(attn_part, axis=2)
        gain2, bias2 = sums(da1, xhat2)
        grad = grad + norm_back(da1, xhat2, inv2, gains[2])

        dm = gather_blocks(grad.astype(BF))
        du0, send, keep = mlp_back(dm, after(u0, attn_part), mlp_all)
        dc0 = scatter_blocks(send, keep)
        dense_part = mlp_weights(c0, dm, du0, g0, attn_part)
        dense_sum = lax.psum_scatter(dense_part, "dp")
        gain1, bias1 = sums(dc0, xhat1)
        grad = grad + norm_back(dc0, xhat1, inv1, gains[1])

        dy0 = gather_blocks(after(grad.astype(BF), got))
        dqkv0, send, keep = attend_back([after(dy0[0], dense_part), *dy0[1:]], w_qkv0, w_out0, qkv0, lse0, code_all)
        out_part0 = mm_tn(o0, jnp.concatenate(dy0, axis=0)).astype(BF).reshape(n_dp, rows, width)
        out_got0 = exchange(after(out_part0, got), "dp")
        qkv_part0 = mm_tn(a0, dqkv0)
        h4 = h3 + mm_tn(pick, y.reshape(experts * slots, width))
        activations = h4.astype(BF)
        da0 = scatter_blocks(send, keep)
        xhat0_blocks = xhat0_all.reshape(NF, tokens, width)
        gain0 = bias0 = 0.0
        for k in range(NF):
            block = keep[k // 2] if k % 2 == 0 else send[k // 2].astype(F32)
            block_gain, block_bias = sums(block, xhat0_blocks[k])
            gain0, bias0 = gain0 + block_gain, bias0 + block_bias
        columns = jnp.stack([gain0, gain1, gain2, gain3, bias0, bias1, bias2, bias3], axis=1)
        columns = jnp.concatenate(
            [columns, router_part, jnp.zeros((width, 128 - 8 - experts), F32), qkv_part0], axis=1
        )
        tail = rows_to_owners(after(columns, out_got0))
        total = jnp.sum(tail, axis=0)
        small_grads = jnp.sum(total[:, :, :128], axis=0)
        qkv_grad0 = qkv_layout(total[:, :, 128:])
        dense_sum = after(dense_sum, tail)
        in_got = jnp.swapaxes(after(in_got, dqkv0).reshape(experts, NF, rows, n_dp * hid), 0, 1)
        in_got = deal(in_got).reshape(NF, experts, rows, n_dp, hid)
        exp_in_grads = jnp.transpose(in_got, (1, 2, 3, 0, 4))
        exp_in_grads = exp_in_grads.reshape(experts, rows, n_dp * NF * hid).astype(F32)
        held = jnp.concatenate([dense_sum[:, :width], dense_sum[:, 2 * width : 2 * width + 3 * part]], axis=1)
        held = exchange(held.reshape(NF, rows, -1), "fsdp").astype(F32)
        mlp_in_grads = held[..., :width].reshape(NF, rows, n_dp, hid)
        mlp_in_grads = jnp.transpose(mlp_in_grads, (1, 2, 0, 3)).reshape(rows, n_dp * NF * hid)
        qkv_grad1 = qkv_layout(held[..., width:])
        mlp_out_grads = dense_sum[:, width : 2 * width].astype(F32)
        out_sum1 = dense_sum[:, 2 * width + 3 * part :].reshape(rows, width).astype(F32)
        out_sums = jnp.stack([jnp.sum(out_got0.astype(F32), axis=0), out_sum1])
        proj_grads = lax.ppermute(out_sums, ALL, to_owner)
        xhat0, inv0 = scale_rows(h0)
        grad = grad + norm_back(da0, xhat0, inv0, gains[0])

        norm_grads = small_grads[:, :8].T
        return (
            activations.reshape(patches.shape),
            grad.reshape(patches.shape),
            norm_grads[:4],
            norm_grads[4:7],
            norm_grads[7],
            jnp.stack([qkv_grad0, qkv_grad1]),
            proj_grads,
            mlp_in_grads,
            mlp_out_grads,
            small_grads[:, 8 : 8 + experts],
            exp_in_grads,
            exp_out_grads,
        )

    return shards


def solution(mesh):
    by_row = P("dp", "fsdp", None)
    second = P(None, ("dp", "fsdp"), None)
    first = P(("dp", "fsdp"), None)
    pair = P("dp", "fsdp")
    norm = P(None, ("dp", "fsdp"))
    return jax.shard_map(
        make_shards(mesh.shape["dp"]),
        mesh=mesh,
        in_specs=(
            by_row, pair, pair, by_row, by_row, norm, norm, second, second, first, first, first,
            second, second, by_row,
        ),
        out_specs=(
            by_row, by_row, norm, norm, P(("dp", "fsdp")), second, second, first, first, first,
            second, second,
        ),
        check_vma=False,
    )
```

```python
import functools

import jax
import jax.numpy as jnp
from jax import lax
from jax.experimental import pallas as pl
from jax.experimental.pallas import tpu as pltpu
from jax.sharding import PartitionSpec as P

HEADS = 12
HD = 64
EPSILON = 1e-06
NF = 4
ALL = ("dp", "fsdp")
BF = jnp.bfloat16
F32 = jnp.float32


def mm(left, right):
    return jnp.dot(left, right, preferred_element_type=F32)


def mm_tn(left, right):
    return lax.dot_general(left, right, (((0,), (0,)), ((), ())), preferred_element_type=F32)


def mm_nt(left, right):
    return lax.dot_general(left, right, (((1,), (1,)), ((), ())), preferred_element_type=F32)


def gelu(values):
    return 0.5 * values * (1.0 + lax.erf(values * (0.5**0.5)))


def gelu_slope(values):
    cdf = 0.5 * (1.0 + lax.erf(values * (0.5**0.5)))
    return cdf + values * jnp.exp(-0.5 * values * values) * 0.3989422804014327


def scale_rows(rows):
    centre = jnp.mean(rows, axis=-1, keepdims=True)
    centred = rows - centre
    inv_scale = lax.rsqrt(jnp.mean(centred * centred, axis=-1, keepdims=True) + EPSILON)
    return centred * inv_scale, inv_scale


def norm_back(out_grad, scaled, inv_scale, gain):
    weighted = out_grad * gain
    return inv_scale * (
        weighted
        - jnp.mean(weighted, axis=-1, keepdims=True)
        - scaled * jnp.mean(weighted * scaled, axis=-1, keepdims=True)
    )


def swap(value, bits):
    return lax.ppermute(value, "fsdp", [(i, i ^ bits) for i in range(NF)])


def gather_blocks(block):
    across = swap(block, 2)
    beside = swap(block, 1)
    corner = swap(across, 1)
    return [block, beside, across, corner]


def gather_row(block):
    return jnp.concatenate(gather_blocks(block), axis=0)


def scatter_blocks(send, keep, *others):
    got = swap(send, 1).astype(F32)
    far = (keep[1] + got[1]).astype(BF)
    far = swap(after(far, *others) if others else far, 2).astype(F32)
    return keep[0] + got[0] + far


def scatter_row(partial):
    blocks = partial.reshape((NF, -1) + partial.shape[1:])
    return scatter_blocks(jnp.stack([blocks[1], blocks[3]]).astype(BF), (blocks[0], blocks[2]))


def after(value, *others):
    return lax.optimization_barrier((value,) + others)[0]


def deal(blocks):
    own = lax.axis_index("fsdp")
    got = []
    for k in range(NF):
        block = lax.dynamic_index_in_dim(blocks, own ^ k, 0, keepdims=False)
        got.append(block if k == 0 else swap(block, k))
    odd, far = own % 2 == 1, own >= 2
    got = [jnp.where(odd, got[k ^ 1], got[k]) for k in range(NF)]
    return jnp.stack([jnp.where(far, got[k ^ 2], got[k]) for k in range(NF)])


def exchange(value, axes, groups=None):
    return lax.all_to_all(value, axes, 0, 0, axis_index_groups=groups, tiled=True)


def dot(left, right, left_dim, right_dim):
    dims = (((left_dim,), (right_dim,)), ((), ()))
    return lax.dot_general(left, right, dims, preferred_element_type=F32)


def put_partial(partial, send_ref, keep_ref):
    tall = partial.shape[0] // NF
    for k in range(NF):
        block = partial[k * tall : (k + 1) * tall]
        if k % 2 == 0:
            keep_ref[k // 2] = block
        else:
            send_ref[k // 2] = block.astype(BF)


def partial_shapes(tokens, width):
    tall = tokens // NF
    return (
        jax.ShapeDtypeStruct((NF // 2, tall, width), BF),
        jax.ShapeDtypeStruct((NF // 2, tall, width), F32),
    )


def project_kernel(out_ref, wo_ref, send_ref, keep_ref):
    put_partial(mm(out_ref[...], wo_ref[...]), send_ref, keep_ref)


def attend_kernel(*refs, count, heads, lanes):
    a_refs, (w_ref, col_ref, row_ref) = refs[:count], refs[count : count + 3]
    qkv_ref, out_ref, lse_ref = refs[count + 3 :]
    tall = a_refs[0].shape[0]
    for k in range(count):
        qkv_ref[k * tall : (k + 1) * tall] = mm(a_refs[k][...], w_ref[:, lanes]).astype(BF)
    part = heads * HD
    live = (col_ref[...] % 2).astype(F32)
    for h in range(heads):
        q = qkv_ref[:, h * HD : (h + 1) * HD] * BF(HD**-0.5)
        k = qkv_ref[:, part + h * HD : part + (h + 1) * HD]
        v = qkv_ref[:, 2 * part + h * HD : 2 * part + (h + 1) * HD]
        scores = jnp.where(col_ref[...] == row_ref[...], dot(k, q, 1, 1), -1e30)
        top = jnp.max(scores, axis=0, keepdims=True)
        shifted = jnp.exp(scores - top)
        total = jnp.sum(shifted, axis=0, keepdims=True)
        soft = (shifted * (1.0 / total)).astype(BF)
        out_ref[:, h * HD : (h + 1) * HD] = (dot(soft, v, 0, 0) * live).astype(BF)
        lse_ref[h : h + 1] = top + jnp.log(total)


def attend_back_kernel(*refs, count, heads, lanes):
    dy_refs, (w_ref, wo_ref, qkv_ref, lse_ref, col_ref, row_ref) = refs[:count], refs[count : count + 6]
    dqkv_ref, send_ref, keep_ref, do_ref = refs[count + 6 :]
    tall = dy_refs[0].shape[0]
    part = heads * HD
    for k in range(count):
        live = (col_ref[k * tall : (k + 1) * tall] % 2).astype(F32)
        do_ref[k * tall : (k + 1) * tall] = (dot(dy_refs[k][...], wo_ref[...], 1, 1) * live).astype(BF)
    for h in range(heads):
        q = qkv_ref[:, h * HD : (h + 1) * HD] * BF(HD**-0.5)
        k = qkv_ref[:, part + h * HD : part + (h + 1) * HD]
        v = qkv_ref[:, 2 * part + h * HD : 2 * part + (h + 1) * HD]
        do = do_ref[:, h * HD : (h + 1) * HD]
        soft = jnp.exp(dot(k, q, 1, 1) - lse_ref[h : h + 1])
        soft = jnp.where(col_ref[...] == row_ref[...], soft, 0.0)
        soft_grad = dot(v, do, 1, 1)
        row_dot = jnp.sum(soft * soft_grad, axis=0, keepdims=True)
        score_grad = (soft * (soft_grad - row_dot)).astype(BF)
        dq = dot(score_grad, k, 0, 0) * HD**-0.5
        dqkv_ref[:, h * HD : (h + 1) * HD] = dq.astype(BF)
        dk = dot(score_grad, q, 1, 0)
        dqkv_ref[:, part + h * HD : part + (h + 1) * HD] = dk.astype(BF)
        dv = dot(soft.astype(BF), do, 1, 0)
        dqkv_ref[:, 2 * part + h * HD : 2 * part + (h + 1) * HD] = dv.astype(BF)
    put_partial(dot(dqkv_ref[...], w_ref[:, lanes], 1, 1), send_ref, keep_ref)


def mlp_parts(w_ref):
    groups, rows, width = w_ref.shape
    half = rows // 2
    return w_ref[:, :half].reshape(groups * half, width), w_ref[:, half:].reshape(groups * half, width)


def mlp_kernel(*refs):
    c_refs, (w_ref, u_ref, g_ref, send_ref, keep_ref) = refs[:NF], refs[NF:]
    w_in, w_out = mlp_parts(w_ref)
    for k in range(NF):
        u = mm(c_refs[k][...], w_in)
        u_ref[k] = u
        g = gelu(u).astype(BF)
        g_ref[k] = g
        partial = mm(g, w_out)
        if k % 2 == 0:
            keep_ref[k // 2] = partial
        else:
            send_ref[k // 2] = partial.astype(BF)


def mlp_back_kernel(*refs):
    dm_refs, (u_ref, w_ref, du_ref, send_ref, keep_ref) = refs[:NF], refs[NF:]
    w_in, w_out = mlp_parts(w_ref)
    for k in range(NF):
        du = (dot(dm_refs[k][...], w_out, 1, 1) * gelu_slope(u_ref[k])).astype(BF)
        du_ref[k] = du
        partial = dot(du, w_in, 1, 1)
        if k % 2 == 0:
            keep_ref[k // 2] = partial
        else:
            send_ref[k // 2] = partial.astype(BF)


def mlp_weights_kernel(*refs):
    c_refs, dm_refs = refs[:NF], refs[NF : 2 * NF]
    du_ref, g_ref, rest_ref, out_ref, sum_ref = refs[2 * NF :]
    groups, rows, width = rest_ref.shape
    for step in range(2):
        for k in range(NF):
            if step == 0:
                term = dot(c_refs[k][...], du_ref[k], 0, 0)
            else:
                term = dot(g_ref[k], dm_refs[k][...], 0, 0)
            if k == 0:
                sum_ref[...] = term
            else:
                sum_ref[...] += term
        for d in range(groups):
            out_ref[d, :, step * width : (step + 1) * width] = sum_ref[d * rows : (d + 1) * rows].astype(BF)
    for d in range(groups):
        out_ref[d, :, 2 * width :] = rest_ref[d]


def whole(kernel, outs, args, flops, scratch=()):
    space = pl.BlockSpec(memory_space=pltpu.VMEM)
    return pl.pallas_call(
        kernel,
        out_shape=outs,
        in_specs=[space] * len(args),
        out_specs=jax.tree.map(lambda _: space, outs),
        scratch_shapes=scratch,
        compiler_params=pltpu.CompilerParams(vmem_limit_bytes=48 * 2**20),
        cost_estimate=pl.CostEstimate(flops=flops, bytes_accessed=2**16, transcendentals=0),
    )(*args)


def attend(a_blocks, w_qkv, w_out, code_row):
    w_qkv, lanes = w_qkv
    tokens, width = code_row.shape[0], w_qkv.shape[0]
    heads = HEADS // NF
    part = heads * HD
    outs = (
        jax.ShapeDtypeStruct((tokens, 3 * part), BF),
        jax.ShapeDtypeStruct((tokens, part), BF),
        jax.ShapeDtypeStruct((heads, tokens), F32),
    )
    kernel = functools.partial(attend_kernel, count=len(a_blocks), heads=heads, lanes=lanes)
    args = (*a_blocks, w_qkv, code_row[:, None], code_row[None])
    qkv, out, lse = whole(kernel, outs, args, 4 * 10**8)
    send, keep = whole(project_kernel, partial_shapes(tokens, width), (out, w_out), 10**8)
    return qkv, out, lse, send, keep


def attend_back(dy_blocks, w_qkv, w_out, qkv, lse, code_row):
    w_qkv, lanes = w_qkv
    tokens, width = code_row.shape[0], w_qkv.shape[0]
    heads = HEADS // NF
    outs = (jax.ShapeDtypeStruct(qkv.shape, BF),) + partial_shapes(tokens, width)
    kernel = functools.partial(attend_back_kernel, count=len(dy_blocks), heads=heads, lanes=lanes)
    args = (*dy_blocks, w_qkv, w_out, qkv, lse, code_row[:, None], code_row[None])
    return whole(kernel, outs, args, 11 * 10**9, (pltpu.VMEM((tokens, heads * HD), BF),))


def mlp(c_blocks, weights):
    tall, width = c_blocks[0].shape
    hidden = weights.shape[0] * weights.shape[1] // 2
    outs = (
        jax.ShapeDtypeStruct((NF, tall, hidden), F32),
        jax.ShapeDtypeStruct((NF, tall, hidden), BF),
    ) + partial_shapes(NF * tall, width)
    return whole(mlp_kernel, outs, (*c_blocks, weights), 3 * 10**8)


def mlp_back(dm_blocks, u, weights):
    tall, width = dm_blocks[0].shape
    outs = (jax.ShapeDtypeStruct(u.shape, BF),) + partial_shapes(NF * tall, width)
    return whole(mlp_back_kernel, outs, (*dm_blocks, u, weights), 10**8)


def mlp_weights(c_blocks, dm_blocks, du, g, rest):
    groups, rows, width = rest.shape
    if rows % 16 == 0:
        outs = jax.ShapeDtypeStruct((groups, rows, 3 * width), BF)
        args = (*c_blocks, *dm_blocks, du, g, rest)
        return whole(mlp_weights_kernel, outs, args, 10**8, (pltpu.VMEM((width, width), F32),))
    parts = [mm_tn(jnp.concatenate(c_blocks, axis=0), du.reshape(-1, width))]
    parts.append(mm_tn(g.reshape(-1, width), jnp.concatenate(dm_blocks, axis=0)))
    parts = [value.astype(BF).reshape(groups, rows, width) for value in parts]
    return jnp.concatenate(parts + [rest], axis=2)


def expert_gate(own, x, router):
    logits = mm(x, router)
    lane = lax.broadcasted_iota(jnp.int32, logits.shape, 1)
    shifted = jnp.exp(logits - jnp.max(logits, axis=1, keepdims=True))
    probs = shifted / jnp.sum(shifted, axis=1, keepdims=True)
    mine = (lane == own).astype(F32)
    return probs, mine, jnp.sum(probs * mine, axis=1, keepdims=True)


def expert_quarter(x, dyx, w_in, w_out):
    ue = mm(x, w_in)
    cdf = 0.5 * (1.0 + lax.erf(ue * (0.5**0.5)))
    slope = cdf + ue * jnp.exp(-0.5 * ue * ue) * 0.3989422804014327
    ge = (ue * cdf).astype(BF)
    due = (dot(dyx, w_out, 1, 1) * slope).astype(BF)
    return mm(ge, w_out), dot(due, w_in, 1, 1), dot(x, due, 0, 0), dot(ge, dyx, 0, 0)


def expert_near_kernel(own_ref, x0, x1, dz0, dz1, in_ref, out_ref, router_ref, y_ref, dx_ref, din_ref, dout_ref):
    for i, (x_ref, dz_ref) in enumerate(((x0, dz0), (x1, dz1))):
        x = x_ref[...]
        gate = expert_gate(own_ref[0], x, router_ref[...])[2].astype(BF).astype(F32)
        dyx = (gate * dz_ref[...].astype(F32)).astype(BF)
        y_ref[i], dx_ref[i], din, dout = expert_quarter(x, dyx, in_ref[...], out_ref[...])
        if i == 0:
            din_ref[...], dout_ref[...] = din, dout
        else:
            din_ref[...] += din
            dout_ref[...] += dout


def expert_far_kernel(*refs):
    own_ref, x_refs, dz_refs, (in_ref, out_ref, router_ref, y_ref, dx_ref) = refs[0], refs[1:3], refs[3:5], refs[5:10]
    dx_send, dx_keep, y_send, y_keep, din_ref, dout_ref, drouter_ref, din_sum, dout_sum = refs[10:]
    router = router_ref[...]
    for i in range(2):
        x, dz = x_refs[i][...], dz_refs[i][...].astype(F32)
        probs, mine, prob = expert_gate(own_ref[0], x, router)
        gate = prob.astype(BF).astype(F32)
        y, dx, din, dout = expert_quarter(x, (gate * dz).astype(BF), in_ref[...], out_ref[...])
        y, dx = y + y_ref[i], dx + dx_ref[i]
        dgate = jnp.sum(dz * y, axis=1, keepdims=True)
        dlogits = (dgate * prob * (mine - probs)).astype(BF)
        dx = dx + dot(dlogits, router, 1, 1)
        y = gate * y
        if i == 0:
            din_sum[...], dout_sum[...], drouter_ref[...] = din, dout, dot(x, dlogits, 0, 0)
            dx_keep[...], y_keep[...] = dx, y
        else:
            din_sum[...] += din
            dout_sum[...] += dout
            drouter_ref[...] += dot(x, dlogits, 0, 0)
            dx_send[...], y_send[...] = dx.astype(BF), y.astype(BF)
    din_ref[...], dout_ref[...] = din_sum[...].astype(BF), dout_sum[...].astype(BF)


def expert_call(kernel, outs, own, args, flops, scratch=()):
    space = pl.BlockSpec(memory_space=pltpu.VMEM)
    return pl.pallas_call(
        kernel,
        out_shape=outs,
        in_specs=[pl.BlockSpec(memory_space=pltpu.SMEM)] + [space] * len(args),
        out_specs=(space,) * len(outs),
        scratch_shapes=scratch,
        compiler_params=pltpu.CompilerParams(vmem_limit_bytes=56 * 2**20),
        cost_estimate=pl.CostEstimate(flops=flops, bytes_accessed=2**20, transcendentals=0),
    )(own.astype(jnp.int32)[None], *args)


def expert_compute(own, x_blocks, dz_blocks, w_in, w_out, router):
    tall, width = x_blocks[0].shape
    square = w_in[0].shape
    send, keep = jax.ShapeDtypeStruct((tall, width), BF), jax.ShapeDtypeStruct((tall, width), F32)
    near, far = jax.ShapeDtypeStruct(square, F32), jax.ShapeDtypeStruct(square, BF)
    both = jax.ShapeDtypeStruct((2, tall, width), F32)
    flops = 24 * tall * width * square[1]
    args = (*x_blocks, *dz_blocks, w_in[0], w_out[0], router)
    y, dx, din_own, dout_own = expert_call(expert_near_kernel, (both, both, near, near), own, args, 10**7)
    args = (*x_blocks, *dz_blocks, w_in[1], w_out[1], router, y, dx)
    outs = (send, keep, send, keep, far, far, jax.ShapeDtypeStruct(router.shape, F32))
    scratch = (pltpu.VMEM(square, F32), pltpu.VMEM(square, F32))
    got = expert_call(expert_far_kernel, outs, own, args, flops, scratch)
    dx_send, dx_keep, y_send, y_keep, din_far, dout_far, drouter = got
    return dx_send, dx_keep, y_send, y_keep, din_own, din_far, dout_own, dout_far, drouter


def make_shards(n_dp):
    n_all = n_dp * NF

    def shards(
        patches, segment_ids, live, expert_ids, ranks, norm_gains, norm_biases, attn_qkv, attn_out,
        mlp_in, mlp_out, router, exp_in, exp_out, cotangent,
    ):
        width = patches.shape[-1]
        tokens = patches.shape[0] * patches.shape[1]
        experts = exp_in.shape[0]
        clones = n_dp // experts
        part = width // NF
        rows = attn_qkv.shape[1]
        hid = mlp_out.shape[0]
        own_f = lax.axis_index("fsdp")
        own_dp = lax.axis_index("dp")
        groups = ring = None
        if clones > 1:
            groups = [[g * experts + e for e in range(experts)] for g in range(clones)]
            ring = [[g * experts + e for g in range(clones)] for e in range(experts)]
        capacity = (210 * tokens + 100 * experts - 1) // (100 * experts)
        slots = (capacity + 7) // 8 * 8

        code = (segment_ids * 2 + live).reshape(tokens)
        code_all = gather_row(code)
        live_all = (code_all % 2).astype(F32)
        rows_all = gather_row(patches.reshape(tokens, width))

        def qkv_block(layer):
            weight = attn_qkv[layer].reshape(rows, 3, NF, part)
            return jnp.transpose(weight, (2, 0, 1, 3)).reshape(NF, rows, 3 * part)

        small = jnp.concatenate(
            [norm_gains.T, norm_biases.T, router, jnp.zeros((rows, 128 - 8 - experts), BF)], axis=1
        )
        small = jnp.broadcast_to(small[None], (NF, rows, 128))
        def to_everyone(blocks):
            full = jnp.broadcast_to(blocks[None], (n_dp,) + blocks.shape)
            return exchange(full.reshape((n_all, rows, -1)), ALL).reshape(width, -1)

        first = to_everyone(jnp.concatenate([small, qkv_block(0)], axis=2))
        small_all, w_qkv0 = first[:, :128], (first, slice(128, 128 + 3 * part))
        norms = small_all[:, :8].T.astype(F32)
        gains, biases = norms[:4], norms[4:]
        w_router = small_all[:, 8 : 8 + experts]

        mlp_block = jnp.transpose(mlp_in.reshape(rows, n_dp, NF, hid), (2, 0, 1, 3))
        mlp_block = deal(mlp_block.reshape(NF, rows, n_dp * hid)).reshape(NF * rows, width)
        mlp_all = lax.all_gather(jnp.concatenate([mlp_block, mlp_out], axis=0), "dp")

        to_heads = [(j, j % n_dp * NF + j // n_dp) for j in range(n_all)]
        to_owner = [(b, a) for a, b in to_heads]
        held_out = lax.ppermute(attn_out, ALL, to_heads)
        held = after(held_out[0], first)
        w_out0 = exchange(jnp.broadcast_to(held[None], (n_dp, rows, width)), "dp").reshape(part, width)

        choice = expert_ids.reshape(tokens, 2)
        rank = ranks.reshape(tokens, 2)
        place = jnp.where(rank < capacity, choice * slots + rank, -1)
        slot_index = jnp.arange(experts * slots, dtype=jnp.int32)[:, None]
        pick = (place[:, 0][None] == slot_index) | (place[:, 1][None] == slot_index)
        pick = pick.astype(BF)

        def to_experts(block):
            held = mm(pick, block).astype(BF).reshape(experts, slots, width)
            return exchange(held, "dp", groups).reshape(experts * slots, width)

        top_grad = cotangent.reshape(tokens, width)
        in_block = jnp.transpose(exp_in.reshape(experts, rows, n_dp, NF, hid), (3, 0, 1, 2, 4))
        in_block = in_block.reshape(NF, experts, rows, n_dp * hid)
        if clones == 1:
            in_block = jnp.swapaxes(deal(in_block), 0, 1).reshape(experts, NF * rows, n_dp * hid)
            held = deal(qkv_block(1)).reshape(NF * rows, 3 * part)
            held = jnp.concatenate([held, held_out[1].reshape(NF * rows, part)], axis=1)
            held = jnp.broadcast_to(held[None], (n_dp,) + held.shape)
            in_block = jnp.concatenate([in_block, held], axis=2)

        h0 = patches.reshape(tokens, width).astype(F32)
        xhat0_all, _ = scale_rows(rows_all.astype(F32))
        a0 = (xhat0_all * gains[0] + biases[0]).astype(BF)
        qkv0, o0, lse0, send, keep = attend([a0], w_qkv0, w_out0, code_all)
        h1 = h0 + scatter_blocks(after(send, in_block) if clones == 1 else send, keep)

        if clones == 1:
            held = exchange(after(in_block, w_out0), "dp").reshape(width, -1)
            cut = n_dp * hid
            w_exp_in, w_qkv1 = held[:, :cut], (held, slice(cut, cut + 3 * part))
            w_out1 = held[:, cut + 3 * part :].reshape(part, width)
        else:
            held = exchange(in_block, "fsdp")
            held = exchange(jnp.swapaxes(held, 0, 1), "dp", groups)
            w_exp_in = lax.all_gather(held, "dp", axis_index_groups=ring).reshape(width, n_dp * hid)
            w_qkv1 = (to_everyone(qkv_block(1)), slice(0, 3 * part))
            w_out1 = lax.all_gather(held_out[1], "dp").reshape(part, width)
        if clones == 1:
            dz = mm(pick, top_grad).astype(BF).reshape(experts, slots, width)
            held = exchange(after(jnp.concatenate([dz, exp_out], axis=1), w_exp_in), "dp")
            dz, w_exp_out = held[:, :slots].reshape(experts * slots, width), held[:, slots:]
        else:
            dz = to_experts(top_grad)
            w_exp_out = exchange(exp_out, "dp", groups)
            w_exp_out = lax.all_gather(w_exp_out, "dp", axis_index_groups=ring)
        w_exp_out = w_exp_out.reshape(n_dp * hid, width)

        xhat1, inv1 = scale_rows(h1)
        c0 = gather_blocks((xhat1 * gains[1] + biases[1]).astype(BF))
        u0, g0, send, keep = mlp(c0, mlp_all)
        h2 = h1 + scatter_blocks(send, keep)

        w_in_far = swap(w_exp_in, 2)
        xhat2, inv2 = scale_rows(h2)
        a1 = gather_blocks(after((xhat2 * gains[2] + biases[2]).astype(BF), w_exp_in))
        qkv1, o1, lse1, send, keep = attend(a1, w_qkv1, w_out1, code_all)
        h3 = h2 + scatter_blocks(send, keep, w_in_far)

        xhat3, inv3 = scale_rows(h3)
        c1 = after((xhat3 * gains[3] + biases[3]).astype(BF), dz, w_exp_out)
        w_out_far = swap(w_exp_out, 2)
        dz = (dz, swap(dz, 1))
        x = to_experts(c1)
        x = (x, swap(x, 1))
        dx_send, dx_keep, y_send, y_keep, din_own, din_far, dout_own, dout_far, router_part = expert_compute(
            own_dp % experts, x, dz, (w_exp_in, w_in_far), (w_exp_out, w_out_far), w_router
        )
        dx = (dx_keep + swap(dx_send, 1).astype(F32)).astype(BF)
        y = (y_keep + swap(after(y_send, dx), 1).astype(F32)).astype(BF)
        exp_in_part = (din_own + swap(after(din_far, dx), 2).astype(F32)).astype(BF)
        exp_out_part = (dout_own + swap(after(dout_far, exp_in_part), 2).astype(F32)).astype(BF)
        dx = exchange(dx.reshape(experts, slots, width), "dp", groups)

        if clones == 1:
            back = exp_out_part.reshape(experts, hid, width)
            back = jnp.concatenate([y.reshape(experts, slots, width), back], axis=1)
            in_got = exchange(after(exp_in_part.reshape(n_dp, NF * rows, n_dp * hid), dx), "dp")
            got = exchange(after(back, in_got), "dp")
            y, exp_out_grads = got[:, :slots], got[:, slots:].astype(F32)
        else:
            back = lax.psum_scatter(
                exp_out_part.reshape(clones, experts, hid, width), "dp", axis_index_groups=ring
            )
            exp_out_grads = exchange(back, "dp", groups).astype(F32)
            got = exp_out_grads
            y = exchange(y.reshape(experts, slots, width), "dp", groups)
            held = lax.psum_scatter(
                exp_in_part.reshape(clones, experts, NF, rows, n_dp * hid), "dp", axis_index_groups=ring
            )
            in_got = exchange(held, "dp", groups)
        dc1 = mm_tn(pick, after(dx, exp_in_part).reshape(experts * slots, width))

        def rows_to_owners(grad):
            cols = grad.shape[1]
            got = exchange(grad.astype(BF).reshape(n_all, rows, cols), ALL)
            return got.reshape(n_dp, NF, rows, cols).astype(F32)

        def qkv_layout(total):
            parts = total.reshape(NF, rows, 3, part)
            return jnp.transpose(parts, (1, 2, 0, 3)).reshape(rows, 3 * width)

        def sums(out_grad, xhat):
            return jnp.sum(out_grad * xhat, axis=0), jnp.sum(out_grad, axis=0)

        gain3, bias3 = sums(dc1, xhat3)
        grad = top_grad.astype(F32) + norm_back(dc1, xhat3, inv3, gains[3])

        dy1 = gather_blocks(grad.astype(BF))
        dqkv1, send, keep = attend_back(dy1, w_qkv1, w_out1, qkv1, lse1, code_all)
        da1 = scatter_blocks(after(send, in_got), keep)
        attn_part = [
            mm_tn(jnp.concatenate(a1, axis=0), dqkv1).astype(BF).reshape(n_dp, NF * rows, 3 * part),
            mm_tn(o1, jnp.concatenate(dy1, axis=0)).astype(BF).reshape(n_dp, NF * rows, part),
        ]
        attn_part = jnp.concatenate(attn_part, axis=2)
        gain2, bias2 = sums(da1, xhat2)
        grad = grad + norm_back(da1, xhat2, inv2, gains[2])

        dm = gather_blocks(grad.astype(BF))
        du0, send, keep = mlp_back(dm, after(u0, attn_part), mlp_all)
        dc0 = scatter_blocks(send, keep)
        dense_part = mlp_weights(c0, dm, du0, g0, attn_part)
        dense_sum = lax.psum_scatter(dense_part, "dp")
        gain1, bias1 = sums(dc0, xhat1)
        grad = grad + norm_back(dc0, xhat1, inv1, gains[1])

        dy0 = gather_blocks(after(grad.astype(BF), got))
        dqkv0, send, keep = attend_back([after(dy0[0], dense_part), *dy0[1:]], w_qkv0, w_out0, qkv0, lse0, code_all)
        out_part0 = mm_tn(o0, jnp.concatenate(dy0, axis=0)).astype(BF).reshape(n_dp, rows, width)
        out_got0 = exchange(after(out_part0, got), "dp")
        qkv_part0 = mm_tn(a0, dqkv0)
        h4 = h3 + mm_tn(pick, y.reshape(experts * slots, width))
        activations = h4.astype(BF)
        da0 = scatter_blocks(send, keep)
        xhat0_blocks = xhat0_all.reshape(NF, tokens, width)
        gain0 = bias0 = 0.0
        for k in range(NF):
            block = keep[k // 2] if k % 2 == 0 else send[k // 2].astype(F32)
            block_gain, block_bias = sums(block, xhat0_blocks[k])
            gain0, bias0 = gain0 + block_gain, bias0 + block_bias
        columns = jnp.stack([gain0, gain1, gain2, gain3, bias0, bias1, bias2, bias3], axis=1)
        columns = jnp.concatenate(
            [columns, router_part, jnp.zeros((width, 128 - 8 - experts), F32), qkv_part0], axis=1
        )
        tail = rows_to_owners(after(columns, out_got0))
        total = jnp.sum(tail, axis=0)
        small_grads = jnp.sum(total[:, :, :128], axis=0)
        qkv_grad0 = qkv_layout(total[:, :, 128:])
        dense_sum = after(dense_sum, tail)
        in_got = jnp.swapaxes(after(in_got, dqkv0).reshape(experts, NF, rows, n_dp * hid), 0, 1)
        in_got = deal(in_got).reshape(NF, experts, rows, n_dp, hid)
        exp_in_grads = jnp.transpose(in_got, (1, 2, 3, 0, 4))
        exp_in_grads = exp_in_grads.reshape(experts, rows, n_dp * NF * hid).astype(F32)
        held = jnp.concatenate([dense_sum[:, :width], dense_sum[:, 2 * width : 2 * width + 3 * part]], axis=1)
        held = deal(held.reshape(NF, rows, -1)).astype(F32)
        mlp_in_grads = held[..., :width].reshape(NF, rows, n_dp, hid)
        mlp_in_grads = jnp.transpose(mlp_in_grads, (1, 2, 0, 3)).reshape(rows, n_dp * NF * hid)
        qkv_grad1 = qkv_layout(held[..., width:])
        mlp_out_grads = dense_sum[:, width : 2 * width].astype(F32)
        out_sum1 = dense_sum[:, 2 * width + 3 * part :].reshape(rows, width).astype(F32)
        out_sums = jnp.stack([jnp.sum(out_got0.astype(F32), axis=0), out_sum1])
        proj_grads = lax.ppermute(out_sums, ALL, to_owner)
        xhat0, inv0 = scale_rows(h0)
        grad = grad + norm_back(da0, xhat0, inv0, gains[0])

        norm_grads = small_grads[:, :8].T
        return (
            activations.reshape(patches.shape),
            grad.reshape(patches.shape),
            norm_grads[:4],
            norm_grads[4:7],
            norm_grads[7],
            jnp.stack([qkv_grad0, qkv_grad1]),
            proj_grads,
            mlp_in_grads,
            mlp_out_grads,
            small_grads[:, 8 : 8 + experts],
            exp_in_grads,
            exp_out_grads,
        )

    return shards


def solution(mesh):
    by_row = P("dp", "fsdp", None)
    second = P(None, ("dp", "fsdp"), None)
    first = P(("dp", "fsdp"), None)
    pair = P("dp", "fsdp")
    norm = P(None, ("dp", "fsdp"))
    return jax.shard_map(
        make_shards(mesh.shape["dp"]),
        mesh=mesh,
        in_specs=(
            by_row, pair, pair, by_row, by_row, norm, norm, second, second, first, first, first,
            second, second, by_row,
        ),
        out_specs=(
            by_row, by_row, norm, norm, P(("dp", "fsdp")), second, second, first, first, first,
            second, second,
        ),
        check_vma=False,
    )
```

```python
import functools

import jax
import jax.numpy as jnp
from jax import lax
from jax.experimental import pallas as pl
from jax.experimental.pallas import tpu as pltpu
from jax.sharding import PartitionSpec as P

HEADS = 12
HD = 64
EPSILON = 1e-06
NF = 4
ALL = ("dp", "fsdp")
BF = jnp.bfloat16
F32 = jnp.float32


def mm(left, right):
    return jnp.dot(left, right, preferred_element_type=F32)


def mm_tn(left, right):
    return lax.dot_general(left, right, (((0,), (0,)), ((), ())), preferred_element_type=F32)


def mm_nt(left, right):
    return lax.dot_general(left, right, (((1,), (1,)), ((), ())), preferred_element_type=F32)


def gelu(values):
    return 0.5 * values * (1.0 + lax.erf(values * (0.5**0.5)))


def gelu_slope(values):
    cdf = 0.5 * (1.0 + lax.erf(values * (0.5**0.5)))
    return cdf + values * jnp.exp(-0.5 * values * values) * 0.3989422804014327


def scale_rows(rows):
    centre = jnp.mean(rows, axis=-1, keepdims=True)
    centred = rows - centre
    inv_scale = lax.rsqrt(jnp.mean(centred * centred, axis=-1, keepdims=True) + EPSILON)
    return centred * inv_scale, inv_scale


def norm_back(out_grad, scaled, inv_scale, gain):
    weighted = out_grad * gain
    return inv_scale * (
        weighted
        - jnp.mean(weighted, axis=-1, keepdims=True)
        - scaled * jnp.mean(weighted * scaled, axis=-1, keepdims=True)
    )


def swap(value, bits):
    return lax.ppermute(value, "fsdp", [(i, i ^ bits) for i in range(NF)])


def gather_blocks(block):
    across = swap(block, 2)
    beside = swap(block, 1)
    corner = swap(across, 1)
    return [block, beside, across, corner]


def gather_row(block):
    return jnp.concatenate(gather_blocks(block), axis=0)


def scatter_blocks(send, keep, *others):
    got = swap(send, 1).astype(F32)
    far = (keep[1] + got[1]).astype(BF)
    far = swap(after(far, *others) if others else far, 2).astype(F32)
    return keep[0] + got[0] + far


def scatter_row(partial):
    blocks = partial.reshape((NF, -1) + partial.shape[1:])
    return scatter_blocks(jnp.stack([blocks[1], blocks[3]]).astype(BF), (blocks[0], blocks[2]))


def after(value, *others):
    return lax.optimization_barrier((value,) + others)[0]


def deal(blocks):
    own = lax.axis_index("fsdp")
    got = []
    for k in range(NF):
        block = lax.dynamic_index_in_dim(blocks, own ^ k, 0, keepdims=False)
        got.append(block if k == 0 else swap(block, k))
    odd, far = own % 2 == 1, own >= 2
    got = [jnp.where(odd, got[k ^ 1], got[k]) for k in range(NF)]
    return jnp.stack([jnp.where(far, got[k ^ 2], got[k]) for k in range(NF)])


def exchange(value, axes, groups=None):
    return lax.all_to_all(value, axes, 0, 0, axis_index_groups=groups, tiled=True)


def dot(left, right, left_dim, right_dim):
    dims = (((left_dim,), (right_dim,)), ((), ()))
    return lax.dot_general(left, right, dims, preferred_element_type=F32)


def put_partial(partial, send_ref, keep_ref):
    tall = partial.shape[0] // NF
    for k in range(NF):
        block = partial[k * tall : (k + 1) * tall]
        if k % 2 == 0:
            keep_ref[k // 2] = block
        else:
            send_ref[k // 2] = block.astype(BF)


def partial_shapes(tokens, width):
    tall = tokens // NF
    return (
        jax.ShapeDtypeStruct((NF // 2, tall, width), BF),
        jax.ShapeDtypeStruct((NF // 2, tall, width), F32),
    )


def project_kernel(out_ref, wo_ref, send_ref, keep_ref):
    put_partial(mm(out_ref[...], wo_ref[...]), send_ref, keep_ref)


def attend_kernel(*refs, count, heads, lanes):
    a_refs, (w_ref, col_ref, row_ref) = refs[:count], refs[count : count + 3]
    qkv_ref, out_ref, lse_ref = refs[count + 3 :]
    tall = a_refs[0].shape[0]
    for k in range(count):
        qkv_ref[k * tall : (k + 1) * tall] = mm(a_refs[k][...], w_ref[:, lanes]).astype(BF)
    part = heads * HD
    live = (col_ref[...] % 2).astype(F32)
    for h in range(heads):
        q = qkv_ref[:, h * HD : (h + 1) * HD] * BF(HD**-0.5)
        k = qkv_ref[:, part + h * HD : part + (h + 1) * HD]
        v = qkv_ref[:, 2 * part + h * HD : 2 * part + (h + 1) * HD]
        scores = jnp.where(col_ref[...] == row_ref[...], dot(k, q, 1, 1), -1e30)
        top = jnp.max(scores, axis=0, keepdims=True)
        shifted = jnp.exp(scores - top)
        total = jnp.sum(shifted, axis=0, keepdims=True)
        soft = (shifted * (1.0 / total)).astype(BF)
        out_ref[:, h * HD : (h + 1) * HD] = (dot(soft, v, 0, 0) * live).astype(BF)
        lse_ref[h : h + 1] = top + jnp.log(total)


def attend_back_kernel(*refs, count, heads, lanes):
    dy_refs, (w_ref, wo_ref, qkv_ref, lse_ref, col_ref, row_ref) = refs[:count], refs[count : count + 6]
    dqkv_ref, send_ref, keep_ref, do_ref = refs[count + 6 :]
    tall = dy_refs[0].shape[0]
    part = heads * HD
    for k in range(count):
        live = (col_ref[k * tall : (k + 1) * tall] % 2).astype(F32)
        do_ref[k * tall : (k + 1) * tall] = (dot(dy_refs[k][...], wo_ref[...], 1, 1) * live).astype(BF)
    for h in range(heads):
        q = qkv_ref[:, h * HD : (h + 1) * HD] * BF(HD**-0.5)
        k = qkv_ref[:, part + h * HD : part + (h + 1) * HD]
        v = qkv_ref[:, 2 * part + h * HD : 2 * part + (h + 1) * HD]
        do = do_ref[:, h * HD : (h + 1) * HD]
        soft = jnp.exp(dot(k, q, 1, 1) - lse_ref[h : h + 1])
        soft = jnp.where(col_ref[...] == row_ref[...], soft, 0.0)
        soft_grad = dot(v, do, 1, 1)
        row_dot = jnp.sum(soft * soft_grad, axis=0, keepdims=True)
        score_grad = (soft * (soft_grad - row_dot)).astype(BF)
        dq = dot(score_grad, k, 0, 0) * HD**-0.5
        dqkv_ref[:, h * HD : (h + 1) * HD] = dq.astype(BF)
        dk = dot(score_grad, q, 1, 0)
        dqkv_ref[:, part + h * HD : part + (h + 1) * HD] = dk.astype(BF)
        dv = dot(soft.astype(BF), do, 1, 0)
        dqkv_ref[:, 2 * part + h * HD : 2 * part + (h + 1) * HD] = dv.astype(BF)
    put_partial(dot(dqkv_ref[...], w_ref[:, lanes], 1, 1), send_ref, keep_ref)


def mlp_parts(w_ref):
    groups, rows, width = w_ref.shape
    half = rows // 2
    return w_ref[:, :half].reshape(groups * half, width), w_ref[:, half:].reshape(groups * half, width)


def mlp_kernel(*refs):
    c_refs, (w_ref, u_ref, g_ref, send_ref, keep_ref) = refs[:NF], refs[NF:]
    w_in, w_out = mlp_parts(w_ref)
    for k in range(NF):
        u = mm(c_refs[k][...], w_in)
        u_ref[k] = u
        g = gelu(u).astype(BF)
        g_ref[k] = g
        partial = mm(g, w_out)
        if k % 2 == 0:
            keep_ref[k // 2] = partial
        else:
            send_ref[k // 2] = partial.astype(BF)


def mlp_back_kernel(*refs):
    dm_refs, (u_ref, w_ref, du_ref, send_ref, keep_ref) = refs[:NF], refs[NF:]
    w_in, w_out = mlp_parts(w_ref)
    for k in range(NF):
        du = (dot(dm_refs[k][...], w_out, 1, 1) * gelu_slope(u_ref[k])).astype(BF)
        du_ref[k] = du
        partial = dot(du, w_in, 1, 1)
        if k % 2 == 0:
            keep_ref[k // 2] = partial
        else:
            send_ref[k // 2] = partial.astype(BF)


def mlp_weights_kernel(*refs):
    c_refs, dm_refs = refs[:NF], refs[NF : 2 * NF]
    du_ref, g_ref, rest_ref, out_ref, sum_ref = refs[2 * NF :]
    groups, rows, width = rest_ref.shape
    for step in range(2):
        for k in range(NF):
            if step == 0:
                term = dot(c_refs[k][...], du_ref[k], 0, 0)
            else:
                term = dot(g_ref[k], dm_refs[k][...], 0, 0)
            if k == 0:
                sum_ref[...] = term
            else:
                sum_ref[...] += term
        for d in range(groups):
            out_ref[d, :, step * width : (step + 1) * width] = sum_ref[d * rows : (d + 1) * rows].astype(BF)
    for d in range(groups):
        out_ref[d, :, 2 * width :] = rest_ref[d]


def whole(kernel, outs, args, flops, scratch=()):
    space = pl.BlockSpec(memory_space=pltpu.VMEM)
    return pl.pallas_call(
        kernel,
        out_shape=outs,
        in_specs=[space] * len(args),
        out_specs=jax.tree.map(lambda _: space, outs),
        scratch_shapes=scratch,
        compiler_params=pltpu.CompilerParams(vmem_limit_bytes=48 * 2**20),
        cost_estimate=pl.CostEstimate(flops=flops, bytes_accessed=2**16, transcendentals=0),
    )(*args)


def attend(a_blocks, w_qkv, w_out, code_row):
    w_qkv, lanes = w_qkv
    tokens, width = code_row.shape[0], w_qkv.shape[0]
    heads = HEADS // NF
    part = heads * HD
    outs = (
        jax.ShapeDtypeStruct((tokens, 3 * part), BF),
        jax.ShapeDtypeStruct((tokens, part), BF),
        jax.ShapeDtypeStruct((heads, tokens), F32),
    )
    kernel = functools.partial(attend_kernel, count=len(a_blocks), heads=heads, lanes=lanes)
    args = (*a_blocks, w_qkv, code_row[:, None], code_row[None])
    qkv, out, lse = whole(kernel, outs, args, 4 * 10**8)
    send, keep = whole(project_kernel, partial_shapes(tokens, width), (out, w_out), 10**8)
    return qkv, out, lse, send, keep


def attend_back(dy_blocks, w_qkv, w_out, qkv, lse, code_row):
    w_qkv, lanes = w_qkv
    tokens, width = code_row.shape[0], w_qkv.shape[0]
    heads = HEADS // NF
    outs = (jax.ShapeDtypeStruct(qkv.shape, BF),) + partial_shapes(tokens, width)
    kernel = functools.partial(attend_back_kernel, count=len(dy_blocks), heads=heads, lanes=lanes)
    args = (*dy_blocks, w_qkv, w_out, qkv, lse, code_row[:, None], code_row[None])
    return whole(kernel, outs, args, 11 * 10**9, (pltpu.VMEM((tokens, heads * HD), BF),))


def mlp(c_blocks, weights):
    tall, width = c_blocks[0].shape
    hidden = weights.shape[0] * weights.shape[1] // 2
    outs = (
        jax.ShapeDtypeStruct((NF, tall, hidden), F32),
        jax.ShapeDtypeStruct((NF, tall, hidden), BF),
    ) + partial_shapes(NF * tall, width)
    return whole(mlp_kernel, outs, (*c_blocks, weights), 3 * 10**8)


def mlp_back(dm_blocks, u, weights):
    tall, width = dm_blocks[0].shape
    outs = (jax.ShapeDtypeStruct(u.shape, BF),) + partial_shapes(NF * tall, width)
    return whole(mlp_back_kernel, outs, (*dm_blocks, u, weights), 10**8)


def mlp_weights(c_blocks, dm_blocks, du, g, rest):
    groups, rows, width = rest.shape
    if rows % 16 == 0:
        outs = jax.ShapeDtypeStruct((groups, rows, 3 * width), BF)
        args = (*c_blocks, *dm_blocks, du, g, rest)
        return whole(mlp_weights_kernel, outs, args, 10**8, (pltpu.VMEM((width, width), F32),))
    parts = [mm_tn(jnp.concatenate(c_blocks, axis=0), du.reshape(-1, width))]
    parts.append(mm_tn(g.reshape(-1, width), jnp.concatenate(dm_blocks, axis=0)))
    parts = [value.astype(BF).reshape(groups, rows, width) for value in parts]
    return jnp.concatenate(parts + [rest], axis=2)


def expert_gate(own, x, router):
    logits = mm(x, router)
    lane = lax.broadcasted_iota(jnp.int32, logits.shape, 1)
    shifted = jnp.exp(logits - jnp.max(logits, axis=1, keepdims=True))
    probs = shifted / jnp.sum(shifted, axis=1, keepdims=True)
    mine = (lane == own).astype(F32)
    return probs, mine, jnp.sum(probs * mine, axis=1, keepdims=True)


def expert_quarter(x, dyx, w_in, w_out):
    ue = mm(x, w_in)
    cdf = 0.5 * (1.0 + lax.erf(ue * (0.5**0.5)))
    slope = cdf + ue * jnp.exp(-0.5 * ue * ue) * 0.3989422804014327
    ge = (ue * cdf).astype(BF)
    due = (dot(dyx, w_out, 1, 1) * slope).astype(BF)
    return mm(ge, w_out), dot(due, w_in, 1, 1), dot(x, due, 0, 0), dot(ge, dyx, 0, 0)


def expert_near_kernel(own_ref, x0, x1, dz0, dz1, in_ref, out_ref, router_ref, y_ref, dx_ref, din_ref, dout_ref):
    for i, (x_ref, dz_ref) in enumerate(((x0, dz0), (x1, dz1))):
        x = x_ref[...]
        gate = expert_gate(own_ref[0], x, router_ref[...])[2].astype(BF).astype(F32)
        dyx = (gate * dz_ref[...].astype(F32)).astype(BF)
        y_ref[i], dx_ref[i], din, dout = expert_quarter(x, dyx, in_ref[...], out_ref[...])
        if i == 0:
            din_ref[...], dout_ref[...] = din, dout
        else:
            din_ref[...] += din
            dout_ref[...] += dout


def expert_far_kernel(*refs):
    own_ref, x_refs, dz_refs, (in_ref, out_ref, router_ref, y_ref, dx_ref) = refs[0], refs[1:3], refs[3:5], refs[5:10]
    dx_send, dx_keep, y_send, y_keep, din_ref, dout_ref, drouter_ref, din_sum, dout_sum = refs[10:]
    router = router_ref[...]
    for i in range(2):
        x, dz = x_refs[i][...], dz_refs[i][...].astype(F32)
        probs, mine, prob = expert_gate(own_ref[0], x, router)
        gate = prob.astype(BF).astype(F32)
        y, dx, din, dout = expert_quarter(x, (gate * dz).astype(BF), in_ref[...], out_ref[...])
        y, dx = y + y_ref[i], dx + dx_ref[i]
        dgate = jnp.sum(dz * y, axis=1, keepdims=True)
        dlogits = (dgate * prob * (mine - probs)).astype(BF)
        dx = dx + dot(dlogits, router, 1, 1)
        y = gate * y
        if i == 0:
            din_sum[...], dout_sum[...], drouter_ref[...] = din, dout, dot(x, dlogits, 0, 0)
            dx_keep[...], y_keep[...] = dx, y
        else:
            din_sum[...] += din
            dout_sum[...] += dout
            drouter_ref[...] += dot(x, dlogits, 0, 0)
            dx_send[...], y_send[...] = dx.astype(BF), y.astype(BF)
    din_ref[...], dout_ref[...] = din_sum[...].astype(BF), dout_sum[...].astype(BF)


def expert_call(kernel, outs, own, args, flops, scratch=()):
    space = pl.BlockSpec(memory_space=pltpu.VMEM)
    return pl.pallas_call(
        kernel,
        out_shape=outs,
        in_specs=[pl.BlockSpec(memory_space=pltpu.SMEM)] + [space] * len(args),
        out_specs=(space,) * len(outs),
        scratch_shapes=scratch,
        compiler_params=pltpu.CompilerParams(vmem_limit_bytes=56 * 2**20),
        cost_estimate=pl.CostEstimate(flops=flops, bytes_accessed=2**20, transcendentals=0),
    )(own.astype(jnp.int32)[None], *args)


def expert_compute(own, x_blocks, dz_blocks, w_in, w_out, router):
    tall, width = x_blocks[0].shape
    square = w_in[0].shape
    send, keep = jax.ShapeDtypeStruct((tall, width), BF), jax.ShapeDtypeStruct((tall, width), F32)
    near, far = jax.ShapeDtypeStruct(square, F32), jax.ShapeDtypeStruct(square, BF)
    both = jax.ShapeDtypeStruct((2, tall, width), F32)
    flops = 24 * tall * width * square[1]
    args = (*x_blocks, *dz_blocks, w_in[0], w_out[0], router)
    y, dx, din_own, dout_own = expert_call(expert_near_kernel, (both, both, near, near), own, args, 10**7)
    args = (*x_blocks, *dz_blocks, w_in[1], w_out[1], router, y, dx)
    outs = (send, keep, send, keep, far, far, jax.ShapeDtypeStruct(router.shape, F32))
    scratch = (pltpu.VMEM(square, F32), pltpu.VMEM(square, F32))
    got = expert_call(expert_far_kernel, outs, own, args, flops, scratch)
    dx_send, dx_keep, y_send, y_keep, din_far, dout_far, drouter = got
    return dx_send, dx_keep, y_send, y_keep, din_own, din_far, dout_own, dout_far, drouter


def make_shards(n_dp):
    n_all = n_dp * NF

    def shards(
        patches, segment_ids, live, expert_ids, ranks, norm_gains, norm_biases, attn_qkv, attn_out,
        mlp_in, mlp_out, router, exp_in, exp_out, cotangent,
    ):
        width = patches.shape[-1]
        tokens = patches.shape[0] * patches.shape[1]
        experts = exp_in.shape[0]
        clones = n_dp // experts
        part = width // NF
        rows = attn_qkv.shape[1]
        hid = mlp_out.shape[0]
        own_f = lax.axis_index("fsdp")
        own_dp = lax.axis_index("dp")
        groups = ring = None
        if clones > 1:
            groups = [[g * experts + e for e in range(experts)] for g in range(clones)]
            ring = [[g * experts + e for g in range(clones)] for e in range(experts)]
        capacity = (210 * tokens + 100 * experts - 1) // (100 * experts)
        slots = (capacity + 7) // 8 * 8

        code = (segment_ids * 2 + live).reshape(tokens)
        code_all = gather_row(code)
        live_all = (code_all % 2).astype(F32)
        rows_all = gather_row(patches.reshape(tokens, width))

        def qkv_block(layer):
            weight = attn_qkv[layer].reshape(rows, 3, NF, part)
            return jnp.transpose(weight, (2, 0, 1, 3)).reshape(NF, rows, 3 * part)

        small = jnp.concatenate(
            [norm_gains.T, norm_biases.T, router, jnp.zeros((rows, 64 - 8 - experts), BF)], axis=1
        )
        small = jnp.broadcast_to(small[None], (NF, rows, 64))
        def to_everyone(blocks):
            full = jnp.broadcast_to(blocks[None], (n_dp,) + blocks.shape)
            return exchange(full.reshape((n_all, rows, -1)), ALL).reshape(width, -1)

        first = to_everyone(jnp.concatenate([qkv_block(0), small], axis=2))
        small_all, w_qkv0 = first[:, 3 * part :], (first, slice(0, 3 * part))
        norms = small_all[:, :8].T.astype(F32)
        gains, biases = norms[:4], norms[4:]
        w_router = small_all[:, 8 : 8 + experts]

        mlp_block = jnp.transpose(mlp_in.reshape(rows, n_dp, NF, hid), (2, 0, 1, 3))
        mlp_block = deal(mlp_block.reshape(NF, rows, n_dp * hid)).reshape(NF * rows, width)
        mlp_all = lax.all_gather(jnp.concatenate([mlp_block, mlp_out], axis=0), "dp")

        to_heads = [(j, j % n_dp * NF + j // n_dp) for j in range(n_all)]
        to_owner = [(b, a) for a, b in to_heads]
        held_out = lax.ppermute(attn_out, ALL, to_heads)
        held = after(held_out[0], first)
        w_out0 = exchange(jnp.broadcast_to(held[None], (n_dp, rows, width)), "dp").reshape(part, width)

        choice = expert_ids.reshape(tokens, 2)
        rank = ranks.reshape(tokens, 2)
        place = jnp.where(rank < capacity, choice * slots + rank, -1)
        slot_index = jnp.arange(experts * slots, dtype=jnp.int32)[:, None]
        pick = (place[:, 0][None] == slot_index) | (place[:, 1][None] == slot_index)
        pick = pick.astype(BF)

        def to_experts(block):
            held = mm(pick, block).astype(BF).reshape(experts, slots, width)
            return exchange(held, "dp", groups).reshape(experts * slots, width)

        top_grad = cotangent.reshape(tokens, width)
        in_block = jnp.transpose(exp_in.reshape(experts, rows, n_dp, NF, hid), (3, 0, 1, 2, 4))
        in_block = in_block.reshape(NF, experts, rows, n_dp * hid)
        if clones == 1:
            in_block = jnp.swapaxes(deal(in_block), 0, 1).reshape(experts, NF * rows, n_dp * hid)
            held = deal(qkv_block(1)).reshape(NF * rows, 3 * part)
            held = jnp.concatenate([held, held_out[1].reshape(NF * rows, part)], axis=1)
            held = jnp.broadcast_to(held[None], (n_dp,) + held.shape)
            in_block = jnp.concatenate([in_block, held], axis=2)

        h0 = patches.reshape(tokens, width).astype(F32)
        xhat0_all, _ = scale_rows(rows_all.astype(F32))
        a0 = (xhat0_all * gains[0] + biases[0]).astype(BF)
        qkv0, o0, lse0, send, keep = attend([a0], w_qkv0, w_out0, code_all)
        h1 = h0 + scatter_blocks(after(send, in_block) if clones == 1 else send, keep)

        if clones == 1:
            held = exchange(after(in_block, w_out0), "dp").reshape(width, -1)
            cut = n_dp * hid
            w_exp_in, w_qkv1 = held[:, :cut], (held, slice(cut, cut + 3 * part))
            w_out1 = held[:, cut + 3 * part :].reshape(part, width)
        else:
            held = exchange(in_block, "fsdp")
            held = exchange(jnp.swapaxes(held, 0, 1), "dp", groups)
            w_exp_in = lax.all_gather(held, "dp", axis_index_groups=ring).reshape(width, n_dp * hid)
            w_qkv1 = (to_everyone(qkv_block(1)), slice(0, 3 * part))
            w_out1 = lax.all_gather(held_out[1], "dp").reshape(part, width)
        if clones == 1:
            dz = mm(pick, top_grad).astype(BF).reshape(experts, slots, width)
            held = exchange(after(jnp.concatenate([dz, exp_out], axis=1), w_exp_in), "dp")
            dz, w_exp_out = held[:, :slots].reshape(experts * slots, width), held[:, slots:]
        else:
            dz = to_experts(top_grad)
            w_exp_out = exchange(exp_out, "dp", groups)
            w_exp_out = lax.all_gather(w_exp_out, "dp", axis_index_groups=ring)
        w_exp_out = w_exp_out.reshape(n_dp * hid, width)

        xhat1, inv1 = scale_rows(h1)
        c0 = gather_blocks((xhat1 * gains[1] + biases[1]).astype(BF))
        u0, g0, send, keep = mlp(c0, mlp_all)
        h2 = h1 + scatter_blocks(send, keep)

        w_in_far = swap(w_exp_in, 2)
        xhat2, inv2 = scale_rows(h2)
        a1 = gather_blocks(after((xhat2 * gains[2] + biases[2]).astype(BF), w_exp_in))
        qkv1, o1, lse1, send, keep = attend(a1, w_qkv1, w_out1, code_all)
        h3 = h2 + scatter_blocks(send, keep, w_in_far)

        xhat3, inv3 = scale_rows(h3)
        c1 = after((xhat3 * gains[3] + biases[3]).astype(BF), dz, w_exp_out)
        w_out_far = swap(w_exp_out, 2)
        dz = (dz, swap(dz, 1))
        x = to_experts(c1)
        x = (x, swap(x, 1))
        dx_send, dx_keep, y_send, y_keep, din_own, din_far, dout_own, dout_far, router_part = expert_compute(
            own_dp % experts, x, dz, (w_exp_in, w_in_far), (w_exp_out, w_out_far), w_router
        )
        dx = (dx_keep + swap(dx_send, 1).astype(F32)).astype(BF)
        y = (y_keep + swap(after(y_send, dx), 1).astype(F32)).astype(BF)
        exp_in_part = (din_own + swap(after(din_far, dx), 2).astype(F32)).astype(BF)
        exp_out_part = (dout_own + swap(after(dout_far, exp_in_part), 2).astype(F32)).astype(BF)
        dx = exchange(dx.reshape(experts, slots, width), "dp", groups)

        if clones == 1:
            back = exp_out_part.reshape(experts, hid, width)
            back = jnp.concatenate([y.reshape(experts, slots, width), back], axis=1)
            in_got = exchange(after(exp_in_part.reshape(n_dp, NF * rows, n_dp * hid), dx), "dp")
            got = exchange(after(back, in_got), "dp")
            y, exp_out_grads = got[:, :slots], got[:, slots:].astype(F32)
        else:
            back = lax.psum_scatter(
                exp_out_part.reshape(clones, experts, hid, width), "dp", axis_index_groups=ring
            )
            exp_out_grads = exchange(back, "dp", groups).astype(F32)
            got = exp_out_grads
            y = exchange(y.reshape(experts, slots, width), "dp", groups)
            held = lax.psum_scatter(
                exp_in_part.reshape(clones, experts, NF, rows, n_dp * hid), "dp", axis_index_groups=ring
            )
            in_got = exchange(held, "dp", groups)
        dc1 = mm_tn(pick, after(dx, exp_in_part).reshape(experts * slots, width))

        def rows_to_owners(grad):
            cols = grad.shape[1]
            got = exchange(grad.astype(BF).reshape(n_all, rows, cols), ALL)
            return got.reshape(n_dp, NF, rows, cols).astype(F32)

        def qkv_layout(total):
            parts = total.reshape(NF, rows, 3, part)
            return jnp.transpose(parts, (1, 2, 0, 3)).reshape(rows, 3 * width)

        def sums(out_grad, xhat):
            return jnp.sum(out_grad * xhat, axis=0), jnp.sum(out_grad, axis=0)

        gain3, bias3 = sums(dc1, xhat3)
        grad = top_grad.astype(F32) + norm_back(dc1, xhat3, inv3, gains[3])

        dy1 = gather_blocks(grad.astype(BF))
        dqkv1, send, keep = attend_back(dy1, w_qkv1, w_out1, qkv1, lse1, code_all)
        da1 = scatter_blocks(after(send, in_got), keep)
        attn_part = [
            mm_tn(jnp.concatenate(a1, axis=0), dqkv1).astype(BF).reshape(n_dp, NF * rows, 3 * part),
            mm_tn(o1, jnp.concatenate(dy1, axis=0)).astype(BF).reshape(n_dp, NF * rows, part),
        ]
        attn_part = jnp.concatenate(attn_part, axis=2)
        gain2, bias2 = sums(da1, xhat2)
        grad = grad + norm_back(da1, xhat2, inv2, gains[2])

        dm = gather_blocks(grad.astype(BF))
        du0, send, keep = mlp_back(dm, after(u0, attn_part), mlp_all)
        dc0 = scatter_blocks(send, keep)
        dense_part = mlp_weights(c0, dm, du0, g0, attn_part)
        dense_sum = lax.psum_scatter(dense_part, "dp")
        gain1, bias1 = sums(dc0, xhat1)
        grad = grad + norm_back(dc0, xhat1, inv1, gains[1])

        dy0 = gather_blocks(after(grad.astype(BF), got))
        dqkv0, send, keep = attend_back([after(dy0[0], dense_part), *dy0[1:]], w_qkv0, w_out0, qkv0, lse0, code_all)
        out_part0 = mm_tn(o0, jnp.concatenate(dy0, axis=0)).astype(BF).reshape(n_dp, rows, width)
        out_got0 = exchange(after(out_part0, got), "dp")
        qkv_part0 = mm_tn(a0, dqkv0)
        h4 = h3 + mm_tn(pick, y.reshape(experts * slots, width))
        activations = h4.astype(BF)
        da0 = scatter_blocks(send, keep)
        xhat0_blocks = xhat0_all.reshape(NF, tokens, width)
        gain0 = bias0 = 0.0
        for k in range(NF):
            block = keep[k // 2] if k % 2 == 0 else send[k // 2].astype(F32)
            block_gain, block_bias = sums(block, xhat0_blocks[k])
            gain0, bias0 = gain0 + block_gain, bias0 + block_bias
        columns = jnp.stack([gain0, gain1, gain2, gain3, bias0, bias1, bias2, bias3], axis=1)
        columns = jnp.concatenate(
            [qkv_part0, columns, router_part, jnp.zeros((width, 64 - 8 - experts), F32)], axis=1
        )
        tail = rows_to_owners(after(columns, out_got0))
        total = jnp.sum(tail, axis=0)
        small_grads = jnp.sum(total[:, :, 3 * part :], axis=0)
        qkv_grad0 = qkv_layout(total[:, :, : 3 * part])
        dense_sum = after(dense_sum, tail)
        in_got = jnp.swapaxes(after(in_got, dqkv0).reshape(experts, NF, rows, n_dp * hid), 0, 1)
        in_got = deal(in_got).reshape(NF, experts, rows, n_dp, hid)
        exp_in_grads = jnp.transpose(in_got, (1, 2, 3, 0, 4))
        exp_in_grads = exp_in_grads.reshape(experts, rows, n_dp * NF * hid).astype(F32)
        held = jnp.concatenate([dense_sum[:, :width], dense_sum[:, 2 * width : 2 * width + 3 * part]], axis=1)
        held = deal(held.reshape(NF, rows, -1)).astype(F32)
        mlp_in_grads = held[..., :width].reshape(NF, rows, n_dp, hid)
        mlp_in_grads = jnp.transpose(mlp_in_grads, (1, 2, 0, 3)).reshape(rows, n_dp * NF * hid)
        qkv_grad1 = qkv_layout(held[..., width:])
        mlp_out_grads = dense_sum[:, width : 2 * width].astype(F32)
        out_sum1 = dense_sum[:, 2 * width + 3 * part :].reshape(rows, width).astype(F32)
        out_sums = jnp.stack([jnp.sum(out_got0.astype(F32), axis=0), out_sum1])
        proj_grads = lax.ppermute(out_sums, ALL, to_owner)
        xhat0, inv0 = scale_rows(h0)
        grad = grad + norm_back(da0, xhat0, inv0, gains[0])

        norm_grads = small_grads[:, :8].T
        return (
            activations.reshape(patches.shape),
            grad.reshape(patches.shape),
            norm_grads[:4],
            norm_grads[4:7],
            norm_grads[7],
            jnp.stack([qkv_grad0, qkv_grad1]),
            proj_grads,
            mlp_in_grads,
            mlp_out_grads,
            small_grads[:, 8 : 8 + experts],
            exp_in_grads,
            exp_out_grads,
        )

    return shards


def solution(mesh):
    by_row = P("dp", "fsdp", None)
    second = P(None, ("dp", "fsdp"), None)
    first = P(("dp", "fsdp"), None)
    pair = P("dp", "fsdp")
    norm = P(None, ("dp", "fsdp"))
    return jax.shard_map(
        make_shards(mesh.shape["dp"]),
        mesh=mesh,
        in_specs=(
            by_row, pair, pair, by_row, by_row, norm, norm, second, second, first, first, first,
            second, second, by_row,
        ),
        out_specs=(
            by_row, by_row, norm, norm, P(("dp", "fsdp")), second, second, first, first, first,
            second, second,
        ),
        check_vma=False,
    )
```
